256 devices in a mesh: member: 32 (over y, z_hi, core), space: 8 (over z_lo, x).
Axes of the slice: x: 4, y: 4, z: 8 (z_hi: 4, z_lo: 2; z = z_hi * 2 + z_lo), core: 2. Of those that a mesh axis runs over, the one named last changes fastest.
Arguments:
- state: float32 [256, 256, 3, 512], P('member', 'space'), may hold values from -6 to 6
- depth: float32 [256, 512], P('space'), may hold values from 0.5 to 2
- obs_cell: int32 [8, 32, 32], P('space', 'member'), may hold values from 0 to 511
- obs_value: float32 [8, 32, 32], P('space', 'member'), may hold values from -6 to 6
- obs_var: float32 [8, 32, 32], P('space', 'member'), may hold values from 0.05 to 5
Outputs:
- analysis: float32 [256, 256, 3, 512], P('member', 'space')
The draws below stay inside these ranges and needn't reach their ends.
Inputs may be any that keep to these rules, and one draw needn't show every extreme that they name: obs_cell[b, t, j] names a cell of the 1 row of tile t of band b, counted row by row.
All inputs are finite; a program needn't handle non-finite values.
Results may differ from the reference program's by a relative error of at most 0.00021.
Values sent between devices are 32-bit elements; how exact they have to be, the bound alone decides.
No kernel may reach another device: no remote copies, remote signals or barrier semaphores. Data moves between devices by JAX's collectives and lax.ppermute only.
A program may use at most 128 MiB of HBM per device.

```python
import math
import jax
import jax.numpy as jnp
from jax import lax

NLON = 512
OBS_DEV = 32
STEPS = 3
NS_ITERS = 5
MEMBERS = 256
BANDS = 8
TILES = 32
NLAT = 256
TILE_ROWS = 1


def touch_ends(values, own_key, least, high):
    longest = values.shape.index(max(values.shape))
    spots = []
    for shift in (0, 1):
        where = [jax.random.randint(jax.random.fold_in(own_key, axis), (), 0, length) for axis, length in enumerate(values.shape)]
        where[longest] = (where[longest] + shift) % values.shape[longest]
        spots.append(tuple(where))
    return values.at[spots[0]].set(least).at[spots[1]].set(high)


def level_of(stream_key, dims, shards, least, high):
    level = 1.0
    for position, blocks in shards:
        steps = jax.random.uniform(jax.random.fold_in(jax.random.fold_in(stream_key, 6), position), (blocks,), jnp.float32, least / len(shards), high / len(shards))
        level = level * jnp.repeat(jnp.exp(steps), dims[position] // blocks).reshape((-1,) + (1,) * (len(dims) - 1 - position))
    return level


def gaussian(key, dims, deviation, limit, shards=(), held_as=jnp.bfloat16):
    result = jax.random.normal(key, dims, jnp.float32) * deviation
    if len(shards) > 0:
        result = level_of(key, dims, shards, -0.22, 0.18) * result
    return jnp.clip(result, min=-limit, max=limit).astype(held_as)


def setup_inputs(seed: int = 0) -> dict:
    streams_of = jax.random.split(jax.random.key(seed), 6)
    return {
        "state": gaussian(streams_of[0], (MEMBERS, NLAT, 3, NLON), 1.0, 6.0, ((0, 32), (1, 8)), jnp.float32),
        "depth": jnp.clip(jnp.exp(math.log(2.0) - 1.3862944 * jax.random.uniform(streams_of[1], (NLAT, NLON), jnp.float32) ** level_of(streams_of[1], (NLAT, NLON), ((0, 8),), -0.2, 0.2)), 0.5, 2.0),
        "obs_cell": touch_ends(jax.random.randint(streams_of[2], (BANDS, TILES, OBS_DEV), 0, TILE_ROWS * NLON), jax.random.fold_in(streams_of[2], 1), 0, (TILE_ROWS * NLON) - 1).astype(jnp.int32),
        "obs_value": gaussian(streams_of[3], (BANDS, TILES, OBS_DEV), 1.0, 6.0, ((0, 8), (1, 32)), jnp.float32),
        "obs_var": jnp.clip(jnp.exp(math.log(5.0) - 4.6051702 * jax.random.uniform(streams_of[4], (BANDS, TILES, OBS_DEV), jnp.float32) ** level_of(streams_of[4], (BANDS, TILES, OBS_DEV), ((0, 8), (1, 32)), -0.2, 0.2)), 0.05, 5.0),
    }


courant = 0.3

def cols_diff(field):
    return jnp.roll(field, -1, axis=-1) - jnp.roll(field, 1, axis=-1)

def rows_diff(field):
    padded = jnp.pad(field, ((1, 1), (0, 0)))
    return padded[2:] - padded[:-2]

def march_forward(single_member, depth):
    for step in range(STEPS):
        height = single_member[:, 0]
        zonal = single_member[:, 1]
        meridional = single_member[:, 2]
        new_height = height - courant * depth * (cols_diff(zonal) + rows_diff(meridional))
        new_zonal = zonal - courant * cols_diff(new_height)
        new_meridional = meridional - courant * rows_diff(new_height)
        single_member = jnp.stack([new_height, new_zonal, new_meridional], axis=1)
    return single_member

def transform(gram, projection):
    count = gram.shape[0]
    identity = jnp.eye(count, dtype=jnp.float32)
    system = identity + gram / (count - 1)
    scale = jnp.sqrt(jnp.sum(system * system))

    def newton_iteration(index, carry):
        current, root_inv = carry
        factor = 1.5 * identity - 0.5 * jnp.dot(root_inv, current, precision=lax.Precision.HIGHEST)
        current = jnp.dot(current, factor, precision=lax.Precision.HIGHEST)
        root_inv = jnp.dot(factor, root_inv, precision=lax.Precision.HIGHEST)
        return (current, root_inv)
    current, root_inv = lax.fori_loop(0, NS_ITERS, newton_iteration, (system / scale, identity))
    root = root_inv / jnp.sqrt(scale)
    inner = jnp.dot(root, projection, precision=lax.Precision.HIGHEST)
    mean_weights = jnp.dot(root, inner, precision=lax.Precision.HIGHEST) / (count - 1)
    return mean_weights[:, None] + root

def reference(state, depth, obs_cell, obs_value, obs_var):
    prior_prediction = lax.map(lambda single_member: march_forward(single_member, depth), state)
    ensemble_centre = lax.optimization_barrier(jnp.mean(prior_prediction, axis=0))
    member_deviations = prior_prediction - ensemble_centre
    band_ids = jnp.arange(BANDS, dtype=jnp.int32)[:, None, None]
    tile_ids = jnp.arange(TILES, dtype=jnp.int32)[None, :, None]
    row_ids = (band_ids * TILES + tile_ids) * TILE_ROWS + obs_cell // NLON
    col_ids = obs_cell % NLON
    observed = member_deviations[:, row_ids, 0, col_ids].reshape(MEMBERS, -1)
    innovation = (obs_value - ensemble_centre[row_ids, 0, col_ids]).reshape(-1)
    weighted = observed / obs_var.reshape(-1)
    gram = jnp.dot(weighted, observed.T, precision=lax.Precision.HIGHEST)
    projection = jnp.dot(weighted, innovation, precision=lax.Precision.HIGHEST)
    weights = transform(gram, projection)
    update = jnp.dot(weights.T, member_deviations.reshape(MEMBERS, -1), precision=lax.Precision.HIGHEST)
    return ensemble_centre + update.reshape(state.shape)
```

```python
import functools

import jax
import jax.numpy as jnp
from jax import lax
from jax.experimental import pallas as pl
from jax.experimental.pallas import tpu as pltpu
from jax.sharding import PartitionSpec as P

STEPS = 3
NS_ITERS = 5
COURANT = 0.3
HALO = 8
LANES = 128
VMEM = 40 * 1024 * 1024
HIGHEST = lax.Precision.HIGHEST


def dot(a, b, dims=((1,), (0,))):
    return lax.dot_general(a, b, (dims, ((), ())), precision=HIGHEST, preferred_element_type=jnp.float32)


def cost(flops, bytes_accessed):
    return pl.CostEstimate(flops=flops, bytes_accessed=bytes_accessed, transcendentals=0)


def forecast_kernel(bands, state_ref, above_ref, below_ref, depth_ref, depth_above_ref, depth_below_ref, height_ref, wind_ref, lanes_ref):
    members, _, rows, cols = state_ref.shape
    total = rows + 2 * HALO
    band = lax.axis_index("space")
    row = lax.broadcasted_iota(jnp.int32, (total, cols), 0) + band * rows - HALO
    inside = jnp.logical_and(row >= 0, row < bands * rows)
    depth = jnp.concatenate([depth_above_ref[...], depth_ref[...], depth_below_ref[...]], axis=0)
    pull = jnp.where(inside, COURANT * depth, 0.0)
    push = jnp.where(inside, COURANT, 0.0)

    def cols_diff(f):
        return pltpu.roll(f, cols - 1, 1) - pltpu.roll(f, 1, 1)

    def rows_diff(f):
        return pltpu.roll(f, total - 1, 0) - pltpu.roll(f, 1, 0)

    for m in range(members):
        height, zonal, meridional = (
            jnp.concatenate([above_ref[m, k], state_ref[m, k], below_ref[m, k]], axis=0) for k in range(3)
        )
        for _ in range(STEPS):
            height = height - pull * (cols_diff(zonal) + rows_diff(meridional))
            zonal = zonal - COURANT * cols_diff(height)
            meridional = meridional - push * rows_diff(height)
        for k, field in enumerate((height, zonal, meridional)):
            for c in range(cols // LANES):
                lanes_ref[k * (cols // LANES) + c, pl.ds(m, rows, stride=members), :] = field[HALO:HALO + rows, c * LANES:(c + 1) * LANES]
    for c in range(cols // LANES):
        height_ref[:, c * LANES:(c + 1) * LANES] = lanes_ref[c]
    for c in range(2 * cols // LANES):
        wind_ref[:, c * LANES:(c + 1) * LANES] = lanes_ref[cols // LANES + c]


def forecast(state, above, below, depth, depth_above, depth_below, bands):
    members, fields, rows, cols = state.shape
    return pl.pallas_call(
        functools.partial(forecast_kernel, bands),
        out_shape=(
            jax.ShapeDtypeStruct((rows * members, cols), jnp.float32),
            jax.ShapeDtypeStruct((rows * members, 2 * cols), jnp.float32),
        ),
        scratch_shapes=[pltpu.VMEM((fields * cols // LANES, rows * members, LANES), jnp.float32)],
        compiler_params=pltpu.CompilerParams(vmem_limit_bytes=VMEM),
        cost_estimate=cost(STEPS * 12 * state.size, 8 * state.size),
        name="forecast",
    )(state, above, below, depth, depth_above, depth_below)


def spots(count, block):
    i = lax.broadcasted_iota(jnp.int32, (count, count), 0)
    j = lax.broadcasted_iota(jnp.int32, (count, count), 1)
    return j == (i - i % block) + (i + 1) % block


def gram_kernel(block, height_ref, cell_ref, value_ref, var_ref, out_ref):
    count, cols = height_ref.shape
    number = cell_ref.shape[1]
    picks = lax.broadcasted_iota(jnp.int32, (cols, number), 0) == cell_ref[...]
    seen = dot(height_ref[...], jnp.where(picks, 1.0, 0.0))
    centre = jnp.sum(seen, axis=0, keepdims=True) / count
    observed = seen - centre
    innovation = value_ref[...] - centre
    weighted = observed / var_ref[...]
    gram = dot(weighted, observed, ((1,), (1,)))
    projection = jnp.sum(weighted * innovation, axis=1, keepdims=True)
    out_ref[...] = jnp.where(spots(count, block), projection, gram)


def gram_of(height, cell, value, var, block):
    count = height.shape[0]
    return pl.pallas_call(
        functools.partial(gram_kernel, block),
        out_shape=jax.ShapeDtypeStruct((count, count), jnp.float32),
        compiler_params=pltpu.CompilerParams(vmem_limit_bytes=VMEM),
        cost_estimate=cost(6 * 2 * height.size * cell.shape[1], 4 * height.size),
        name="gram",
    )(height, cell, value, var)


def transform_kernel(block, packed_ref, weights_ref):
    packed = packed_ref[...]
    count = packed.shape[0]
    places = spots(count, block)
    projection = jnp.sum(jnp.where(places, packed, 0.0), axis=1, keepdims=True)
    gram = jnp.where(places, packed.T, packed)
    i = lax.broadcasted_iota(jnp.int32, (count, count), 0)
    j = lax.broadcasted_iota(jnp.int32, (count, count), 1)
    identity = jnp.where(i == j, 1.0, 0.0)
    system = identity + gram / (count - 1)
    scale = jnp.sqrt(jnp.sum(jnp.sum(system * system, axis=1, keepdims=True), axis=0, keepdims=True))
    current = system / scale
    root_inv = identity
    for step in range(NS_ITERS):
        product = current if step == 0 else dot(root_inv, current)
        factor = 1.5 * identity - 0.5 * product
        if step < NS_ITERS - 1:
            current = dot(current, factor)
        root_inv = factor if step == 0 else dot(factor, root_inv)
    root = root_inv / jnp.sqrt(scale)
    inner = dot(root, jnp.broadcast_to(projection, (count, 128)))
    mean_weights = dot(root, inner) / (count - 1)
    weights_ref[...] = mean_weights[:, :1] + root


def transform(packed, block):
    return pl.pallas_call(
        functools.partial(transform_kernel, block),
        out_shape=jax.ShapeDtypeStruct(packed.shape, jnp.float32),
        compiler_params=pltpu.CompilerParams(vmem_limit_bytes=VMEM),
        cost_estimate=cost(6 * 2 * 14 * packed.shape[0] ** 3, 8 * packed.size),
        name="transform",
    )(packed)


def mix_kernel(weights_ref, height_ref, wind_ref, out_ref):
    weights = weights_ref[...]
    count, cols = height_ref.shape

    def mixed(values):
        centre = jnp.sum(values, axis=0, keepdims=True) / count
        return centre + dot(weights, values - centre, ((0,), (0,)))

    out_ref[:, :cols] = mixed(height_ref[...])
    out_ref[:, cols:2 * cols] = mixed(wind_ref[:, :cols])
    out_ref[:, 2 * cols:] = mixed(wind_ref[:, cols:])


def mix(weights, height, wind):
    count, cols = height.shape
    return pl.pallas_call(
        mix_kernel,
        out_shape=jax.ShapeDtypeStruct((count, 3 * cols), jnp.float32),
        compiler_params=pltpu.CompilerParams(vmem_limit_bytes=VMEM),
        cost_estimate=cost(6 * 2 * count * count * 3 * cols, 4 * count * 6 * cols),
        name="mix",
    )(weights, height, wind)


def unfold_kernel(rows_ref, out_ref, lanes_ref):
    members, fields, rows, cols = out_ref.shape
    for c in range(fields * cols // LANES):
        lanes_ref[c] = rows_ref[:, c * LANES:(c + 1) * LANES]
    for m in range(members):
        for k in range(fields):
            for c in range(cols // LANES):
                out_ref[m, k, :, c * LANES:(c + 1) * LANES] = lanes_ref[k * (cols // LANES) + c, pl.ds(m, rows, stride=members), :]


def unfold(rows, shape):
    return pl.pallas_call(
        unfold_kernel,
        out_shape=jax.ShapeDtypeStruct(shape, jnp.float32),
        scratch_shapes=[pltpu.VMEM((rows.shape[1] // LANES, rows.shape[0], LANES), jnp.float32)],
        compiler_params=pltpu.CompilerParams(vmem_limit_bytes=VMEM),
        cost_estimate=cost(0, 8 * rows.size),
        name="unfold",
    )(rows)


def exchange(blocks, axis):
    return lax.all_to_all(blocks, axis, split_axis=0, concat_axis=0, tiled=True)


def spread(block, axis):
    return exchange(jnp.broadcast_to(block, (lax.axis_size(axis),) + block.shape), axis)


def shards(state, depth, obs_cell, obs_value, obs_var):
    bands, tiles = lax.axis_size("space"), lax.axis_size("member")
    members, rows, fields, cols = state.shape
    state = state.transpose(0, 2, 1, 3)
    up = [(i, i + 1) for i in range(bands - 1)]
    down = [(i + 1, i) for i in range(bands - 1)]
    above = lax.ppermute(state[:, :, rows - HALO:], "space", up)
    below = lax.ppermute(state[:, :, :HALO], "space", down)
    depth_above = lax.ppermute(depth[rows - HALO:], "space", up)
    depth_below = lax.ppermute(depth[:HALO], "space", down)
    height, wind = forecast(state, above, below, depth, depth_above, depth_below, bands)
    ensemble = tiles * members
    height = exchange(height.reshape(tiles, members, cols), "member").reshape(ensemble, cols)
    wind = exchange(wind.reshape(tiles, members, 2 * cols), "member").reshape(ensemble, 2 * cols)
    part = gram_of(height, obs_cell[0], obs_value[0], obs_var[0], members)
    part = jnp.sum(exchange(part.reshape(tiles, members, ensemble), "member"), axis=0)
    part = jnp.sum(spread(part, "space"), axis=0)
    packed = spread(part, "member").reshape(ensemble, ensemble)
    weights = transform(packed, members)
    analysed = mix(weights, height, wind)
    back = exchange(analysed.reshape(tiles, members, fields * cols), "member").reshape(ensemble, fields * cols)
    return unfold(back, (members, fields, rows, cols)).transpose(0, 2, 1, 3)


def solution(mesh):
    placed = (
        P("member", "space", None, None),
        P("space", None),
        P("space", "member", None),
        P("space", "member", None),
        P("space", "member", None),
    )
    return jax.shard_map(
        shards,
        mesh=mesh,
        in_specs=placed,
        out_specs=P("member", "space", None, None),
        check_vma=False,
    )
```

```python
import functools

import jax
import jax.numpy as jnp
from jax import lax
from jax.experimental import pallas as pl
from jax.experimental.pallas import tpu as pltpu
from jax.sharding import PartitionSpec as P

STEPS = 3
NS_ITERS = 5
COURANT = 0.3
HALO = 8
LANES = 128
ROW_BLOCK = 4
VMEM = 40 * 1024 * 1024
HIGHEST = lax.Precision.HIGHEST


def dot(a, b, dims=((1,), (0,))):
    return lax.dot_general(a, b, (dims, ((), ())), precision=HIGHEST, preferred_element_type=jnp.float32)


def cost(flops, bytes_accessed):
    return pl.CostEstimate(flops=flops, bytes_accessed=bytes_accessed, transcendentals=0)


def forecast_kernel(bands, state_ref, above_ref, below_ref, depth_ref, height_ref, keep_ref, send_ref, field_ref, pull_ref):
    members, fields, rows, cols = state_ref.shape
    chunks = cols // LANES
    total = rows + 2 * HALO
    band = lax.axis_index("space")
    here = lax.axis_index("member")
    lane = lax.broadcasted_iota(jnp.int32, (1, LANES), 1)

    for m in range(members):
        for c in range(chunks):
            lanes = slice(c * LANES, (c + 1) * LANES)
            for k in range(fields):
                field_ref[k, c, pl.ds(m, HALO, stride=members), :] = above_ref[m * fields + k, :, lanes]
                field_ref[k, c, pl.ds(HALO * members + m, rows, stride=members), :] = state_ref[m, k, :, lanes]
                field_ref[k, c, pl.ds((HALO + rows) * members + m, HALO, stride=members), :] = below_ref[m * fields + k, :, lanes]
            pull_ref[c, pl.ds(m, HALO, stride=members), :] = COURANT * above_ref[members * fields, :, lanes]
            pull_ref[c, pl.ds(HALO * members + m, rows, stride=members), :] = COURANT * depth_ref[:, lanes]
            pull_ref[c, pl.ds((HALO + rows) * members + m, HALO, stride=members), :] = COURANT * below_ref[members * fields, :, lanes]

    def cols_diff(parts):
        left = [pltpu.roll(p, 1, 1) for p in parts]
        right = [pltpu.roll(p, LANES - 1, 1) for p in parts]
        return [
            jnp.where(lane == LANES - 1, right[(c + 1) % chunks], right[c]) - jnp.where(lane == 0, left[c - 1], left[c])
            for c in range(chunks)
        ]

    def take(k, first, count):
        return [field_ref[k, c, first * members:(first + count) * members, :] for c in range(chunks)]

    def push_of(first, count):
        if first >= HALO and first + count <= HALO + rows:
            return COURANT
        row = lax.broadcasted_iota(jnp.int32, (count * members, LANES), 0) + (first * members + (band * rows - HALO) * members)
        return jnp.where(jnp.logical_and(row >= 0, row < bands * rows * members), COURANT, 0.0)

    def blocks(first, last):
        edges = [first] + [e for e in range(0, total, ROW_BLOCK) if first < e < last] + [last]
        return [(lo, hi - lo) for lo, hi in zip(edges[:-1], edges[1:])]

    for step in range(STEPS):
        reach = 2 * (STEPS - 1 - step)
        for first, count in blocks(HALO - reach - 1, HALO + rows + reach + 1):
            height = take(0, first, count)
            slope = cols_diff(take(1, first, count))
            north = take(2, first + 1, count)
            south = take(2, first - 1, count)
            for c in range(chunks):
                span = slice(first * members, (first + count) * members)
                field_ref[0, c, span, :] = height[c] - pull_ref[c, span, :] * (slope[c] + (north[c] - south[c]))
        for first, count in blocks(HALO - reach, HALO + rows + reach):
            slope = cols_diff(take(0, first, count))
            zonal = take(1, first, count)
            meridional = take(2, first, count)
            north = take(0, first + 1, count)
            south = take(0, first - 1, count)
            push = push_of(first, count)
            for c in range(chunks):
                span = slice(first * members, (first + count) * members)
                field_ref[1, c, span, :] = zonal[c] - COURANT * slope[c]
                field_ref[2, c, span, :] = meridional[c] - push * (north[c] - south[c])

    for c in range(chunks):
        for t in range(rows):
            height_ref[t, :, c * LANES:(c + 1) * LANES] = field_ref[0, c, (HALO + t) * members:(HALO + t + 1) * members, :]
    core = here % 2
    for k in range(rows // 2):
        partner = (here // 2) ^ k
        for out_ref, other in ((keep_ref, core), (send_ref, 1 - core)):
            start = pl.multiple_of((HALO + 2 * partner + other) * members, members)
            for f in (1, 2):
                for c in range(chunks):
                    lanes = slice(((f - 1) * chunks + c) * LANES, ((f - 1) * chunks + c + 1) * LANES)
                    out_ref[k, :, lanes] = field_ref[f, c, pl.ds(start, members), :]


def forecast(state, above, below, depth, bands):
    members, fields, rows, cols = state.shape
    total = rows + 2 * HALO
    return pl.pallas_call(
        functools.partial(forecast_kernel, bands),
        out_shape=(
            jax.ShapeDtypeStruct((rows, members, cols), jnp.float32),
            jax.ShapeDtypeStruct((rows // 2, members, 2 * cols), jnp.float32),
            jax.ShapeDtypeStruct((rows // 2, members, 2 * cols), jnp.float32),
        ),
        scratch_shapes=[
            pltpu.VMEM((fields, cols // LANES, total * members, LANES), jnp.float32),
            pltpu.VMEM((cols // LANES, total * members, LANES), jnp.float32),
        ],
        compiler_params=pltpu.CompilerParams(vmem_limit_bytes=VMEM),
        cost_estimate=cost(STEPS * 12 * state.size, 8 * state.size),
        name="forecast",
    )(state, above, below, depth)


def pack_kernel(keep_ref, got_ref, *out_refs):
    core = lax.axis_index("member") % 2
    for k, out_ref in enumerate(out_refs):
        out_ref[core] = keep_ref[k]
        out_ref[1 - core] = got_ref[k]


def pack(keep, got):
    return pl.pallas_call(
        pack_kernel,
        out_shape=[jax.ShapeDtypeStruct((2,) + keep.shape[1:], jnp.float32)] * keep.shape[0],
        compiler_params=pltpu.CompilerParams(vmem_limit_bytes=VMEM),
        cost_estimate=cost(0, 16 * keep.size),
        name="pack",
    )(keep, got)


def spots(count, block):
    i = lax.broadcasted_iota(jnp.int32, (count, count), 0)
    j = lax.broadcasted_iota(jnp.int32, (count, count), 1)
    return j == (i - i % block) + (i + 1) % block


def gram_kernel(block, height_ref, cell_ref, value_ref, var_ref, keep_ref, send_ref, whole_ref):
    count, cols = height_ref.shape
    number = cell_ref.shape[1]
    picks = lax.broadcasted_iota(jnp.int32, (cols, number), 0) == cell_ref[...]
    seen = dot(height_ref[...], jnp.where(picks, 1.0, 0.0))
    centre = jnp.sum(seen, axis=0, keepdims=True) / count
    observed = seen - centre
    innovation = value_ref[...] - centre
    weighted = observed / var_ref[...]
    gram = dot(weighted, observed, ((1,), (1,)))
    projection = jnp.sum(weighted * innovation, axis=1, keepdims=True)
    whole_ref[...] = jnp.where(spots(count, block), projection, gram)
    half = count // 2
    core = lax.axis_index("member") % 2
    keep_ref[...] = whole_ref[pl.ds(pl.multiple_of(core * half, half), half), :]
    send_ref[...] = whole_ref[pl.ds(pl.multiple_of((1 - core) * half, half), half), :]


def gram_of(height, cell, value, var, block):
    count = height.shape[0]
    return pl.pallas_call(
        functools.partial(gram_kernel, block),
        out_shape=[jax.ShapeDtypeStruct((count // 2, count), jnp.float32)] * 2,
        scratch_shapes=[pltpu.VMEM((count, count), jnp.float32)],
        compiler_params=pltpu.CompilerParams(vmem_limit_bytes=VMEM),
        cost_estimate=cost(6 * 2 * height.size * cell.shape[1], 4 * height.size),
        name="gram",
    )(height, cell, value, var)


def transform_kernel(block, keep_ref, got_ref, weights_ref, packed_ref):
    half, count = keep_ref.shape
    core = lax.axis_index("member") % 2
    packed_ref[pl.ds(pl.multiple_of(core * half, half), half), :] = keep_ref[...]
    packed_ref[pl.ds(pl.multiple_of((1 - core) * half, half), half), :] = got_ref[...]
    packed = packed_ref[...]
    places = spots(count, block)
    projection = jnp.sum(jnp.where(places, packed, 0.0), axis=1, keepdims=True)
    gram = jnp.where(places, packed.T, packed)
    i = lax.broadcasted_iota(jnp.int32, (count, count), 0)
    j = lax.broadcasted_iota(jnp.int32, (count, count), 1)
    identity = jnp.where(i == j, 1.0, 0.0)
    system = identity + gram / (count - 1)
    scale = jnp.sqrt(jnp.sum(jnp.sum(system * system, axis=1, keepdims=True), axis=0, keepdims=True))
    current = system / scale
    root_inv = identity
    for step in range(NS_ITERS):
        product = current if step == 0 else dot(root_inv, current)
        factor = 1.5 * identity - 0.5 * product
        if step < NS_ITERS - 1:
            current = dot(current, factor)
        root_inv = factor if step == 0 else dot(factor, root_inv)
    root = root_inv / jnp.sqrt(scale)
    inner = dot(root, jnp.broadcast_to(projection, (count, 128)))
    mean_weights = dot(root, inner) / (count - 1)
    weights_ref[...] = mean_weights[:, :1] + root


def transform(keep, got, block):
    count = keep.shape[1]
    return pl.pallas_call(
        functools.partial(transform_kernel, block),
        out_shape=jax.ShapeDtypeStruct((count, count), jnp.float32),
        scratch_shapes=[pltpu.VMEM((count, count), jnp.float32)],
        compiler_params=pltpu.CompilerParams(vmem_limit_bytes=VMEM),
        cost_estimate=cost(6 * 2 * 14 * count ** 3, 8 * count ** 2),
        name="transform",
    )(keep, got)


def mix_kernel(weights_ref, height_ref, *refs):
    wind_refs, out_ref, order_ref = refs[:-2], refs[-2], refs[-1]
    count, cols = height_ref.shape
    group = count // len(wind_refs)
    weights = weights_ref[...]
    chip = lax.axis_index("member") // 2
    for k in range(len(wind_refs)):
        order_ref[k * group:(k + 1) * group, :] = weights_ref[pl.ds(pl.multiple_of((chip ^ k) * group, group), group), :]
    order = order_ref[...]

    def mixed(values, coefficients):
        centre = jnp.sum(values, axis=0, keepdims=True) / count
        return centre + dot(coefficients, values - centre, ((0,), (0,)))

    out_ref[:, :cols] = mixed(height_ref[...], weights)
    for f in (1, 2):
        values = jnp.concatenate([w[:, :, (f - 1) * cols:f * cols].reshape(group, cols) for w in wind_refs], axis=0)
        out_ref[:, f * cols:(f + 1) * cols] = mixed(values, order)


def mix(weights, height, winds):
    count, cols = height.shape
    return pl.pallas_call(
        mix_kernel,
        out_shape=jax.ShapeDtypeStruct((count, 3 * cols), jnp.float32),
        scratch_shapes=[pltpu.VMEM((count, count), jnp.float32)],
        compiler_params=pltpu.CompilerParams(vmem_limit_bytes=VMEM),
        cost_estimate=cost(6 * 2 * count * count * 3 * cols, 4 * count * 6 * cols),
        name="mix",
    )(weights, height, *winds)


def unfold_kernel(rows_ref, out_ref, lanes_ref):
    members, fields, rows, cols = out_ref.shape
    for c in range(fields * cols // LANES):
        lanes_ref[c] = rows_ref[:, c * LANES:(c + 1) * LANES]
    for m in range(members):
        for k in range(fields):
            for c in range(cols // LANES):
                out_ref[m, k, :, c * LANES:(c + 1) * LANES] = lanes_ref[k * (cols // LANES) + c, pl.ds(m, rows, stride=members), :]


def unfold(rows, shape):
    return pl.pallas_call(
        unfold_kernel,
        out_shape=jax.ShapeDtypeStruct(shape, jnp.float32),
        scratch_shapes=[pltpu.VMEM((rows.shape[1] // LANES, rows.shape[0], LANES), jnp.float32)],
        compiler_params=pltpu.CompilerParams(vmem_limit_bytes=VMEM),
        cost_estimate=cost(0, 8 * rows.size),
        name="unfold",
    )(rows)


def exchange(blocks, axis, groups=None):
    return lax.all_to_all(blocks, axis, split_axis=0, concat_axis=0, tiled=True, axis_index_groups=groups)


def spread(block, axis, count, groups=None):
    return exchange(jnp.broadcast_to(block, (count,) + block.shape), axis, groups)


def shards(state, depth, obs_cell, obs_value, obs_var):
    bands, tiles = lax.axis_size("space"), lax.axis_size("member")
    members, rows, fields, cols = state.shape
    ensemble, chips = tiles * members, tiles // 2
    sibling = [(i, i ^ 1) for i in range(tiles)]
    same_core = [[2 * q + core for q in range(chips)] for core in range(2)]

    state = state.transpose(0, 2, 1, 3)
    up = [(i, i + 1) for i in range(bands - 1)]
    down = [(i + 1, i) for i in range(bands - 1)]

    def edge(first):
        part = state[:, :, first:first + HALO].reshape(members * fields, HALO, cols)
        return jnp.concatenate([part, depth[None, first:first + HALO]], axis=0)

    above = lax.ppermute(edge(rows - HALO), "space", up)
    below = lax.ppermute(edge(0), "space", down)
    height, keep, send = forecast(state, above, below, depth, bands)

    def send_winds(first, last, after):
        parts, after = lax.optimization_barrier((winds[first:last], after))
        return [
            lax.ppermute(part, "member", [(i, i ^ (2 * k)) for i in range(tiles)])
            for k, part in zip(range(first, last), parts)
        ]

    def meet(parts, value):
        return lax.optimization_barrier((parts, value))

    third = (chips + 2) // 3
    winds = pack(keep, lax.ppermute(send, "member", sibling))
    height = exchange(height, "member").reshape(ensemble, cols)
    got = list(winds[:1])
    moved = send_winds(1, third, height)

    keep, send = gram_of(height, obs_cell[0], obs_value[0], obs_var[0], members)
    half = keep + lax.ppermute(send, "member", sibling)
    part = jnp.sum(exchange(half.reshape(bands, -1, ensemble), "space"), axis=0)
    moved, part = meet(moved, part)
    got, moved = got + list(moved), send_winds(third, 2 * third, part)
    part = jnp.sum(spread(part, "member", chips, same_core), axis=0)
    moved, part = meet(moved, part)
    got, moved = got + list(moved), send_winds(2 * third, chips, part)
    half = spread(part, "space", bands).reshape(ensemble // 2, ensemble)
    moved, half = meet(moved, half)
    got = got + list(moved)
    weights = transform(half, lax.ppermute(half, "member", sibling), members)

    analysed = mix(weights, height, got)
    back = exchange(analysed.reshape(tiles, members, fields * cols), "member").reshape(ensemble, fields * cols)
    return unfold(back, (members, fields, rows, cols)).transpose(0, 2, 1, 3)


def solution(mesh):
    placed = (
        P("member", "space", None, None),
        P("space", None),
        P("space", "member", None),
        P("space", "member", None),
        P("space", "member", None),
    )
    return jax.shard_map(
        shards,
        mesh=mesh,
        in_specs=placed,
        out_specs=P("member", "space", None, None),
        check_vma=False,
    )
```

```python
import functools

import jax
import jax.numpy as jnp
from jax import lax
from jax.experimental import pallas as pl
from jax.experimental.pallas import tpu as pltpu
from jax.sharding import PartitionSpec as P

STEPS = 3
NS_ITERS = 5
COURANT = 0.3
HALO = 2 * STEPS
LANES = 128
ROW_BLOCK = 4
MIX_BLOCK = 512
VMEM = 40 * 1024 * 1024
HIGHEST = lax.Precision.HIGHEST


def dot(a, b, dims=((1,), (0,))):
    return lax.dot_general(a, b, (dims, ((), ())), precision=HIGHEST, preferred_element_type=jnp.float32)


def cost(flops, bytes_accessed):
    return pl.CostEstimate(flops=flops, bytes_accessed=bytes_accessed, transcendentals=0)


def edges_kernel(top_ref, bottom_ref, depth_ref, down_ref, up_ref):
    members, fields, block, cols = top_ref.shape
    rows = depth_ref.shape[0]
    for out_ref, field_ref, last in ((down_ref, top_ref, False), (up_ref, bottom_ref, True)):
        for c in range(cols // LANES):
            lanes = slice(c * LANES, (c + 1) * LANES)
            at = 0
            for k in range(fields):
                count = HALO if k == 2 else HALO - 1
                first = block - count if last else 0
                for m in range(members):
                    out_ref[c, pl.ds(at + m, count, stride=members), :] = field_ref[m, k, first:first + count, lanes]
                at += count * members
            first = rows - HALO + 1 if last else 0
            out_ref[c, at:at + HALO - 1, :] = depth_ref[first:first + HALO - 1, lanes]


def edges(state, depth):
    members, fields, rows, cols = state.shape
    block = 8
    shape = jax.ShapeDtypeStruct((cols // LANES, (3 * HALO - 2) * members + 8, LANES), jnp.float32)
    return pl.pallas_call(
        edges_kernel,
        grid=(1,),
        in_specs=[
            pl.BlockSpec((members, fields, block, cols), lambda i: (0, 0, 0, 0)),
            pl.BlockSpec((members, fields, block, cols), lambda i: (0, 0, rows // block - 1, 0)),
            pl.BlockSpec(depth.shape, lambda i: (0, 0)),
        ],
        out_specs=[pl.BlockSpec(shape.shape, lambda i: (0, 0, 0))] * 2,
        out_shape=[shape] * 2,
        compiler_params=pltpu.CompilerParams(vmem_limit_bytes=VMEM),
        cost_estimate=cost(0, 4 * state.size),
        name="edges",
    )(state, state, depth)


def forecast_kernel(bands, state_ref, above_ref, below_ref, depth_ref, out_ref, field_ref, pull_ref):
    members, fields, rows, cols = state_ref.shape
    chunks = cols // LANES
    band = lax.axis_index("space")
    lane = lax.broadcasted_iota(jnp.int32, (1, LANES), 1)

    for c in range(chunks):
        lanes = slice(c * LANES, (c + 1) * LANES)
        at = 0
        for k in range(fields):
            count = HALO if k == 2 else HALO - 1
            size = count * members
            field_ref[k, c, (HALO - count) * members:HALO * members, :] = above_ref[c, at:at + size, :]
            field_ref[k, c, (HALO + rows) * members:(HALO + rows + count) * members, :] = below_ref[c, at:at + size, :]
            at += size
            for m in range(members):
                field_ref[k, c, pl.ds(HALO * members + m, rows, stride=members), :] = state_ref[m, k, :, lanes]
        pull_above = COURANT * above_ref[c, at:at + HALO - 1, :]
        pull_here = COURANT * depth_ref[:, lanes]
        pull_below = COURANT * below_ref[c, at:at + HALO - 1, :]
        for m in range(members):
            pull_ref[c, pl.ds(members + m, HALO - 1, stride=members), :] = pull_above
            pull_ref[c, pl.ds(HALO * members + m, rows, stride=members), :] = pull_here
            pull_ref[c, pl.ds((HALO + rows) * members + m, HALO - 1, stride=members), :] = pull_below

    def cols_diff(parts):
        left = [pltpu.roll(p, 1, 1) for p in parts]
        right = [pltpu.roll(p, LANES - 1, 1) for p in parts]
        return [
            jnp.where(lane == LANES - 1, right[(c + 1) % chunks], right[c]) - jnp.where(lane == 0, left[c - 1], left[c])
            for c in range(chunks)
        ]

    def take(k, first, count):
        return [field_ref[k, c, first * members:(first + count) * members, :] for c in range(chunks)]

    def push_of(first, count):
        if first >= HALO and first + count <= HALO + rows:
            return COURANT
        row = lax.broadcasted_iota(jnp.int32, (count * members, LANES), 0) + (first + band * rows - HALO) * members
        return jnp.where(jnp.logical_and(row >= 0, row < bands * rows * members), COURANT, 0.0)

    def blocks(first, last):
        cuts = sorted({HALO, HALO + rows} | set(range(HALO, HALO + rows, ROW_BLOCK)))
        ends = [first] + [e for e in cuts if first < e < last] + [last]
        return [(lo, hi - lo) for lo, hi in zip(ends[:-1], ends[1:])]

    for step in range(STEPS):
        reach = 2 * (STEPS - 1 - step)
        for first, count in blocks(HALO - reach - 1, HALO + rows + reach + 1):
            height = take(0, first, count)
            slope = cols_diff(take(1, first, count))
            north = take(2, first + 1, count)
            south = take(2, first - 1, count)
            span = slice(first * members, (first + count) * members)
            for c in range(chunks):
                field_ref[0, c, span, :] = height[c] - pull_ref[c, span, :] * (slope[c] + (north[c] - south[c]))
        for first, count in blocks(HALO - reach, HALO + rows + reach):
            slope = cols_diff(take(0, first, count))
            zonal = take(1, first, count)
            meridional = take(2, first, count)
            north = take(0, first + 1, count)
            south = take(0, first - 1, count)
            push = push_of(first, count)
            span = slice(first * members, (first + count) * members)
            for c in range(chunks):
                zonal[c] = zonal[c] - COURANT * slope[c]
                meridional[c] = meridional[c] - push * (north[c] - south[c])
                if step < STEPS - 1:
                    field_ref[1, c, span, :] = zonal[c]
                    field_ref[2, c, span, :] = meridional[c]
            if step == STEPS - 1:
                here = take(0, first, count)
                for k, parts in enumerate((here, zonal, meridional)):
                    for c in range(chunks):
                        for t in range(count):
                            out_ref[first - HALO + t, :, k * cols + c * LANES:k * cols + (c + 1) * LANES] = parts[c][t * members:(t + 1) * members]


def forecast(state, above, below, depth, bands):
    members, fields, rows, cols = state.shape
    total = rows + 2 * HALO
    return pl.pallas_call(
        functools.partial(forecast_kernel, bands),
        out_shape=jax.ShapeDtypeStruct((rows, members, fields * cols), jnp.float32),
        scratch_shapes=[
            pltpu.VMEM((fields, cols // LANES, total * members, LANES), jnp.float32),
            pltpu.VMEM((cols // LANES, total * members, LANES), jnp.float32),
        ],
        compiler_params=pltpu.CompilerParams(vmem_limit_bytes=VMEM),
        cost_estimate=cost(STEPS * 12 * state.size, 8 * state.size),
        name="forecast",
    )(state, above, below, depth)


def spots(count, block):
    i = lax.broadcasted_iota(jnp.int32, (count, count), 0)
    j = lax.broadcasted_iota(jnp.int32, (count, count), 1)
    return j == (i - i % block) + (i + 1) % block


def gram_kernel(block, cols, state_ref, cell_ref, value_ref, var_ref, keep_ref, send_ref, whole_ref):
    count = state_ref.shape[0]
    number = cell_ref.shape[1]
    picks = lax.broadcasted_iota(jnp.int32, (cols, number), 0) == cell_ref[...]
    seen = dot(state_ref[:, :cols], jnp.where(picks, 1.0, 0.0))
    centre = jnp.sum(seen, axis=0, keepdims=True) / count
    observed = seen - centre
    innovation = value_ref[...] - centre
    weighted = observed / var_ref[...]
    gram = dot(weighted, observed, ((1,), (1,)))
    projection = jnp.sum(weighted * innovation, axis=1, keepdims=True)
    whole_ref[...] = jnp.where(spots(count, block), projection, gram)
    half = count // 2
    core = lax.axis_index("member") % 2
    keep_ref[...] = whole_ref[pl.ds(pl.multiple_of(core * half, half), half), :]
    send_ref[...] = whole_ref[pl.ds(pl.multiple_of((1 - core) * half, half), half), :]


def gram_of(spread_state, cell, value, var, block, cols):
    count = spread_state.shape[0]
    return pl.pallas_call(
        functools.partial(gram_kernel, block, cols),
        out_shape=[jax.ShapeDtypeStruct((count // 2, count), jnp.float32)] * 2,
        scratch_shapes=[pltpu.VMEM((count, count), jnp.float32)],
        compiler_params=pltpu.CompilerParams(vmem_limit_bytes=VMEM),
        cost_estimate=cost(6 * 2 * count * cols * cell.shape[1], 4 * count * cols),
        name="gram",
    )(spread_state, cell, value, var)


def transform_kernel(block, keep_ref, got_ref, weights_ref, packed_ref):
    half, count = keep_ref.shape
    core = lax.axis_index("member") % 2
    packed_ref[pl.ds(pl.multiple_of(core * half, half), half), :] = keep_ref[...]
    packed_ref[pl.ds(pl.multiple_of((1 - core) * half, half), half), :] = got_ref[...]
    packed = packed_ref[...]
    places = spots(count, block)
    projection = jnp.sum(jnp.where(places, packed, 0.0), axis=1, keepdims=True)
    gram = jnp.where(places, packed.T, packed)
    i = lax.broadcasted_iota(jnp.int32, (count, count), 0)
    j = lax.broadcasted_iota(jnp.int32, (count, count), 1)
    identity = jnp.where(i == j, 1.0, 0.0)
    system = identity + gram / (count - 1)
    scale = jnp.sqrt(jnp.sum(jnp.sum(system * system, axis=1, keepdims=True), axis=0, keepdims=True))
    current = system / scale
    root_inv = identity
    for step in range(NS_ITERS):
        product = current if step == 0 else dot(root_inv, current)
        factor = 1.5 * identity - 0.5 * product
        if step == 0:
            current, root_inv = dot(current, factor), factor
        elif step < NS_ITERS - 1:
            both = dot(jnp.concatenate([current, root_inv], axis=0), factor)
            current, root_inv = both[:count], both[count:]
        else:
            root_inv = dot(root_inv, factor)
    root = root_inv / jnp.sqrt(scale)
    inner = dot(root, jnp.broadcast_to(projection, (count, 128)))
    mean_weights = dot(root, inner) / (count - 1)
    weights_ref[...] = mean_weights[:, :1] + root


def transform(keep, got, block):
    count = keep.shape[1]
    return pl.pallas_call(
        functools.partial(transform_kernel, block),
        out_shape=jax.ShapeDtypeStruct((count, count), jnp.float32),
        scratch_shapes=[pltpu.VMEM((count, count), jnp.float32)],
        compiler_params=pltpu.CompilerParams(vmem_limit_bytes=VMEM),
        cost_estimate=cost(6 * 2 * 14 * count ** 3, 8 * count ** 2),
        name="transform",
    )(keep, got)


def mix_kernel(weights_ref, state_ref, out_ref):
    weights = weights_ref[...]
    count, width = state_ref.shape
    for first in range(0, width, MIX_BLOCK):
        values = state_ref[:, first:first + MIX_BLOCK]
        centre = jnp.sum(values, axis=0, keepdims=True) / count
        out_ref[:, first:first + MIX_BLOCK] = centre + dot(weights, values - centre, ((0,), (0,)))


def mix(weights, spread_state):
    count, width = spread_state.shape
    return pl.pallas_call(
        mix_kernel,
        out_shape=jax.ShapeDtypeStruct((count, width), jnp.float32),
        compiler_params=pltpu.CompilerParams(vmem_limit_bytes=VMEM),
        cost_estimate=cost(6 * 2 * count * count * width, 8 * count * width),
        name="mix",
    )(weights, spread_state)


def unfold_kernel(rows_ref, out_ref, lanes_ref):
    members, fields, rows, cols = out_ref.shape
    for c in range(fields * cols // LANES):
        lanes_ref[c] = rows_ref[:, c * LANES:(c + 1) * LANES]
    for m in range(members):
        for k in range(fields):
            for c in range(cols // LANES):
                out_ref[m, k, :, c * LANES:(c + 1) * LANES] = lanes_ref[k * (cols // LANES) + c, pl.ds(m, rows, stride=members), :]


def unfold(rows, shape):
    return pl.pallas_call(
        unfold_kernel,
        out_shape=jax.ShapeDtypeStruct(shape, jnp.float32),
        scratch_shapes=[pltpu.VMEM((rows.shape[1] // LANES, rows.shape[0], LANES), jnp.float32)],
        compiler_params=pltpu.CompilerParams(vmem_limit_bytes=VMEM),
        cost_estimate=cost(0, 8 * rows.size),
        name="unfold",
    )(rows)


def exchange(blocks, axis, groups=None):
    return lax.all_to_all(blocks, axis, split_axis=0, concat_axis=0, tiled=True, axis_index_groups=groups)


def spread(block, axis, count, groups=None):
    return exchange(jnp.broadcast_to(block, (count,) + block.shape), axis, groups)


def shards(state, depth, obs_cell, obs_value, obs_var):
    bands, tiles = lax.axis_size("space"), lax.axis_size("member")
    members, rows, fields, cols = state.shape
    ensemble, chips = tiles * members, tiles // 2
    sibling = [(i, i ^ 1) for i in range(tiles)]
    same_core = [[2 * q + core for q in range(chips)] for core in range(2)]

    state = state.transpose(0, 2, 1, 3)
    up = [(i, i + 1) for i in range(bands - 1)]
    down = [(i + 1, i) for i in range(bands - 1)]

    to_below, to_above = edges(state, depth)
    above = lax.ppermute(to_above, "space", up)
    below = lax.ppermute(to_below, "space", down)
    ahead = forecast(state, above, below, depth, bands)
    ahead = exchange(ahead, "member").reshape(ensemble, fields * cols)

    keep, send = gram_of(ahead, obs_cell[0], obs_value[0], obs_var[0], members, cols)
    half = keep + lax.ppermute(send, "member", sibling)
    part = jnp.sum(exchange(half.reshape(bands, -1, ensemble), "space"), axis=0)
    part = jnp.sum(spread(part, "member", chips, same_core), axis=0)
    half = spread(part, "space", bands).reshape(ensemble // 2, ensemble)
    weights = transform(half, lax.ppermute(half, "member", sibling), members)

    analysed = mix(weights, ahead)
    back = exchange(analysed.reshape(tiles, members, fields * cols), "member").reshape(ensemble, fields * cols)
    return unfold(back, (members, fields, rows, cols)).transpose(0, 2, 1, 3)


def solution(mesh):
    placed = (
        P("member", "space", None, None),
        P("space", None),
        P("space", "member", None),
        P("space", "member", None),
        P("space", "member", None),
    )
    return jax.shard_map(
        shards,
        mesh=mesh,
        in_specs=placed,
        out_specs=P("member", "space", None, None),
        check_vma=False,
    )
```

```python
import functools

import jax
import jax.numpy as jnp
from jax import lax
from jax.experimental import pallas as pl
from jax.experimental.pallas import tpu as pltpu
from jax.sharding import PartitionSpec as P

STEPS = 3
NS_ITERS = 5
COURANT = 0.3
HALO = 2 * STEPS
LANES = 128
ROW_BLOCK = 4
VMEM = 40 * 1024 * 1024
HIGHEST = lax.Precision.HIGHEST


def dot(a, b, dims=((1,), (0,))):
    return lax.dot_general(a, b, (dims, ((), ())), precision=HIGHEST, preferred_element_type=jnp.float32)


def halves(a):
    high = a.astype(jnp.bfloat16)
    return high, (a - high.astype(jnp.float32)).astype(jnp.bfloat16)


def dot3(a, b, dims=((1,), (0,))):
    def one(x, y):
        return lax.dot_general(x, y, (dims, ((), ())), preferred_element_type=jnp.float32)

    (a_high, a_low), (b_high, b_low) = halves(a), halves(b)
    return one(a_high, b_high) + (one(a_high, b_low) + one(a_low, b_high))


def cost(flops, bytes_accessed):
    return pl.CostEstimate(flops=flops, bytes_accessed=bytes_accessed, transcendentals=0)


def edges_kernel(state_ref, depth_ref, down_ref, up_ref, top_ref, bottom_ref, sems):
    members, fields, block, cols = top_ref.shape
    rows = depth_ref.shape[0]
    copies = [
        pltpu.make_async_copy(state_ref.at[:, :, pl.ds(rows - block, block), :], bottom_ref, sems.at[1]),
        pltpu.make_async_copy(state_ref.at[:, :, pl.ds(0, block), :], top_ref, sems.at[0]),
    ]
    for copy in copies:
        copy.start()
    for copy, out_ref, field_ref, last in zip(copies, (up_ref, down_ref), (bottom_ref, top_ref), (True, False)):
        copy.wait()
        for c in range(cols // LANES):
            lanes = slice(c * LANES, (c + 1) * LANES)
            at = 0
            for k in range(fields):
                count = HALO if k == 2 else HALO - 1
                first = block - count if last else 0
                for m in range(members):
                    out_ref[c, pl.ds(at + m, count, stride=members), :] = field_ref[m, k, first:first + count, lanes]
                at += count * members
            first = rows - HALO + 1 if last else 0
            out_ref[c, at:at + HALO - 1, :] = depth_ref[first:first + HALO - 1, lanes]


def edges(state, depth):
    members, fields, rows, cols = state.shape
    block = 8
    shape = jax.ShapeDtypeStruct((cols // LANES, (3 * HALO - 2) * members + 8, LANES), jnp.float32)
    return pl.pallas_call(
        edges_kernel,
        in_specs=[pl.BlockSpec(memory_space=pltpu.HBM), pl.BlockSpec(memory_space=pltpu.VMEM)],
        out_shape=[shape] * 2,
        scratch_shapes=[
            pltpu.VMEM((members, fields, block, cols), jnp.float32),
            pltpu.VMEM((members, fields, block, cols), jnp.float32),
            pltpu.SemaphoreType.DMA((2,)),
        ],
        compiler_params=pltpu.CompilerParams(vmem_limit_bytes=VMEM),
        cost_estimate=cost(0, 2 * state.size),
        name="edges",
    )(state, depth)


def forecast_kernel(bands, state_ref, above_ref, below_ref, depth_ref, height_ref, keep_ref, send_ref, field_ref, pull_ref):
    members, fields, rows, cols = state_ref.shape
    chunks = cols // LANES
    band = lax.axis_index("space")
    lane = lax.broadcasted_iota(jnp.int32, (1, LANES), 1)

    for c in range(chunks):
        lanes = slice(c * LANES, (c + 1) * LANES)
        at = 0
        for k in range(fields):
            count = HALO if k == 2 else HALO - 1
            size = count * members
            field_ref[k, c, (HALO - count) * members:HALO * members, :] = above_ref[c, at:at + size, :]
            field_ref[k, c, (HALO + rows) * members:(HALO + rows + count) * members, :] = below_ref[c, at:at + size, :]
            at += size
            for m in range(members):
                field_ref[k, c, pl.ds(HALO * members + m, rows, stride=members), :] = state_ref[m, k, :, lanes]
        pull_above = COURANT * above_ref[c, at:at + HALO - 1, :]
        pull_here = COURANT * depth_ref[:, lanes]
        pull_below = COURANT * below_ref[c, at:at + HALO - 1, :]
        for m in range(members):
            pull_ref[c, pl.ds(members + m, HALO - 1, stride=members), :] = pull_above
            pull_ref[c, pl.ds(HALO * members + m, rows, stride=members), :] = pull_here
            pull_ref[c, pl.ds((HALO + rows) * members + m, HALO - 1, stride=members), :] = pull_below

    def cols_diff(parts):
        left = [pltpu.roll(p, 1, 1) for p in parts]
        right = [pltpu.roll(p, LANES - 1, 1) for p in parts]
        return [
            jnp.where(lane == LANES - 1, right[(c + 1) % chunks], right[c]) - jnp.where(lane == 0, left[c - 1], left[c])
            for c in range(chunks)
        ]

    def take(k, first, count):
        return [field_ref[k, c, first * members:(first + count) * members, :] for c in range(chunks)]

    def push_of(first, count):
        if first >= HALO and first + count <= HALO + rows:
            return COURANT
        row = lax.broadcasted_iota(jnp.int32, (count * members, LANES), 0) + (first + band * rows - HALO) * members
        return jnp.where(jnp.logical_and(row >= 0, row < bands * rows * members), COURANT, 0.0)

    def blocks(first, last):
        cuts = sorted({HALO, HALO + rows} | set(range(HALO, HALO + rows, ROW_BLOCK)))
        ends = [first] + [e for e in cuts if first < e < last] + [last]
        return [(lo, hi - lo) for lo, hi in zip(ends[:-1], ends[1:])]

    for step in range(STEPS):
        reach = 2 * (STEPS - 1 - step)
        for first, count in blocks(HALO - reach - 1, HALO + rows + reach + 1):
            height = take(0, first, count)
            slope = cols_diff(take(1, first, count))
            north = take(2, first + 1, count)
            south = take(2, first - 1, count)
            span = slice(first * members, (first + count) * members)
            for c in range(chunks):
                field_ref[0, c, span, :] = height[c] - pull_ref[c, span, :] * (slope[c] + (north[c] - south[c]))
        for first, count in blocks(HALO - reach, HALO + rows + reach):
            slope = cols_diff(take(0, first, count))
            zonal = take(1, first, count)
            meridional = take(2, first, count)
            north = take(0, first + 1, count)
            south = take(0, first - 1, count)
            push = push_of(first, count)
            span = slice(first * members, (first + count) * members)
            for c in range(chunks):
                zonal[c] = zonal[c] - COURANT * slope[c]
                meridional[c] = meridional[c] - push * (north[c] - south[c])
                field_ref[1, c, span, :] = zonal[c]
                field_ref[2, c, span, :] = meridional[c]

    core = lax.axis_index("member") % 2
    for c in range(chunks):
        for t in range(rows):
            height_ref[t, :, c * LANES:(c + 1) * LANES] = field_ref[0, c, (HALO + t) * members:(HALO + t + 1) * members, :]
    for k in range(rows // 2):
        partner = (lax.axis_index("member") // 2) ^ k
        for out_ref, other in ((keep_ref, core), (send_ref, 1 - core)):
            start = pl.multiple_of((HALO + 2 * partner + other) * members, members)
            for f in (1, 2):
                for c in range(chunks):
                    first = (f - 1) * cols + c * LANES
                    out_ref[k, :, first:first + LANES] = field_ref[f, c, pl.ds(start, members), :]


def forecast(state, above, below, depth, bands):
    members, fields, rows, cols = state.shape
    total = rows + 2 * HALO
    return pl.pallas_call(
        functools.partial(forecast_kernel, bands),
        out_shape=[
            jax.ShapeDtypeStruct((rows, members, cols), jnp.float32),
            jax.ShapeDtypeStruct((rows // 2, members, 2 * cols), jnp.float32),
            jax.ShapeDtypeStruct((rows // 2, members, 2 * cols), jnp.float32),
        ],
        scratch_shapes=[
            pltpu.VMEM((fields, cols // LANES, total * members, LANES), jnp.float32),
            pltpu.VMEM((cols // LANES, total * members, LANES), jnp.float32),
        ],
        compiler_params=pltpu.CompilerParams(vmem_limit_bytes=VMEM),
        cost_estimate=cost(STEPS * 12 * state.size, 8 * state.size),
        name="forecast",
    )(state, above, below, depth)


def pack_kernel(keep_ref, got_ref, *out_refs):
    core = lax.axis_index("member") % 2
    for kz, out_ref in enumerate(out_refs):
        for ky in range(out_ref.shape[0]):
            out_ref[ky, core] = keep_ref[ky * len(out_refs) + kz]
            out_ref[ky, 1 - core] = got_ref[ky * len(out_refs) + kz]


def pack(keep, got, across):
    chips, members, width = keep.shape
    return pl.pallas_call(
        pack_kernel,
        out_shape=[jax.ShapeDtypeStruct((chips // across, 2, members, width), jnp.float32)] * across,
        compiler_params=pltpu.CompilerParams(vmem_limit_bytes=VMEM),
        cost_estimate=cost(0, 16 * keep.size),
        name="pack",
    )(keep, got)


def turn_kernel(*refs):
    count = len(refs) // 2
    for kz in range(count):
        for ky in range(count):
            refs[count + ky][kz] = refs[kz][ky]


def turn(parts):
    return pl.pallas_call(
        turn_kernel,
        out_shape=[jax.ShapeDtypeStruct(parts[0].shape, jnp.float32)] * len(parts),
        compiler_params=pltpu.CompilerParams(vmem_limit_bytes=VMEM),
        cost_estimate=cost(0, 8 * parts[0].size * len(parts)),
        name="turn",
    )(*parts)


def spots(count, block):
    i = lax.broadcasted_iota(jnp.int32, (count, count), 0)
    j = lax.broadcasted_iota(jnp.int32, (count, count), 1)
    return j == (i - i % block) + (i + 1) % block


def gram_kernel(block, height_ref, cell_ref, value_ref, var_ref, keep_ref, send_ref, whole_ref):
    count, cols = height_ref.shape
    number = cell_ref.shape[1]
    picks = lax.broadcasted_iota(jnp.int32, (cols, number), 0) == cell_ref[...]
    seen = dot(height_ref[...], jnp.where(picks, 1.0, 0.0))
    centre = jnp.sum(seen, axis=0, keepdims=True) / count
    observed = seen - centre
    innovation = value_ref[...] - centre
    weighted = observed / var_ref[...]
    gram = dot(weighted, observed, ((1,), (1,)))
    projection = jnp.sum(weighted * innovation, axis=1, keepdims=True)
    whole_ref[...] = jnp.where(spots(count, block), projection, gram)
    half = count // 2
    core = lax.axis_index("member") % 2
    keep_ref[...] = whole_ref[pl.ds(pl.multiple_of(core * half, half), half), :]
    send_ref[...] = whole_ref[pl.ds(pl.multiple_of((1 - core) * half, half), half), :]


def gram_of(height, cell, value, var, block):
    count, cols = height.shape
    return pl.pallas_call(
        functools.partial(gram_kernel, block),
        out_shape=[jax.ShapeDtypeStruct((count // 2, count), jnp.float32)] * 2,
        scratch_shapes=[pltpu.VMEM((count, count), jnp.float32)],
        compiler_params=pltpu.CompilerParams(vmem_limit_bytes=VMEM),
        cost_estimate=cost(6 * 2 * count * cols * cell.shape[1], 4 * count * cols),
        name="gram",
    )(height, cell, value, var)


def transform_kernel(block, keep_ref, got_ref, weights_ref, packed_ref):
    half, count = keep_ref.shape
    core = lax.axis_index("member") % 2
    packed_ref[pl.ds(pl.multiple_of(core * half, half), half), :] = keep_ref[...]
    packed_ref[pl.ds(pl.multiple_of((1 - core) * half, half), half), :] = got_ref[...]
    packed = packed_ref[...]
    places = spots(count, block)
    projection = jnp.sum(jnp.where(places, packed, 0.0), axis=1, keepdims=True)
    gram = jnp.where(places, packed.T, packed)
    i = lax.broadcasted_iota(jnp.int32, (count, count), 0)
    j = lax.broadcasted_iota(jnp.int32, (count, count), 1)
    identity = jnp.where(i == j, 1.0, 0.0)
    system = identity + gram / (count - 1)
    scale = jnp.sqrt(jnp.sum(jnp.sum(system * system, axis=1, keepdims=True), axis=0, keepdims=True))
    current = system / scale
    root_inv = identity
    for step in range(NS_ITERS):
        product = current if step == 0 else dot3(root_inv, current)
        factor = 1.5 * identity - 0.5 * product
        if step < NS_ITERS - 1:
            current = dot3(current, factor)
        root_inv = factor if step == 0 else dot3(factor, root_inv)
    root = root_inv / jnp.sqrt(scale)

    def times(column):
        return jnp.sum(root * jnp.sum(jnp.where(i == j, column, 0.0), axis=0, keepdims=True), axis=1, keepdims=True)

    weights_ref[...] = times(times(projection)) / (count - 1) + root


def transform(keep, got, block):
    count = keep.shape[1]
    return pl.pallas_call(
        functools.partial(transform_kernel, block),
        out_shape=jax.ShapeDtypeStruct((count, count), jnp.float32),
        scratch_shapes=[pltpu.VMEM((count, count), jnp.float32)],
        compiler_params=pltpu.CompilerParams(vmem_limit_bytes=VMEM),
        cost_estimate=cost(6 * 2 * 14 * count ** 3, 8 * count ** 2),
        name="transform",
    )(keep, got)


def mix_kernel(weights_ref, height_ref, *refs):
    wind_refs, out_ref, order_ref = refs[:-2], refs[-2], refs[-1]
    count, cols = height_ref.shape
    each = count // len(wind_refs)
    group = each // wind_refs[0].shape[0]
    chip = lax.axis_index("member") // 2
    for k in range(count // group):
        order_ref[k * group:(k + 1) * group, :] = weights_ref[pl.ds(pl.multiple_of((chip ^ k) * group, group), group), :]

    def mixed(values, coefficients):
        centre = jnp.sum(values, axis=0, keepdims=True) / count
        return centre + dot3(coefficients, values - centre, ((0,), (0,)))

    out_ref[:, :cols] = mixed(height_ref[...], weights_ref[...])
    for f in (1, 2):
        values = jnp.concatenate([w[:, :, :, (f - 1) * cols:f * cols].reshape(each, cols) for w in wind_refs], axis=0)
        out_ref[:, f * cols:(f + 1) * cols] = mixed(values, order_ref[...])


def mix(weights, height, winds):
    count, cols = height.shape
    return pl.pallas_call(
        mix_kernel,
        out_shape=jax.ShapeDtypeStruct((count, 3 * cols), jnp.float32),
        scratch_shapes=[pltpu.VMEM((count, count), jnp.float32)],
        compiler_params=pltpu.CompilerParams(vmem_limit_bytes=VMEM),
        cost_estimate=cost(6 * 2 * count * count * 3 * cols, 4 * count * 6 * cols),
        name="mix",
    )(weights, height, *winds)


def unfold_kernel(rows_ref, out_ref, lanes_ref):
    members, fields, rows, cols = out_ref.shape
    for c in range(fields * cols // LANES):
        lanes_ref[c] = rows_ref[:, c * LANES:(c + 1) * LANES]
    for m in range(members):
        for k in range(fields):
            for c in range(cols // LANES):
                out_ref[m, k, :, c * LANES:(c + 1) * LANES] = lanes_ref[k * (cols // LANES) + c, pl.ds(m, rows, stride=members), :]


def unfold(rows, shape):
    return pl.pallas_call(
        unfold_kernel,
        out_shape=jax.ShapeDtypeStruct(shape, jnp.float32),
        scratch_shapes=[pltpu.VMEM((rows.shape[1] // LANES, rows.shape[0], LANES), jnp.float32)],
        compiler_params=pltpu.CompilerParams(vmem_limit_bytes=VMEM),
        cost_estimate=cost(0, 8 * rows.size),
        name="unfold",
    )(rows)


def exchange(blocks, axis, groups=None):
    return lax.all_to_all(blocks, axis, split_axis=0, concat_axis=0, tiled=True, axis_index_groups=groups)


def spread(block, axis, count, groups=None):
    return exchange(jnp.broadcast_to(block, (count,) + block.shape), axis, groups)


def shards(state, depth, obs_cell, obs_value, obs_var):
    bands, tiles = lax.axis_size("space"), lax.axis_size("member")
    members, rows, fields, cols = state.shape
    ensemble, chips = tiles * members, tiles // 2
    sibling = [(i, i ^ 1) for i in range(tiles)]
    same_core = [[2 * q + core for q in range(chips)] for core in range(2)]

    state = state.transpose(0, 2, 1, 3)
    up = [(i, i + 1) for i in range(bands - 1)]
    down = [(i + 1, i) for i in range(bands - 1)]

    to_below, to_above = edges(state, depth)
    above = lax.ppermute(to_above, "space", up)
    below = lax.ppermute(to_below, "space", down)
    height, keep, send = forecast(state, above, below, depth, bands)
    across = 4 if chips == 16 else 2

    def swap(part, k, unit):
        return lax.ppermute(part, "member", [(i, i ^ (2 * unit * k)) for i in range(tiles)])

    def meet(*values):
        return lax.optimization_barrier(values)

    parts = list(pack(keep, lax.ppermute(send, "member", sibling), across))
    height = exchange(height, "member").reshape(ensemble, cols)
    parts, height = meet(parts, height)
    odd, even = range(1, across, 2), range(2, across, 2)
    keep, send = gram_of(height, obs_cell[0], obs_value[0], obs_var[0], members)
    half = keep + lax.ppermute(send, "member", sibling)
    half, parts = meet(half, parts)
    for k in odd:
        parts[k] = swap(parts[k], k, 1)
    part = jnp.sum(exchange(half.reshape(bands, -1, ensemble), "space"), axis=0)
    part, parts = meet(part, parts)
    for k in even:
        parts[k] = swap(parts[k], k, 1)
    part = jnp.sum(spread(part, "member", chips, same_core), axis=0)
    part, parts = meet(part, list(turn(parts)))
    for k in odd:
        parts[k] = swap(parts[k], k, across)
    half = spread(part, "space", bands).reshape(ensemble // 2, ensemble)
    half, parts = meet(half, parts)
    for k in even:
        parts[k] = swap(parts[k], k, across)
    weights = transform(half, lax.ppermute(half, "member", sibling), members)

    analysed = mix(weights, height, parts)
    back = exchange(analysed.reshape(tiles, members, fields * cols), "member").reshape(ensemble, fields * cols)
    return unfold(back, (members, fields, rows, cols)).transpose(0, 2, 1, 3)


def solution(mesh):
    placed = (
        P("member", "space", None, None),
        P("space", None),
        P("space", "member", None),
        P("space", "member", None),
        P("space", "member", None),
    )
    return jax.shard_map(
        shards,
        mesh=mesh,
        in_specs=placed,
        out_specs=P("member", "space", None, None),
        check_vma=False,
    )
```

```python
import functools

import jax
import jax.numpy as jnp
from jax import lax
from jax.experimental import pallas as pl
from jax.experimental.pallas import tpu as pltpu
from jax.sharding import PartitionSpec as P

STEPS = 3
NS_ITERS = 5
COURANT = 0.3
HALO = 2 * STEPS
LANES = 128
ROW_BLOCK = 4
VMEM = 40 * 1024 * 1024
ALL_VMEM = 60 * 1024 * 1024
HIGHEST = lax.Precision.HIGHEST


def dot(a, b, dims=((1,), (0,))):
    return lax.dot_general(a, b, (dims, ((), ())), precision=HIGHEST, preferred_element_type=jnp.float32)


def halves(a):
    high = a.astype(jnp.bfloat16)
    return high, (a - high.astype(jnp.float32)).astype(jnp.bfloat16)


def dot3(a, b, dims=((1,), (0,))):
    def one(x, y):
        return lax.dot_general(x, y, (dims, ((), ())), preferred_element_type=jnp.float32)

    (a_high, a_low), (b_high, b_low) = a, b
    return one(a_high, b_high) + (one(a_high, b_low) + one(a_low, b_high))


def cost(flops, bytes_accessed):
    return pl.CostEstimate(flops=flops, bytes_accessed=bytes_accessed, transcendentals=0)


def edges_kernel(state_ref, depth_ref, down_ref, up_ref, top_ref, bottom_ref, sems):
    members, fields, block, cols = top_ref.shape
    rows = depth_ref.shape[0]
    copies = [
        pltpu.make_async_copy(state_ref.at[:, :, pl.ds(rows - block, block), :], bottom_ref, sems.at[1]),
        pltpu.make_async_copy(state_ref.at[:, :, pl.ds(0, block), :], top_ref, sems.at[0]),
    ]
    for copy in copies:
        copy.start()
    for copy, out_ref, field_ref, last in zip(copies, (up_ref, down_ref), (bottom_ref, top_ref), (True, False)):
        copy.wait()
        for c in range(cols // LANES):
            lanes = slice(c * LANES, (c + 1) * LANES)
            at = 0
            for k in range(fields):
                count = HALO if k == 2 else HALO - 1
                first = block - count if last else 0
                for m in range(members):
                    out_ref[c, pl.ds(at + m, count, stride=members), :] = field_ref[m, k, first:first + count, lanes]
                at += count * members
            first = rows - HALO + 1 if last else 0
            out_ref[c, at:at + HALO - 1, :] = depth_ref[first:first + HALO - 1, lanes]


def edges(state, depth):
    members, fields, rows, cols = state.shape
    block = 8
    shape = jax.ShapeDtypeStruct((cols // LANES, (3 * HALO - 2) * members + 8, LANES), jnp.float32)
    return pl.pallas_call(
        edges_kernel,
        in_specs=[pl.BlockSpec(memory_space=pl.ANY), pl.BlockSpec(memory_space=pltpu.VMEM)],
        out_shape=[shape] * 2,
        scratch_shapes=[
            pltpu.VMEM((members, fields, block, cols), jnp.float32),
            pltpu.VMEM((members, fields, block, cols), jnp.float32),
            pltpu.SemaphoreType.DMA((2,)),
        ],
        compiler_params=pltpu.CompilerParams(vmem_limit_bytes=ALL_VMEM),
        cost_estimate=cost(0, 2 * state.size),
        name="edges",
    )(state, depth)


def forecast_kernel(bands, state_ref, above_ref, below_ref, depth_ref, out_ref, field_ref, pull_ref):
    members, fields, rows, cols = state_ref.shape
    chunks = cols // LANES
    band = lax.axis_index("space")
    lane = lax.broadcasted_iota(jnp.int32, (1, LANES), 1)

    for c in range(chunks):
        lanes = slice(c * LANES, (c + 1) * LANES)
        at = 0
        for k in range(fields):
            count = HALO if k == 2 else HALO - 1
            size = count * members
            field_ref[k, c, (HALO - count) * members:HALO * members, :] = above_ref[c, at:at + size, :]
            field_ref[k, c, (HALO + rows) * members:(HALO + rows + count) * members, :] = below_ref[c, at:at + size, :]
            at += size
            for m in range(members):
                field_ref[k, c, pl.ds(HALO * members + m, rows, stride=members), :] = state_ref[m, k, :, lanes]
        pull_above = COURANT * above_ref[c, at:at + HALO - 1, :]
        pull_here = COURANT * depth_ref[:, lanes]
        pull_below = COURANT * below_ref[c, at:at + HALO - 1, :]
        for m in range(members):
            pull_ref[c, pl.ds(members + m, HALO - 1, stride=members), :] = pull_above
            pull_ref[c, pl.ds(HALO * members + m, rows, stride=members), :] = pull_here
            pull_ref[c, pl.ds((HALO + rows) * members + m, HALO - 1, stride=members), :] = pull_below

    def cols_diff(parts):
        left = [pltpu.roll(p, 1, 1) for p in parts]
        right = [pltpu.roll(p, LANES - 1, 1) for p in parts]
        return [
            jnp.where(lane == LANES - 1, right[(c + 1) % chunks], right[c]) - jnp.where(lane == 0, left[c - 1], left[c])
            for c in range(chunks)
        ]

    def take(k, first, count):
        return [field_ref[k, c, first * members:(first + count) * members, :] for c in range(chunks)]

    def push_of(first, count):
        if first >= HALO and first + count <= HALO + rows:
            return COURANT
        row = lax.broadcasted_iota(jnp.int32, (count * members, LANES), 0) + (first + band * rows - HALO) * members
        return jnp.where(jnp.logical_and(row >= 0, row < bands * rows * members), COURANT, 0.0)

    def blocks(first, last):
        cuts = sorted({HALO, HALO + rows} | set(range(HALO, HALO + rows, ROW_BLOCK)))
        ends = [first] + [e for e in cuts if first < e < last] + [last]
        return [(lo, hi - lo) for lo, hi in zip(ends[:-1], ends[1:])]

    for step in range(STEPS):
        reach = 2 * (STEPS - 1 - step)
        for first, count in blocks(HALO - reach - 1, HALO + rows + reach + 1):
            height = take(0, first, count)
            slope = cols_diff(take(1, first, count))
            north = take(2, first + 1, count)
            south = take(2, first - 1, count)
            span = slice(first * members, (first + count) * members)
            for c in range(chunks):
                field_ref[0, c, span, :] = height[c] - pull_ref[c, span, :] * (slope[c] + (north[c] - south[c]))
        for first, count in blocks(HALO - reach, HALO + rows + reach):
            slope = cols_diff(take(0, first, count))
            zonal = take(1, first, count)
            meridional = take(2, first, count)
            north = take(0, first + 1, count)
            south = take(0, first - 1, count)
            push = push_of(first, count)
            span = slice(first * members, (first + count) * members)
            for c in range(chunks):
                zonal[c] = zonal[c] - COURANT * slope[c]
                meridional[c] = meridional[c] - push * (north[c] - south[c])
                if step < STEPS - 1:
                    field_ref[1, c, span, :] = zonal[c]
                    field_ref[2, c, span, :] = meridional[c]
            if step == STEPS - 1:
                here = take(0, first, count)
                for k, parts in enumerate((here, zonal, meridional)):
                    for c in range(chunks):
                        for t in range(count):
                            out_ref[first - HALO + t, :, k * cols + c * LANES:k * cols + (c + 1) * LANES] = parts[c][t * members:(t + 1) * members]


def forecast(state, above, below, depth, bands):
    members, fields, rows, cols = state.shape
    total = rows + 2 * HALO
    return pl.pallas_call(
        functools.partial(forecast_kernel, bands),
        out_shape=jax.ShapeDtypeStruct((rows, members, fields * cols), jnp.float32),
        scratch_shapes=[
            pltpu.VMEM((fields, cols // LANES, total * members, LANES), jnp.float32),
            pltpu.VMEM((cols // LANES, total * members, LANES), jnp.float32),
        ],
        compiler_params=pltpu.CompilerParams(vmem_limit_bytes=VMEM),
        cost_estimate=cost(STEPS * 12 * state.size, 8 * state.size),
        name="forecast",
    )(state, above, below, depth)


def pick_kernel(first, state_ref, out_ref):
    chips, members, width = out_ref.shape
    other = 1 - lax.axis_index("member") % 2
    out_ref[...] = state_ref[:, pl.ds(other, 1), :, first:first + width].reshape(out_ref.shape)


def pick(state, first, last):
    chips, cores, members, _ = state.shape
    shape = jax.ShapeDtypeStruct((chips, members, last - first), jnp.float32)
    return pl.pallas_call(
        functools.partial(pick_kernel, first),
        out_shape=shape,
        compiler_params=pltpu.CompilerParams(vmem_limit_bytes=VMEM),
        cost_estimate=cost(0, 8 * shape.size),
        name="pick",
    )(state)


def spots(count, block):
    i = lax.broadcasted_iota(jnp.int32, (count, count), 0)
    j = lax.broadcasted_iota(jnp.int32, (count, count), 1)
    return j == (i - i % block) + (i + 1) % block


def gram_kernel(state_ref, got_ref, cell_ref, value_ref, var_ref, keep_ref, send_ref, seen_ref, whole_ref):
    chips, cores, members, _ = state_ref.shape
    cols, number = got_ref.shape[2], cell_ref.shape[1]
    count, half = chips * cores * members, chips * members
    core = lax.axis_index("member") % cores
    picks = lax.broadcasted_iota(jnp.int32, (cols, number), 0) == cell_ref[...]
    picks = jnp.where(picks, 1.0, 0.0)
    own = state_ref[:, pl.ds(core, 1), :, :cols].reshape(half, cols)
    seen_ref[:, pl.ds(core, 1)] = dot(own, picks).reshape(chips, 1, members, number)
    seen_ref[:, pl.ds(1 - core, 1)] = dot(got_ref[...].reshape(half, cols), picks).reshape(chips, 1, members, number)
    seen = seen_ref[...].reshape(count, number)
    centre = jnp.sum(seen, axis=0, keepdims=True) / count
    observed = seen - centre
    innovation = value_ref[...] - centre
    weighted = observed / var_ref[...]
    gram = dot(weighted, observed, ((1,), (1,)))
    projection = jnp.sum(weighted * innovation, axis=1, keepdims=True)
    whole_ref[...] = jnp.where(spots(count, members), projection, gram)
    keep_ref[...] = whole_ref[pl.ds(pl.multiple_of(core * half, half), half), :]
    send_ref[...] = whole_ref[pl.ds(pl.multiple_of((1 - core) * half, half), half), :]


def gram_of(state, got, cell, value, var):
    chips, cores, members, _ = state.shape
    count, number = chips * cores * members, cell.shape[1]
    return pl.pallas_call(
        gram_kernel,
        out_shape=[jax.ShapeDtypeStruct((count // 2, count), jnp.float32)] * 2,
        scratch_shapes=[
            pltpu.VMEM((chips, cores, members, number), jnp.float32),
            pltpu.VMEM((count, count), jnp.float32),
        ],
        compiler_params=pltpu.CompilerParams(vmem_limit_bytes=VMEM),
        cost_estimate=cost(6 * 4 * got.size * number, 8 * got.size),
        name="gram",
    )(state, got, cell, value, var)


def transform_kernel(block, keep_ref, got_ref, weights_ref, packed_ref):
    half, count = keep_ref.shape
    core = lax.axis_index("member") % 2
    packed_ref[pl.ds(pl.multiple_of(core * half, half), half), :] = keep_ref[...]
    packed_ref[pl.ds(pl.multiple_of((1 - core) * half, half), half), :] = got_ref[...]
    packed = packed_ref[...]
    places = spots(count, block)
    projection = jnp.sum(jnp.where(places, packed, 0.0), axis=1, keepdims=True)
    gram = jnp.where(places, packed.T, packed)
    i = lax.broadcasted_iota(jnp.int32, (count, count), 0)
    j = lax.broadcasted_iota(jnp.int32, (count, count), 1)
    identity = jnp.where(i == j, 1.0, 0.0)
    system = identity + gram / (count - 1)
    scale = jnp.sqrt(jnp.sum(jnp.sum(system * system, axis=1, keepdims=True), axis=0, keepdims=True))
    current = system / scale
    root_inv = identity
    for step in range(NS_ITERS):
        parts, inv_parts = halves(current), halves(root_inv)
        product = current if step == 0 else dot3(inv_parts, parts)
        factor = 1.5 * identity - 0.5 * product
        factor_parts = halves(factor)
        if step < NS_ITERS - 1:
            current = dot3(parts, factor_parts)
        root_inv = factor if step == 0 else dot3(factor_parts, inv_parts)
    root = root_inv / jnp.sqrt(scale)

    def times(column):
        return jnp.sum(root * jnp.sum(jnp.where(i == j, column, 0.0), axis=0, keepdims=True), axis=1, keepdims=True)

    weights_ref[...] = times(times(projection)) / (count - 1) + root


def transform(keep, got, block):
    count = keep.shape[1]
    return pl.pallas_call(
        functools.partial(transform_kernel, block),
        out_shape=jax.ShapeDtypeStruct((count, count), jnp.float32),
        scratch_shapes=[pltpu.VMEM((count, count), jnp.float32)],
        compiler_params=pltpu.CompilerParams(vmem_limit_bytes=VMEM),
        cost_estimate=cost(6 * 2 * 14 * count ** 3, 8 * count ** 2),
        name="transform",
    )(keep, got)


def mix_kernel(weights_ref, state_ref, got_height_ref, got_wind_ref, out_ref, order_ref):
    chips, cores, members, width = state_ref.shape
    cols, half, count = got_height_ref.shape[2], chips * members, chips * cores * members
    core = lax.axis_index("member") % cores
    for q in range(chips):
        for side, other in ((0, core), (1, 1 - core)):
            start = pl.multiple_of((q * cores + other) * members, members)
            order_ref[side * half + q * members:side * half + (q + 1) * members, :] = weights_ref[pl.ds(start, members), :]
    order = halves(order_ref[...])
    for first in range(0, width, cols):
        own = state_ref[:, pl.ds(core, 1), :, first:first + cols].reshape(half, cols)
        got = got_height_ref[...] if first == 0 else got_wind_ref[:, :, first - cols:first]
        values = jnp.concatenate([own, got.reshape(half, cols)], axis=0)
        centre = jnp.sum(values, axis=0, keepdims=True) / count
        mixed = centre + dot3(order, halves(values - centre), ((0,), (0,)))
        out_ref[:, :, :, first:first + cols] = mixed.reshape(chips, cores, members, cols)


def mix(weights, state, got_height, got_wind):
    count = weights.shape[0]
    return pl.pallas_call(
        mix_kernel,
        out_shape=jax.ShapeDtypeStruct(state.shape, jnp.float32),
        scratch_shapes=[pltpu.VMEM(weights.shape, jnp.float32)],
        compiler_params=pltpu.CompilerParams(vmem_limit_bytes=VMEM),
        cost_estimate=cost(3 * 2 * count * state.size, 8 * state.size),
        name="mix",
    )(weights, state, got_height, got_wind)


def unfold_kernel(state_ref, got_ref, out_ref, lanes_ref):
    members, fields, rows, cols = out_ref.shape
    core = lax.axis_index("member") % 2
    for c in range(fields * cols // LANES):
        lanes = slice(c * LANES, (c + 1) * LANES)
        for q in range(rows // 2):
            own = pl.multiple_of((2 * q + core) * members, members)
            other = pl.multiple_of((2 * q + 1 - core) * members, members)
            lanes_ref[c, pl.ds(own, members), :] = state_ref[q, pl.ds(core, 1), :, lanes].reshape(members, LANES)
            lanes_ref[c, pl.ds(other, members), :] = got_ref[q, :, lanes]
    for m in range(members):
        for k in range(fields):
            for c in range(cols // LANES):
                out_ref[m, k, :, c * LANES:(c + 1) * LANES] = lanes_ref[k * (cols // LANES) + c, pl.ds(m, rows, stride=members), :]


def unfold(state, got, shape):
    return pl.pallas_call(
        unfold_kernel,
        out_shape=jax.ShapeDtypeStruct(shape, jnp.float32),
        scratch_shapes=[pltpu.VMEM((shape[1] * shape[3] // LANES, shape[0] * shape[2], LANES), jnp.float32)],
        compiler_params=pltpu.CompilerParams(vmem_limit_bytes=VMEM),
        cost_estimate=cost(0, 8 * state.size),
        name="unfold",
    )(state, got)


def exchange(blocks, axis, groups=None):
    return lax.all_to_all(blocks, axis, split_axis=0, concat_axis=0, tiled=True, axis_index_groups=groups)


def spread(block, axis, count, groups=None):
    return exchange(jnp.broadcast_to(block, (count,) + block.shape), axis, groups)


def shards(state, depth, obs_cell, obs_value, obs_var):
    bands, tiles = lax.axis_size("space"), lax.axis_size("member")
    members, rows, fields, cols = state.shape
    ensemble, chips = tiles * members, tiles // 2
    sibling = [(i, i ^ 1) for i in range(tiles)]
    same_core = [[2 * q + core for q in range(chips)] for core in range(2)]

    state = state.transpose(0, 2, 1, 3)
    up = [(i, i + 1) for i in range(bands - 1)]
    down = [(i + 1, i) for i in range(bands - 1)]

    to_below, to_above = edges(state, depth)
    above = lax.ppermute(to_above, "space", up)
    below = lax.ppermute(to_below, "space", down)
    ahead = forecast(state, above, below, depth, bands).reshape(chips, 2, members, fields * cols)

    def to_sibling(values, first, last):
        return lax.ppermute(pick(values, first, last), "member", sibling)

    ahead = exchange(ahead, "member", same_core)
    got_height = to_sibling(ahead, 0, cols)
    got_wind = to_sibling(ahead, cols, fields * cols)

    keep, send = gram_of(ahead, got_height, obs_cell[0], obs_value[0], obs_var[0])
    half = keep + lax.ppermute(send, "member", sibling)
    part = jnp.sum(exchange(half.reshape(bands, -1, ensemble), "space"), axis=0)
    part = jnp.sum(spread(part, "member", chips, same_core), axis=0)
    half = spread(part, "space", bands).reshape(ensemble // 2, ensemble)
    weights = transform(half, lax.ppermute(half, "member", sibling), members)

    analysed = exchange(mix(weights, ahead, got_height, got_wind), "member", same_core)
    got = to_sibling(analysed, 0, fields * cols)
    return unfold(analysed, got, (members, fields, rows, cols)).transpose(0, 2, 1, 3)


def solution(mesh):
    placed = (
        P("member", "space", None, None),
        P("space", None),
        P("space", "member", None),
        P("space", "member", None),
        P("space", "member", None),
    )
    return jax.shard_map(
        shards,
        mesh=mesh,
        in_specs=placed,
        out_specs=P("member", "space", None, None),
        check_vma=False,
    )
```

```python
import functools

import jax
import jax.numpy as jnp
from jax import lax
from jax.experimental import pallas as pl
from jax.experimental.pallas import tpu as pltpu
from jax.sharding import PartitionSpec as P

STEPS = 3
NS_ITERS = 5
COURANT = 0.3
HALO = 2 * STEPS
LANES = 128
ROW_BLOCK = 4
MIX_BLOCK = 512
VMEM = 40 * 1024 * 1024
ALL_VMEM = 60 * 1024 * 1024
HIGHEST = lax.Precision.HIGHEST


def dot(a, b, dims=((1,), (0,))):
    return lax.dot_general(a, b, (dims, ((), ())), precision=HIGHEST, preferred_element_type=jnp.float32)


def halves(a):
    high = a.astype(jnp.bfloat16)
    return high, (a - high.astype(jnp.float32)).astype(jnp.bfloat16)


def dot3(a, b, dims=((1,), (0,))):
    def one(x, y):
        return lax.dot_general(x, y, (dims, ((), ())), preferred_element_type=jnp.float32)

    (a_high, a_low), (b_high, b_low) = a, b
    return one(a_high, b_high) + (one(a_high, b_low) + one(a_low, b_high))


def cost(flops, bytes_accessed):
    return pl.CostEstimate(flops=flops, bytes_accessed=bytes_accessed, transcendentals=0)


def edges_kernel(state_ref, depth_ref, down_ref, up_ref, top_ref, bottom_ref, depth_top_ref, depth_bottom_ref, sems):
    members, fields, block, cols = top_ref.shape
    rows = depth_ref.shape[0]
    sides = (
        (up_ref, bottom_ref, depth_bottom_ref, rows - block, True),
        (down_ref, top_ref, depth_top_ref, 0, False),
    )
    copies = []
    for side, (_, field_ref, edge_ref, start, _) in enumerate(sides):
        copies.append([
            pltpu.make_async_copy(state_ref.at[m, :, pl.ds(start, block), :], field_ref.at[m], sems.at[side, m])
            for m in range(members)
        ] + [pltpu.make_async_copy(depth_ref.at[pl.ds(start, block), :], edge_ref, sems.at[side, members])])
        for copy in copies[-1]:
            copy.start()
    for (out_ref, field_ref, edge_ref, _, last), waits in zip(sides, copies):
        for copy in waits:
            copy.wait()
        for c in range(cols // LANES):
            lanes = slice(c * LANES, (c + 1) * LANES)
            at = 0
            for k in range(fields):
                count = HALO if k == 2 else HALO - 1
                first = block - count if last else 0
                for m in range(members):
                    out_ref[c, pl.ds(at + m, count, stride=members), :] = field_ref[m, k, first:first + count, lanes]
                at += count * members
            first = block - HALO + 1 if last else 0
            out_ref[c, at:at + HALO - 1, :] = edge_ref[first:first + HALO - 1, lanes]


def edges(state, depth):
    members, fields, rows, cols = state.shape
    block = 8
    shape = jax.ShapeDtypeStruct((cols // LANES, (3 * HALO - 2) * members + 8, LANES), jnp.float32)
    return pl.pallas_call(
        edges_kernel,
        in_specs=[pl.BlockSpec(memory_space=pl.ANY)] * 2,
        out_shape=[shape] * 2,
        scratch_shapes=[
            pltpu.VMEM((members, fields, block, cols), jnp.float32),
            pltpu.VMEM((members, fields, block, cols), jnp.float32),
            pltpu.VMEM((block, cols), jnp.float32),
            pltpu.VMEM((block, cols), jnp.float32),
            pltpu.SemaphoreType.DMA((2, members + 1)),
        ],
        compiler_params=pltpu.CompilerParams(vmem_limit_bytes=ALL_VMEM),
        cost_estimate=cost(0, 2 * state.size),
        name="edges",
    )(state, depth)


def forecast_kernel(bands, state_ref, above_ref, below_ref, depth_ref, out_ref, field_ref, pull_ref):
    members, fields, rows, cols = state_ref.shape
    chunks = cols // LANES
    band = lax.axis_index("space")
    lane = lax.broadcasted_iota(jnp.int32, (1, LANES), 1)

    for c in range(chunks):
        lanes = slice(c * LANES, (c + 1) * LANES)
        at = 0
        for k in range(fields):
            count = HALO if k == 2 else HALO - 1
            size = count * members
            field_ref[k, c, (HALO - count) * members:HALO * members, :] = above_ref[c, at:at + size, :]
            field_ref[k, c, (HALO + rows) * members:(HALO + rows + count) * members, :] = below_ref[c, at:at + size, :]
            at += size
            for m in range(members):
                field_ref[k, c, pl.ds(HALO * members + m, rows, stride=members), :] = state_ref[m, k, :, lanes]
        pull_above = COURANT * above_ref[c, at:at + HALO - 1, :]
        pull_here = COURANT * depth_ref[:, lanes]
        pull_below = COURANT * below_ref[c, at:at + HALO - 1, :]
        for m in range(members):
            pull_ref[c, pl.ds(members + m, HALO - 1, stride=members), :] = pull_above
            pull_ref[c, pl.ds(HALO * members + m, rows, stride=members), :] = pull_here
            pull_ref[c, pl.ds((HALO + rows) * members + m, HALO - 1, stride=members), :] = pull_below

    def cols_diff(parts):
        left = [pltpu.roll(p, 1, 1) for p in parts]
        right = [pltpu.roll(p, LANES - 1, 1) for p in parts]
        return [
            jnp.where(lane == LANES - 1, right[(c + 1) % chunks], right[c]) - jnp.where(lane == 0, left[c - 1], left[c])
            for c in range(chunks)
        ]

    def take(k, first, count):
        return [field_ref[k, c, first * members:(first + count) * members, :] for c in range(chunks)]

    def push_of(first, count):
        if first >= HALO and first + count <= HALO + rows:
            return COURANT
        row = lax.broadcasted_iota(jnp.int32, (count * members, LANES), 0) + (first + band * rows - HALO) * members
        return jnp.where(jnp.logical_and(row >= 0, row < bands * rows * members), COURANT, 0.0)

    def blocks(first, last):
        cuts = sorted({HALO, HALO + rows} | set(range(HALO, HALO + rows, ROW_BLOCK)))
        ends = [first] + [e for e in cuts if first < e < last] + [last]
        return [(lo, hi - lo) for lo, hi in zip(ends[:-1], ends[1:])]

    for step in range(STEPS):
        reach = 2 * (STEPS - 1 - step)
        for first, count in blocks(HALO - reach - 1, HALO + rows + reach + 1):
            height = take(0, first, count)
            slope = cols_diff(take(1, first, count))
            north = take(2, first + 1, count)
            south = take(2, first - 1, count)
            span = slice(first * members, (first + count) * members)
            for c in range(chunks):
                field_ref[0, c, span, :] = height[c] - pull_ref[c, span, :] * (slope[c] + (north[c] - south[c]))
        for first, count in blocks(HALO - reach, HALO + rows + reach):
            slope = cols_diff(take(0, first, count))
            zonal = take(1, first, count)
            meridional = take(2, first, count)
            north = take(0, first + 1, count)
            south = take(0, first - 1, count)
            push = push_of(first, count)
            span = slice(first * members, (first + count) * members)
            for c in range(chunks):
                zonal[c] = zonal[c] - COURANT * slope[c]
                meridional[c] = meridional[c] - push * (north[c] - south[c])
                if step < STEPS - 1:
                    field_ref[1, c, span, :] = zonal[c]
                    field_ref[2, c, span, :] = meridional[c]
            if step == STEPS - 1:
                here = take(0, first, count)
                for k, parts in enumerate((here, zonal, meridional)):
                    for c in range(chunks):
                        for t in range(count):
                            out_ref[first - HALO + t, :, k * cols + c * LANES:k * cols + (c + 1) * LANES] = parts[c][t * members:(t + 1) * members]


def forecast(state, above, below, depth, bands):
    members, fields, rows, cols = state.shape
    total = rows + 2 * HALO
    return pl.pallas_call(
        functools.partial(forecast_kernel, bands),
        out_shape=jax.ShapeDtypeStruct((rows, members, fields * cols), jnp.float32),
        scratch_shapes=[
            pltpu.VMEM((fields, cols // LANES, total * members, LANES), jnp.float32),
            pltpu.VMEM((cols // LANES, total * members, LANES), jnp.float32),
        ],
        compiler_params=pltpu.CompilerParams(vmem_limit_bytes=VMEM),
        cost_estimate=cost(STEPS * 12 * state.size, 8 * state.size),
        name="forecast",
    )(state, above, below, depth)


def spots(count, block):
    i = lax.broadcasted_iota(jnp.int32, (count, count), 0)
    j = lax.broadcasted_iota(jnp.int32, (count, count), 1)
    return j == (i - i % block) + (i + 1) % block


def gram_kernel(block, cols, state_ref, cell_ref, value_ref, var_ref, keep_ref, send_ref, whole_ref):
    count = state_ref.shape[0]
    number = cell_ref.shape[1]
    picks = lax.broadcasted_iota(jnp.int32, (cols, number), 0) == cell_ref[...]
    seen = dot(state_ref[:, :cols], jnp.where(picks, 1.0, 0.0))
    centre = jnp.sum(seen, axis=0, keepdims=True) / count
    observed = seen - centre
    innovation = value_ref[...] - centre
    weighted = observed / var_ref[...]
    gram = dot(weighted, observed, ((1,), (1,)))
    projection = jnp.sum(weighted * innovation, axis=1, keepdims=True)
    whole_ref[...] = jnp.where(spots(count, block), projection, gram)
    half, pieces = count // 2, count // LANES
    core = lax.axis_index("member") % 2
    for out_ref, other in ((keep_ref, core), (send_ref, 1 - core)):
        part = whole_ref[pl.ds(pl.multiple_of(other * half, half), half), :]
        for c in range(pieces):
            out_ref[pl.ds(c, half, stride=pieces), :] = part[:, c * LANES:(c + 1) * LANES]


def gram_of(spread_state, cell, value, var, block, cols):
    count = spread_state.shape[0]
    return pl.pallas_call(
        functools.partial(gram_kernel, block, cols),
        out_shape=[jax.ShapeDtypeStruct((count // 2 * count // LANES, LANES), jnp.float32)] * 2,
        scratch_shapes=[pltpu.VMEM((count, count), jnp.float32)],
        compiler_params=pltpu.CompilerParams(vmem_limit_bytes=VMEM),
        cost_estimate=cost(6 * 2 * count * cols * cell.shape[1], 4 * count * cols),
        name="gram",
    )(spread_state, cell, value, var)


def transform_kernel(block, keep_ref, got_ref, weights_ref, packed_ref):
    count = packed_ref.shape[0]
    half, pieces = count // 2, count // LANES
    core = lax.axis_index("member") % 2
    for in_ref, other in ((keep_ref, core), (got_ref, 1 - core)):
        for c in range(pieces):
            rows = pl.ds(pl.multiple_of(other * half, half), half)
            packed_ref[rows, c * LANES:(c + 1) * LANES] = in_ref[pl.ds(c, half, stride=pieces), :]
    packed = packed_ref[...]
    places = spots(count, block)
    projection = jnp.sum(jnp.where(places, packed, 0.0), axis=1, keepdims=True)
    gram = jnp.where(places, packed.T, packed)
    i = lax.broadcasted_iota(jnp.int32, (count, count), 0)
    j = lax.broadcasted_iota(jnp.int32, (count, count), 1)
    identity = jnp.where(i == j, 1.0, 0.0)
    system = identity + gram / (count - 1)
    scale = jnp.sqrt(jnp.sum(jnp.sum(system * system, axis=1, keepdims=True), axis=0, keepdims=True))
    current = system / scale
    root_inv = identity
    for step in range(NS_ITERS):
        parts, inv_parts = halves(current), halves(root_inv)
        product = current if step == 0 else dot3(inv_parts, parts)
        factor = 1.5 * identity - 0.5 * product
        factor_parts = halves(factor)
        if step < NS_ITERS - 1:
            current = dot3(parts, factor_parts)
        root_inv = factor if step == 0 else dot3(factor_parts, inv_parts)
    root = root_inv / jnp.sqrt(scale)

    def times(column):
        return jnp.sum(root * jnp.sum(jnp.where(i == j, column, 0.0), axis=0, keepdims=True), axis=1, keepdims=True)

    weights_ref[...] = times(times(projection)) / (count - 1) + root


def transform(keep, got, block, count):
    return pl.pallas_call(
        functools.partial(transform_kernel, block),
        out_shape=jax.ShapeDtypeStruct((count, count), jnp.float32),
        scratch_shapes=[pltpu.VMEM((count, count), jnp.float32)],
        compiler_params=pltpu.CompilerParams(vmem_limit_bytes=VMEM),
        cost_estimate=cost(6 * 2 * 14 * count ** 3, 8 * count ** 2),
        name="transform",
    )(keep, got)


def mix_kernel(weights_ref, state_ref, out_ref):
    weights = halves(weights_ref[...])
    count, width = state_ref.shape
    for first in range(0, width, MIX_BLOCK):
        values = state_ref[:, first:first + MIX_BLOCK]
        centre = jnp.sum(values, axis=0, keepdims=True) / count
        out_ref[:, first:first + MIX_BLOCK] = centre + dot3(weights, halves(values - centre), ((0,), (0,)))


def mix(weights, spread_state):
    count, width = spread_state.shape
    return pl.pallas_call(
        mix_kernel,
        out_shape=jax.ShapeDtypeStruct((count, width), jnp.float32),
        compiler_params=pltpu.CompilerParams(vmem_limit_bytes=VMEM),
        cost_estimate=cost(6 * 2 * count * count * width, 8 * count * width),
        name="mix",
    )(weights, spread_state)


def unfold_kernel(rows_ref, out_ref, lanes_ref):
    members, fields, rows, cols = out_ref.shape
    for c in range(fields * cols // LANES):
        lanes_ref[c] = rows_ref[:, c * LANES:(c + 1) * LANES]
    for m in range(members):
        for k in range(fields):
            for c in range(cols // LANES):
                out_ref[m, k, :, c * LANES:(c + 1) * LANES] = lanes_ref[k * (cols // LANES) + c, pl.ds(m, rows, stride=members), :]


def unfold(rows, shape):
    return pl.pallas_call(
        unfold_kernel,
        out_shape=jax.ShapeDtypeStruct(shape, jnp.float32),
        scratch_shapes=[pltpu.VMEM((rows.shape[1] // LANES, rows.shape[0], LANES), jnp.float32)],
        compiler_params=pltpu.CompilerParams(vmem_limit_bytes=VMEM),
        cost_estimate=cost(0, 8 * rows.size),
        name="unfold",
    )(rows)


def exchange(blocks, axis, groups=None):
    return lax.all_to_all(blocks, axis, split_axis=0, concat_axis=0, tiled=True, axis_index_groups=groups)


def spread(block, axis, count, groups=None):
    return exchange(jnp.broadcast_to(block, (count,) + block.shape), axis, groups)


def shards(state, depth, obs_cell, obs_value, obs_var):
    bands, tiles = lax.axis_size("space"), lax.axis_size("member")
    members, rows, fields, cols = state.shape
    ensemble, chips = tiles * members, tiles // 2
    sibling = [(i, i ^ 1) for i in range(tiles)]

    state = state.transpose(0, 2, 1, 3)
    up = [(i, i + 1) for i in range(bands - 1)]
    down = [(i + 1, i) for i in range(bands - 1)]

    to_below, to_above = edges(state, depth)
    above = lax.ppermute(to_above, "space", up)
    below = lax.ppermute(to_below, "space", down)
    ahead = forecast(state, above, below, depth, bands)
    ahead = exchange(ahead, "member").reshape(ensemble, fields * cols)

    keep, send = gram_of(ahead, obs_cell[0], obs_value[0], obs_var[0], members, cols)
    half = keep + lax.ppermute(send, "member", sibling)
    every = ("member", "space")
    same_core = [
        [(2 * q + core) * bands + band for q in range(chips) for band in range(bands)] for core in range(2)
    ]
    row = jnp.sum(exchange(half.reshape(ensemble // 2, -1, LANES), every, same_core), axis=0)
    half = spread(row, every, chips * bands, same_core).reshape(half.shape)
    weights = transform(half, lax.ppermute(half, "member", sibling), members, ensemble)

    analysed = mix(weights, ahead)
    back = exchange(analysed.reshape(tiles, members, fields * cols), "member").reshape(ensemble, fields * cols)
    return unfold(back, (members, fields, rows, cols)).transpose(0, 2, 1, 3)


def solution(mesh):
    placed = (
        P("member", "space", None, None),
        P("space", None),
        P("space", "member", None),
        P("space", "member", None),
        P("space", "member", None),
    )
    return jax.shard_map(
        shards,
        mesh=mesh,
        in_specs=placed,
        out_specs=P("member", "space", None, None),
        check_vma=False,
    )
```

```python
import functools

import jax
import jax.numpy as jnp
from jax import lax
from jax.experimental import pallas as pl
from jax.experimental.pallas import tpu as pltpu
from jax.sharding import PartitionSpec as P

STEPS = 3
NS_ITERS = 5
COURANT = 0.3
HALO = 2 * STEPS
LANES = 128
ROW_BLOCK = 4
VMEM = 40 * 1024 * 1024
ALL_VMEM = 60 * 1024 * 1024
HIGHEST = lax.Precision.HIGHEST


def dot(a, b, dims=((1,), (0,))):
    return lax.dot_general(a, b, (dims, ((), ())), precision=HIGHEST, preferred_element_type=jnp.float32)


def halves(a):
    high = a.astype(jnp.bfloat16)
    return high, (a - high.astype(jnp.float32)).astype(jnp.bfloat16)


def dot3(a, b, dims=((1,), (0,))):
    def one(x, y):
        return lax.dot_general(x, y, (dims, ((), ())), preferred_element_type=jnp.float32)

    (a_high, a_low), (b_high, b_low) = a, b
    return one(a_high, b_high) + (one(a_high, b_low) + one(a_low, b_high))


def cost(flops, bytes_accessed):
    return pl.CostEstimate(flops=flops, bytes_accessed=bytes_accessed, transcendentals=0)


def edges_kernel(state_ref, depth_ref, down_ref, up_ref, top_ref, bottom_ref, depth_top_ref, depth_bottom_ref, sems):
    members, fields, block, cols = top_ref.shape
    rows = depth_ref.shape[0]
    sides = (
        (up_ref, bottom_ref, depth_bottom_ref, rows - block, True),
        (down_ref, top_ref, depth_top_ref, 0, False),
    )
    copies = []
    for side, (_, field_ref, edge_ref, start, _) in enumerate(sides):
        copies.append([
            pltpu.make_async_copy(state_ref.at[m, :, pl.ds(start, block), :], field_ref.at[m], sems.at[side, m])
            for m in range(members)
        ] + [pltpu.make_async_copy(depth_ref.at[pl.ds(start, block), :], edge_ref, sems.at[side, members])])
        for copy in copies[-1]:
            copy.start()
    for (out_ref, field_ref, edge_ref, _, last), waits in zip(sides, copies):
        for copy in waits:
            copy.wait()
        for c in range(cols // LANES):
            lanes = slice(c * LANES, (c + 1) * LANES)
            at = 0
            for k in range(fields):
                count = HALO if k == 2 else HALO - 1
                first = block - count if last else 0
                for m in range(members):
                    out_ref[c, pl.ds(at + m, count, stride=members), :] = field_ref[m, k, first:first + count, lanes]
                at += count * members
            first = block - HALO + 1 if last else 0
            out_ref[c, at:at + HALO - 1, :] = edge_ref[first:first + HALO - 1, lanes]


def edges(state, depth):
    members, fields, rows, cols = state.shape
    block = 8
    shape = jax.ShapeDtypeStruct((cols // LANES, (3 * HALO - 2) * members + 8, LANES), jnp.float32)
    return pl.pallas_call(
        edges_kernel,
        in_specs=[pl.BlockSpec(memory_space=pl.ANY)] * 2,
        out_shape=[shape] * 2,
        scratch_shapes=[
            pltpu.VMEM((members, fields, block, cols), jnp.float32),
            pltpu.VMEM((members, fields, block, cols), jnp.float32),
            pltpu.VMEM((block, cols), jnp.float32),
            pltpu.VMEM((block, cols), jnp.float32),
            pltpu.SemaphoreType.DMA((2, members + 1)),
        ],
        compiler_params=pltpu.CompilerParams(vmem_limit_bytes=ALL_VMEM),
        cost_estimate=cost(0, 2 * state.size),
        name="edges",
    )(state, depth)


def forecast_kernel(bands, state_ref, above_ref, below_ref, depth_ref, height_ref, wind_ref, field_ref, pull_ref):
    members, fields, rows, cols = state_ref.shape
    chunks = cols // LANES
    band = lax.axis_index("space")
    lane = lax.broadcasted_iota(jnp.int32, (1, LANES), 1)

    for c in range(chunks):
        lanes = slice(c * LANES, (c + 1) * LANES)
        at = 0
        for k in range(fields):
            count = HALO if k == 2 else HALO - 1
            size = count * members
            field_ref[k, c, (HALO - count) * members:HALO * members, :] = above_ref[c, at:at + size, :]
            field_ref[k, c, (HALO + rows) * members:(HALO + rows + count) * members, :] = below_ref[c, at:at + size, :]
            at += size
            for m in range(members):
                field_ref[k, c, pl.ds(HALO * members + m, rows, stride=members), :] = state_ref[m, k, :, lanes]
        pull_above = COURANT * above_ref[c, at:at + HALO - 1, :]
        pull_here = COURANT * depth_ref[:, lanes]
        pull_below = COURANT * below_ref[c, at:at + HALO - 1, :]
        for m in range(members):
            pull_ref[c, pl.ds(members + m, HALO - 1, stride=members), :] = pull_above
            pull_ref[c, pl.ds(HALO * members + m, rows, stride=members), :] = pull_here
            pull_ref[c, pl.ds((HALO + rows) * members + m, HALO - 1, stride=members), :] = pull_below

    def cols_diff(parts):
        left = [pltpu.roll(p, 1, 1) for p in parts]
        right = [pltpu.roll(p, LANES - 1, 1) for p in parts]
        return [
            jnp.where(lane == LANES - 1, right[(c + 1) % chunks], right[c]) - jnp.where(lane == 0, left[c - 1], left[c])
            for c in range(chunks)
        ]

    def take(k, first, count):
        return [field_ref[k, c, first * members:(first + count) * members, :] for c in range(chunks)]

    def push_of(first, count):
        if first >= HALO and first + count <= HALO + rows:
            return COURANT
        row = lax.broadcasted_iota(jnp.int32, (count * members, LANES), 0) + (first + band * rows - HALO) * members
        return jnp.where(jnp.logical_and(row >= 0, row < bands * rows * members), COURANT, 0.0)

    def blocks(first, last):
        cuts = sorted({HALO, HALO + rows} | set(range(HALO, HALO + rows, ROW_BLOCK)))
        ends = [first] + [e for e in cuts if first < e < last] + [last]
        return [(lo, hi - lo) for lo, hi in zip(ends[:-1], ends[1:])]

    for step in range(STEPS):
        reach = 2 * (STEPS - 1 - step)
        for first, count in blocks(HALO - reach - 1, HALO + rows + reach + 1):
            height = take(0, first, count)
            slope = cols_diff(take(1, first, count))
            north = take(2, first + 1, count)
            south = take(2, first - 1, count)
            span = slice(first * members, (first + count) * members)
            for c in range(chunks):
                field_ref[0, c, span, :] = height[c] - pull_ref[c, span, :] * (slope[c] + (north[c] - south[c]))
        for first, count in blocks(HALO - reach, HALO + rows + reach):
            slope = cols_diff(take(0, first, count))
            zonal = take(1, first, count)
            meridional = take(2, first, count)
            north = take(0, first + 1, count)
            south = take(0, first - 1, count)
            push = push_of(first, count)
            span = slice(first * members, (first + count) * members)
            for c in range(chunks):
                zonal[c] = zonal[c] - COURANT * slope[c]
                meridional[c] = meridional[c] - push * (north[c] - south[c])
                if step < STEPS - 1:
                    field_ref[1, c, span, :] = zonal[c]
                    field_ref[2, c, span, :] = meridional[c]
            if step == STEPS - 1:
                here = take(0, first, count)
                for k, parts in enumerate((here, zonal, meridional)):
                    for c in range(chunks):
                        for t in range(count):
                            out_ref, start = (height_ref, 0) if k == 0 else (wind_ref, (k - 1) * cols)
                            lanes = slice(start + c * LANES, start + (c + 1) * LANES)
                            out_ref[first - HALO + t, :, lanes] = parts[c][t * members:(t + 1) * members]


def forecast(state, above, below, depth, bands):
    members, fields, rows, cols = state.shape
    total = rows + 2 * HALO
    return pl.pallas_call(
        functools.partial(forecast_kernel, bands),
        out_shape=[
            jax.ShapeDtypeStruct((rows, members, cols), jnp.float32),
            jax.ShapeDtypeStruct((rows, members, 2 * cols), jnp.float32),
        ],
        scratch_shapes=[
            pltpu.VMEM((fields, cols // LANES, total * members, LANES), jnp.float32),
            pltpu.VMEM((cols // LANES, total * members, LANES), jnp.float32),
        ],
        compiler_params=pltpu.CompilerParams(vmem_limit_bytes=VMEM),
        cost_estimate=cost(STEPS * 12 * state.size, 8 * state.size),
        name="forecast",
    )(state, above, below, depth)


def spots(count, block):
    i = lax.broadcasted_iota(jnp.int32, (count, count), 0)
    j = lax.broadcasted_iota(jnp.int32, (count, count), 1)
    return j == (i - i % block) + (i + 1) % block


def gram_kernel(block, height_ref, cell_ref, value_ref, var_ref, keep_ref, send_ref, whole_ref):
    count, cols = height_ref.shape
    number = cell_ref.shape[1]
    picks = lax.broadcasted_iota(jnp.int32, (cols, number), 0) == cell_ref[...]
    seen = dot(height_ref[...], jnp.where(picks, 1.0, 0.0))
    centre = jnp.sum(seen, axis=0, keepdims=True) / count
    observed = seen - centre
    innovation = value_ref[...] - centre
    weighted = observed / var_ref[...]
    gram = dot(weighted, observed, ((1,), (1,)))
    projection = jnp.sum(weighted * innovation, axis=1, keepdims=True)
    whole_ref[...] = jnp.where(spots(count, block), projection, gram)
    half = count // 2
    core = lax.axis_index("member") % 2
    keep_ref[...] = whole_ref[pl.ds(pl.multiple_of(core * half, half), half), :]
    send_ref[...] = whole_ref[pl.ds(pl.multiple_of((1 - core) * half, half), half), :]


def gram_of(height, cell, value, var, block):
    count, cols = height.shape
    return pl.pallas_call(
        functools.partial(gram_kernel, block),
        out_shape=[jax.ShapeDtypeStruct((count // 2, count), jnp.float32)] * 2,
        scratch_shapes=[pltpu.VMEM((count, count), jnp.float32)],
        compiler_params=pltpu.CompilerParams(vmem_limit_bytes=VMEM),
        cost_estimate=cost(6 * 2 * count * cols * cell.shape[1], 4 * count * cols),
        name="gram",
    )(height, cell, value, var)


def transform_kernel(block, keep_ref, got_ref, weights_ref, packed_ref):
    half, count = keep_ref.shape
    core = lax.axis_index("member") % 2
    packed_ref[pl.ds(pl.multiple_of(core * half, half), half), :] = keep_ref[...]
    packed_ref[pl.ds(pl.multiple_of((1 - core) * half, half), half), :] = got_ref[...]
    packed = packed_ref[...]
    places = spots(count, block)
    projection = jnp.sum(jnp.where(places, packed, 0.0), axis=1, keepdims=True)
    gram = jnp.where(places, packed.T, packed)
    i = lax.broadcasted_iota(jnp.int32, (count, count), 0)
    j = lax.broadcasted_iota(jnp.int32, (count, count), 1)
    identity = jnp.where(i == j, 1.0, 0.0)
    system = identity + gram / (count - 1)
    scale = jnp.sqrt(jnp.sum(jnp.sum(system * system, axis=1, keepdims=True), axis=0, keepdims=True))
    current = system / scale
    root_inv = identity
    for step in range(NS_ITERS):
        parts, inv_parts = halves(current), halves(root_inv)
        product = current if step == 0 else dot3(inv_parts, parts)
        factor = 1.5 * identity - 0.5 * product
        factor_parts = halves(factor)
        if step < NS_ITERS - 1:
            current = dot3(parts, factor_parts)
        root_inv = factor if step == 0 else dot3(factor_parts, inv_parts)
    root = root_inv / jnp.sqrt(scale)

    def times(column):
        return jnp.sum(root * jnp.sum(jnp.where(i == j, column, 0.0), axis=0, keepdims=True), axis=1, keepdims=True)

    weights_ref[...] = times(times(projection)) / (count - 1) + root


def transform(keep, got, block):
    count = keep.shape[1]
    return pl.pallas_call(
        functools.partial(transform_kernel, block),
        out_shape=jax.ShapeDtypeStruct((count, count), jnp.float32),
        scratch_shapes=[pltpu.VMEM((count, count), jnp.float32)],
        compiler_params=pltpu.CompilerParams(vmem_limit_bytes=VMEM),
        cost_estimate=cost(6 * 2 * 14 * count ** 3, 8 * count ** 2),
        name="transform",
    )(keep, got)


def mix_kernel(weights_ref, height_ref, wind_ref, out_ref):
    weights = halves(weights_ref[...])
    count, cols = height_ref.shape
    for first in range(0, 3 * cols, cols):
        values = height_ref[...] if first == 0 else wind_ref[:, first - cols:first]
        centre = jnp.sum(values, axis=0, keepdims=True) / count
        out_ref[:, first:first + cols] = centre + dot3(weights, halves(values - centre), ((0,), (0,)))


def mix(weights, height, wind):
    count, cols = height.shape
    return pl.pallas_call(
        mix_kernel,
        out_shape=jax.ShapeDtypeStruct((count, 3 * cols), jnp.float32),
        compiler_params=pltpu.CompilerParams(vmem_limit_bytes=VMEM),
        cost_estimate=cost(3 * 2 * count * count * 3 * cols, 4 * count * 6 * cols),
        name="mix",
    )(weights, height, wind)


def unfold_kernel(rows_ref, out_ref, lanes_ref):
    members, fields, rows, cols = out_ref.shape
    for c in range(fields * cols // LANES):
        lanes_ref[c] = rows_ref[:, c * LANES:(c + 1) * LANES]
    for m in range(members):
        for k in range(fields):
            for c in range(cols // LANES):
                out_ref[m, k, :, c * LANES:(c + 1) * LANES] = lanes_ref[k * (cols // LANES) + c, pl.ds(m, rows, stride=members), :]


def unfold(rows, shape):
    return pl.pallas_call(
        unfold_kernel,
        out_shape=jax.ShapeDtypeStruct(shape, jnp.float32),
        scratch_shapes=[pltpu.VMEM((rows.shape[1] // LANES, rows.shape[0], LANES), jnp.float32)],
        compiler_params=pltpu.CompilerParams(vmem_limit_bytes=VMEM),
        cost_estimate=cost(0, 8 * rows.size),
        name="unfold",
    )(rows)


def exchange(blocks, axis, groups=None):
    return lax.all_to_all(blocks, axis, split_axis=0, concat_axis=0, tiled=True, axis_index_groups=groups)


def spread(block, axis, count, groups=None):
    return exchange(jnp.broadcast_to(block, (count,) + block.shape), axis, groups)


def shards(state, depth, obs_cell, obs_value, obs_var):
    bands, tiles = lax.axis_size("space"), lax.axis_size("member")
    members, rows, fields, cols = state.shape
    ensemble, chips = tiles * members, tiles // 2
    sibling = [(i, i ^ 1) for i in range(tiles)]
    same_core = [[2 * q + core for q in range(chips)] for core in range(2)]


    state = state.transpose(0, 2, 1, 3)
    up = [(i, i + 1) for i in range(bands - 1)]
    down = [(i + 1, i) for i in range(bands - 1)]

    to_below, to_above = edges(state, depth)
    above = lax.ppermute(to_above, "space", up)
    below = lax.ppermute(to_below, "space", down)
    height, wind = forecast(state, above, below, depth, bands)
    height = exchange(height, "member").reshape(ensemble, cols)
    height, wind = lax.optimization_barrier((height, wind))
    wind = exchange(wind, "member").reshape(ensemble, 2 * cols)

    keep, send = gram_of(height, obs_cell[0], obs_value[0], obs_var[0], members)
    half = keep + lax.ppermute(send, "member", sibling)

    def across(value, k):
        return lax.ppermute(value, "space", [(i, i ^ k) for i in range(bands)])

    half = (half + across(half, 1)) + (across(half, 2) + across(half, 3))
    half = half + across(half, 4)
    half, wind = lax.optimization_barrier((half, wind))
    part = jnp.sum(exchange(half.reshape(chips, -1, ensemble), "member", same_core), axis=0)
    half = spread(part, "member", chips, same_core).reshape(half.shape)
    weights = transform(half, lax.ppermute(half, "member", sibling), members)

    analysed = mix(weights, height, wind)
    back = exchange(analysed.reshape(tiles, members, fields * cols), "member").reshape(ensemble, fields * cols)
    return unfold(back, (members, fields, rows, cols)).transpose(0, 2, 1, 3)


def solution(mesh):
    placed = (
        P("member", "space", None, None),
        P("space", None),
        P("space", "member", None),
        P("space", "member", None),
        P("space", "member", None),
    )
    return jax.shard_map(
        shards,
        mesh=mesh,
        in_specs=placed,
        out_specs=P("member", "space", None, None),
        check_vma=False,
    )
```

```python
import functools

import jax
import jax.numpy as jnp
from jax import lax
from jax.experimental import pallas as pl
from jax.experimental.pallas import tpu as pltpu
from jax.sharding import PartitionSpec as P

STEPS = 3
NS_ITERS = 5
COURANT = 0.3
HALO = 2 * STEPS
LANES = 128
ROW_BLOCK = 4
MIX_BLOCK = 512
VMEM = 40 * 1024 * 1024
ALL_VMEM = 60 * 1024 * 1024
HIGHEST = lax.Precision.HIGHEST


def dot(a, b, dims=((1,), (0,))):
    return lax.dot_general(a, b, (dims, ((), ())), precision=HIGHEST, preferred_element_type=jnp.float32)


def halves(a):
    high = a.astype(jnp.bfloat16)
    return high, (a - high.astype(jnp.float32)).astype(jnp.bfloat16)


def dot3(a, b, dims=((1,), (0,))):
    def one(x, y):
        return lax.dot_general(x, y, (dims, ((), ())), preferred_element_type=jnp.float32)

    (a_high, a_low), (b_high, b_low) = a, b
    return one(a_high, b_high) + (one(a_high, b_low) + one(a_low, b_high))


def picked(a, picks):
    high, low = halves(a)
    rest = (a - high.astype(jnp.float32) - low.astype(jnp.float32)).astype(jnp.bfloat16)
    parts = [jnp.dot(x, picks, preferred_element_type=jnp.float32) for x in (high, low, rest)]
    return parts[0] + (parts[1] + parts[2])


def cost(flops, bytes_accessed):
    return pl.CostEstimate(flops=flops, bytes_accessed=bytes_accessed, transcendentals=0)


def edges_kernel(state_ref, depth_ref, first_ref, second_ref, top_ref, bottom_ref, depth_top_ref, depth_bottom_ref, sems):
    members, fields, block, cols = top_ref.shape
    rows = depth_ref.shape[0]
    even = lax.axis_index("space") % 2 == 0
    sides = (
        (bottom_ref, depth_bottom_ref, rows - block, True),
        (top_ref, depth_top_ref, 0, False),
    )
    copies = []
    for side, (field_ref, edge_ref, start, _) in enumerate(sides):
        copies.append([
            pltpu.make_async_copy(state_ref.at[m, :, pl.ds(start, block), :], field_ref.at[m], sems.at[side, m])
            for m in range(members)
        ] + [pltpu.make_async_copy(depth_ref.at[pl.ds(start, block), :], edge_ref, sems.at[side, members])])
        for copy in copies[-1]:
            copy.start()

    def write(out_ref, field_ref, edge_ref, last):
        for c in range(cols // LANES):
            lanes = slice(c * LANES, (c + 1) * LANES)
            at = 0
            for k in range(fields):
                count = HALO if k == 2 else HALO - 1
                first = block - count if last else 0
                for m in range(members):
                    out_ref[c, pl.ds(at + m, count, stride=members), :] = field_ref[m, k, first:first + count, lanes]
                at += count * members
            first = block - HALO + 1 if last else 0
            out_ref[c, at:at + HALO - 1, :] = edge_ref[first:first + HALO - 1, lanes]

    for (field_ref, edge_ref, _, last), waits in zip(sides, copies):
        for copy in waits:
            copy.wait()
        for out_ref, here in ((first_ref, even), (second_ref, jnp.logical_not(even))):
            @pl.when(here if last else jnp.logical_not(here))
            def _():
                write(out_ref, field_ref, edge_ref, last)


def edges(state, depth):
    members, fields, rows, cols = state.shape
    block = 8
    shape = jax.ShapeDtypeStruct((cols // LANES, (3 * HALO - 2) * members + 8, LANES), jnp.float32)
    return pl.pallas_call(
        edges_kernel,
        in_specs=[pl.BlockSpec(memory_space=pl.ANY)] * 2,
        out_shape=[shape] * 2,
        scratch_shapes=[
            pltpu.VMEM((members, fields, block, cols), jnp.float32),
            pltpu.VMEM((members, fields, block, cols), jnp.float32),
            pltpu.VMEM((block, cols), jnp.float32),
            pltpu.VMEM((block, cols), jnp.float32),
            pltpu.SemaphoreType.DMA((2, members + 1)),
        ],
        compiler_params=pltpu.CompilerParams(vmem_limit_bytes=ALL_VMEM),
        cost_estimate=cost(0, 2 * state.size),
        name="edges",
    )(state, depth)


def forecast_kernel(bands, state_ref, first_ref, second_ref, depth_ref, out_ref, field_ref, pull_ref):
    members, fields, rows, cols = state_ref.shape
    chunks = cols // LANES
    band = lax.axis_index("space")
    lane = lax.broadcasted_iota(jnp.int32, (1, LANES), 1)

    even = band % 2 == 0

    def above(c, first, last):
        return jnp.where(even, second_ref[c, first:last, :], first_ref[c, first:last, :])

    def below(c, first, last):
        return jnp.where(even, first_ref[c, first:last, :], second_ref[c, first:last, :])

    for c in range(chunks):
        lanes = slice(c * LANES, (c + 1) * LANES)
        at = 0
        for k in range(fields):
            count = HALO if k == 2 else HALO - 1
            size = count * members
            field_ref[k, c, (HALO - count) * members:HALO * members, :] = above(c, at, at + size)
            field_ref[k, c, (HALO + rows) * members:(HALO + rows + count) * members, :] = below(c, at, at + size)
            at += size
            for m in range(members):
                field_ref[k, c, pl.ds(HALO * members + m, rows, stride=members), :] = state_ref[m, k, :, lanes]
        pull_above = COURANT * above(c, at, at + HALO - 1)
        pull_here = COURANT * depth_ref[:, lanes]
        pull_below = COURANT * below(c, at, at + HALO - 1)
        for m in range(members):
            pull_ref[c, pl.ds(members + m, HALO - 1, stride=members), :] = pull_above
            pull_ref[c, pl.ds(HALO * members + m, rows, stride=members), :] = pull_here
            pull_ref[c, pl.ds((HALO + rows) * members + m, HALO - 1, stride=members), :] = pull_below

    def cols_diff(parts):
        left = [pltpu.roll(p, 1, 1) for p in parts]
        right = [pltpu.roll(p, LANES - 1, 1) for p in parts]
        return [
            jnp.where(lane == LANES - 1, right[(c + 1) % chunks], right[c]) - jnp.where(lane == 0, left[c - 1], left[c])
            for c in range(chunks)
        ]

    def take(k, first, count):
        return [field_ref[k, c, first * members:(first + count) * members, :] for c in range(chunks)]

    def push_of(first, count):
        if first >= HALO and first + count <= HALO + rows:
            return COURANT
        row = lax.broadcasted_iota(jnp.int32, (count * members, LANES), 0) + (first + band * rows - HALO) * members
        return jnp.where(jnp.logical_and(row >= 0, row < bands * rows * members), COURANT, 0.0)

    def blocks(first, last):
        cuts = sorted({HALO, HALO + rows} | set(range(HALO, HALO + rows, ROW_BLOCK)))
        ends = [first] + [e for e in cuts if first < e < last] + [last]
        return [(lo, hi - lo) for lo, hi in zip(ends[:-1], ends[1:])]

    for step in range(STEPS):
        reach = 2 * (STEPS - 1 - step)
        for first, count in blocks(HALO - reach - 1, HALO + rows + reach + 1):
            height = take(0, first, count)
            slope = cols_diff(take(1, first, count))
            north = take(2, first + 1, count)
            south = take(2, first - 1, count)
            span = slice(first * members, (first + count) * members)
            for c in range(chunks):
                field_ref[0, c, span, :] = height[c] - pull_ref[c, span, :] * (slope[c] + (north[c] - south[c]))
        for first, count in blocks(HALO - reach, HALO + rows + reach):
            slope = cols_diff(take(0, first, count))
            zonal = take(1, first, count)
            meridional = take(2, first, count)
            north = take(0, first + 1, count)
            south = take(0, first - 1, count)
            push = push_of(first, count)
            span = slice(first * members, (first + count) * members)
            for c in range(chunks):
                zonal[c] = zonal[c] - COURANT * slope[c]
                meridional[c] = meridional[c] - push * (north[c] - south[c])
                if step < STEPS - 1:
                    field_ref[1, c, span, :] = zonal[c]
                    field_ref[2, c, span, :] = meridional[c]
            if step == STEPS - 1:
                here = take(0, first, count)
                for k, parts in enumerate((here, zonal, meridional)):
                    for c in range(chunks):
                        for t in range(count):
                            out_ref[first - HALO + t, :, k * cols + c * LANES:k * cols + (c + 1) * LANES] = parts[c][t * members:(t + 1) * members]


def forecast(state, first, second, depth, bands):
    members, fields, rows, cols = state.shape
    total = rows + 2 * HALO
    return pl.pallas_call(
        functools.partial(forecast_kernel, bands),
        out_shape=jax.ShapeDtypeStruct((rows, members, fields * cols), jnp.float32),
        scratch_shapes=[
            pltpu.VMEM((fields, cols // LANES, total * members, LANES), jnp.float32),
            pltpu.VMEM((cols // LANES, total * members, LANES), jnp.float32),
        ],
        compiler_params=pltpu.CompilerParams(vmem_limit_bytes=VMEM),
        cost_estimate=cost(STEPS * 12 * state.size, 8 * state.size),
        name="forecast",
    )(state, first, second, depth)


def spots(count, block):
    i = lax.broadcasted_iota(jnp.int32, (count, count), 0)
    j = lax.broadcasted_iota(jnp.int32, (count, count), 1)
    return j == (i - i % block) + (i + 1) % block


def gram_kernel(block, cols, state_ref, cell_ref, value_ref, var_ref, keep_ref, send_ref, whole_ref):
    count = state_ref.shape[0]
    number = cell_ref.shape[1]
    picks = lax.broadcasted_iota(jnp.int32, (cols, number), 0) == cell_ref[...]
    seen = picked(state_ref[:, :cols], jnp.where(picks, 1.0, 0.0).astype(jnp.bfloat16))
    centre = jnp.sum(seen, axis=0, keepdims=True) / count
    observed = seen - centre
    innovation = value_ref[...] - centre
    weighted = observed / var_ref[...]
    gram = dot(weighted, observed, ((1,), (1,)))
    projection = jnp.sum(weighted * innovation, axis=1, keepdims=True)
    whole_ref[...] = jnp.where(spots(count, block), projection, gram)
    half = count // 2
    core = lax.axis_index("member") % 2
    keep_ref[...] = whole_ref[pl.ds(pl.multiple_of(core * half, half), half), :]
    send_ref[...] = whole_ref[pl.ds(pl.multiple_of((1 - core) * half, half), half), :]


def gram_of(spread_state, cell, value, var, block, cols):
    count = spread_state.shape[0]
    return pl.pallas_call(
        functools.partial(gram_kernel, block, cols),
        out_shape=[jax.ShapeDtypeStruct((count // 2, count), jnp.float32)] * 2,
        scratch_shapes=[pltpu.VMEM((count, count), jnp.float32)],
        compiler_params=pltpu.CompilerParams(vmem_limit_bytes=VMEM),
        cost_estimate=cost(6 * 2 * count * cols * cell.shape[1], 4 * count * cols),
        name="gram",
    )(spread_state, cell, value, var)


def transform_kernel(block, keep_ref, got_ref, weights_ref, packed_ref):
    half, count = keep_ref.shape
    core = lax.axis_index("member") % 2
    packed_ref[pl.ds(pl.multiple_of(core * half, half), half), :] = keep_ref[...]
    packed_ref[pl.ds(pl.multiple_of((1 - core) * half, half), half), :] = got_ref[...]
    packed = packed_ref[...]
    places = spots(count, block)
    projection = jnp.sum(jnp.where(places, packed, 0.0), axis=1, keepdims=True)
    gram = jnp.where(places, packed.T, packed)
    i = lax.broadcasted_iota(jnp.int32, (count, count), 0)
    j = lax.broadcasted_iota(jnp.int32, (count, count), 1)
    identity = jnp.where(i == j, 1.0, 0.0)
    system = identity + gram / (count - 1)
    scale = jnp.sqrt(jnp.sum(jnp.sum(system * system, axis=1, keepdims=True), axis=0, keepdims=True))
    current = system / scale
    root_inv = identity
    for step in range(NS_ITERS):
        parts, inv_parts = halves(current), halves(root_inv)
        product = current if step == 0 else dot3(inv_parts, parts)
        factor = 1.5 * identity - 0.5 * product
        factor_parts = halves(factor)
        if step < NS_ITERS - 1:
            current = dot3(parts, factor_parts)
        root_inv = factor if step == 0 else dot3(factor_parts, inv_parts)
    root = root_inv / jnp.sqrt(scale)

    def times(column):
        return jnp.sum(root * jnp.sum(jnp.where(i == j, column, 0.0), axis=0, keepdims=True), axis=1, keepdims=True)

    weights_ref[...] = times(times(projection)) / (count - 1) + root


def transform(keep, got, block):
    count = keep.shape[1]
    return pl.pallas_call(
        functools.partial(transform_kernel, block),
        out_shape=jax.ShapeDtypeStruct((count, count), jnp.float32),
        scratch_shapes=[pltpu.VMEM((count, count), jnp.float32)],
        compiler_params=pltpu.CompilerParams(vmem_limit_bytes=VMEM),
        cost_estimate=cost(6 * 2 * 14 * count ** 3, 8 * count ** 2),
        name="transform",
    )(keep, got)


def mix_kernel(weights_ref, state_ref, out_ref):
    weights = halves(weights_ref[...])
    count, width = state_ref.shape
    for first in range(0, width, MIX_BLOCK):
        values = state_ref[:, first:first + MIX_BLOCK]
        centre = jnp.sum(values, axis=0, keepdims=True) / count
        out_ref[:, first:first + MIX_BLOCK] = centre + dot3(weights, halves(values - centre), ((0,), (0,)))


def mix(weights, spread_state):
    count, width = spread_state.shape
    return pl.pallas_call(
        mix_kernel,
        out_shape=jax.ShapeDtypeStruct((count, width), jnp.float32),
        compiler_params=pltpu.CompilerParams(vmem_limit_bytes=VMEM),
        cost_estimate=cost(6 * 2 * count * count * width, 8 * count * width),
        name="mix",
    )(weights, spread_state)


def unfold_kernel(rows_ref, out_ref, lanes_ref, whole_ref, sems):
    members, fields, rows, cols = whole_ref.shape
    chunks = cols // LANES
    copies = []
    for k in range(fields):
        for c in range(k * chunks, (k + 1) * chunks):
            lanes_ref[c] = rows_ref[:, c * LANES:(c + 1) * LANES]
        for m in range(members):
            for c in range(chunks):
                whole_ref[m, k, :, c * LANES:(c + 1) * LANES] = lanes_ref[k * chunks + c, pl.ds(m, rows, stride=members), :]
        copies.append(pltpu.make_async_copy(whole_ref.at[:, k], out_ref.at[:, k], sems.at[k]))
        copies[-1].start()
    for copy in copies:
        copy.wait()


def unfold(rows, shape):
    return pl.pallas_call(
        unfold_kernel,
        out_shape=jax.ShapeDtypeStruct(shape, jnp.float32),
        out_specs=pl.BlockSpec(memory_space=pl.ANY),
        scratch_shapes=[
            pltpu.VMEM((rows.shape[1] // LANES, rows.shape[0], LANES), jnp.float32),
            pltpu.VMEM(shape, jnp.float32),
            pltpu.SemaphoreType.DMA((shape[1],)),
        ],
        compiler_params=pltpu.CompilerParams(vmem_limit_bytes=VMEM),
        cost_estimate=cost(0, 8 * rows.size),
        name="unfold",
    )(rows)


def exchange(blocks, axis, groups=None):
    return lax.all_to_all(blocks, axis, split_axis=0, concat_axis=0, tiled=True, axis_index_groups=groups)


def spread(block, axis, count, groups=None):
    return exchange(jnp.broadcast_to(block, (count,) + block.shape), axis, groups)


def shards(state, depth, obs_cell, obs_value, obs_var):
    bands, tiles = lax.axis_size("space"), lax.axis_size("member")
    members, rows, fields, cols = state.shape
    ensemble, chips = tiles * members, tiles // 2
    sibling = [(i, i ^ 1) for i in range(tiles)]

    state = state.transpose(0, 2, 1, 3)
    same_core = [[2 * q + core for q in range(chips)] for core in range(2)]
    upper = [(i, i ^ 1) for i in range(bands)]
    lower = [pair for i in range(1, bands - 1, 2) for pair in ((i, i + 1), (i + 1, i))]

    first, second = edges(state, depth)
    first = lax.ppermute(first, "space", upper)
    second = lax.ppermute(second, "space", lower)
    ahead = forecast(state, first, second, depth, bands)
    ahead = exchange(ahead, "member").reshape(ensemble, fields * cols)

    keep, send = gram_of(ahead, obs_cell[0], obs_value[0], obs_var[0], members, cols)
    half = keep + lax.ppermute(send, "member", sibling)
    part = jnp.sum(exchange(half.reshape(bands, -1, ensemble), "space"), axis=0)
    part = jnp.sum(spread(part, "member", chips, same_core), axis=0)
    half = spread(part, "space", bands).reshape(ensemble // 2, ensemble)
    weights = transform(half, lax.ppermute(half, "member", sibling), members)

    analysed = mix(weights, ahead)
    back = exchange(analysed.reshape(tiles, members, fields * cols), "member").reshape(ensemble, fields * cols)
    return unfold(back, (members, fields, rows, cols)).transpose(0, 2, 1, 3)


def solution(mesh):
    placed = (
        P("member", "space", None, None),
        P("space", None),
        P("space", "member", None),
        P("space", "member", None),
        P("space", "member", None),
    )
    return jax.shard_map(
        shards,
        mesh=mesh,
        in_specs=placed,
        out_specs=P("member", "space", None, None),
        check_vma=False,
    )
```

```python
import functools

import jax
import jax.numpy as jnp
from jax import lax
from jax.experimental import pallas as pl
from jax.experimental.pallas import tpu as pltpu
from jax.sharding import PartitionSpec as P

STEPS = 3
NS_ITERS = 5
COURANT = 0.3
HALO = 2 * STEPS
LANES = 128
ROW_BLOCK = 4
VMEM = 40 * 1024 * 1024
ALL_VMEM = 60 * 1024 * 1024
HIGHEST = lax.Precision.HIGHEST


def dot(a, b, dims=((1,), (0,))):
    return lax.dot_general(a, b, (dims, ((), ())), precision=HIGHEST, preferred_element_type=jnp.float32)


def halves(a):
    high = a.astype(jnp.bfloat16)
    return high, (a - high.astype(jnp.float32)).astype(jnp.bfloat16)


def dot3(a, b, dims=((1,), (0,))):
    def one(x, y):
        return lax.dot_general(x, y, (dims, ((), ())), preferred_element_type=jnp.float32)

    (a_high, a_low), (b_high, b_low) = a, b
    return one(a_high, b_high) + (one(a_high, b_low) + one(a_low, b_high))


def picked(a, picks):
    high, low = halves(a)
    rest = (a - high.astype(jnp.float32) - low.astype(jnp.float32)).astype(jnp.bfloat16)
    parts = [jnp.dot(x, picks, preferred_element_type=jnp.float32) for x in (high, low, rest)]
    return parts[0] + (parts[1] + parts[2])


def cost(flops, bytes_accessed):
    return pl.CostEstimate(flops=flops, bytes_accessed=bytes_accessed, transcendentals=0)


def edges_kernel(state_ref, depth_ref, first_ref, second_ref, top_ref, bottom_ref, depth_top_ref, depth_bottom_ref, sems):
    members, fields, block, cols = top_ref.shape
    rows = depth_ref.shape[0]
    even = lax.axis_index("space") % 2 == 0
    sides = (
        (bottom_ref, depth_bottom_ref, rows - block, True),
        (top_ref, depth_top_ref, 0, False),
    )
    copies = []
    for side, (field_ref, edge_ref, start, _) in enumerate(sides):
        copies.append([
            pltpu.make_async_copy(state_ref.at[m, :, pl.ds(start, block), :], field_ref.at[m], sems.at[side, m])
            for m in range(members)
        ] + [pltpu.make_async_copy(depth_ref.at[pl.ds(start, block), :], edge_ref, sems.at[side, members])])
        for copy in copies[-1]:
            copy.start()

    def write(out_ref, field_ref, edge_ref, last):
        for c in range(cols // LANES):
            lanes = slice(c * LANES, (c + 1) * LANES)
            at = 0
            for k in range(fields):
                count = HALO if k == 2 else HALO - 1
                first = block - count if last else 0
                for m in range(members):
                    out_ref[c, pl.ds(at + m, count, stride=members), :] = field_ref[m, k, first:first + count, lanes]
                at += count * members
            first = block - HALO + 1 if last else 0
            out_ref[c, at:at + HALO - 1, :] = edge_ref[first:first + HALO - 1, lanes]

    for (field_ref, edge_ref, _, last), waits in zip(sides, copies):
        for copy in waits:
            copy.wait()
        for out_ref, here in ((first_ref, even), (second_ref, jnp.logical_not(even))):
            @pl.when(here if last else jnp.logical_not(here))
            def _():
                write(out_ref, field_ref, edge_ref, last)


def edges(state, depth):
    members, fields, rows, cols = state.shape
    block = 8
    shape = jax.ShapeDtypeStruct((cols // LANES, (3 * HALO - 2) * members + 8, LANES), jnp.float32)
    return pl.pallas_call(
        edges_kernel,
        in_specs=[pl.BlockSpec(memory_space=pl.ANY)] * 2,
        out_shape=[shape] * 2,
        scratch_shapes=[
            pltpu.VMEM((members, fields, block, cols), jnp.float32),
            pltpu.VMEM((members, fields, block, cols), jnp.float32),
            pltpu.VMEM((block, cols), jnp.float32),
            pltpu.VMEM((block, cols), jnp.float32),
            pltpu.SemaphoreType.DMA((2, members + 1)),
        ],
        compiler_params=pltpu.CompilerParams(vmem_limit_bytes=ALL_VMEM),
        cost_estimate=cost(0, 2 * state.size),
        name="edges",
    )(state, depth)


def forecast_kernel(bands, state_ref, first_ref, second_ref, depth_ref, height_ref, wind_ref, field_ref, pull_ref):
    members, fields, rows, cols = state_ref.shape
    chunks = cols // LANES
    band = lax.axis_index("space")
    lane = lax.broadcasted_iota(jnp.int32, (1, LANES), 1)

    even = band % 2 == 0

    def above(c, first, last):
        return jnp.where(even, second_ref[c, first:last, :], first_ref[c, first:last, :])

    def below(c, first, last):
        return jnp.where(even, first_ref[c, first:last, :], second_ref[c, first:last, :])

    for c in range(chunks):
        lanes = slice(c * LANES, (c + 1) * LANES)
        at = 0
        for k in range(fields):
            count = HALO if k == 2 else HALO - 1
            size = count * members
            field_ref[k, c, (HALO - count) * members:HALO * members, :] = above(c, at, at + size)
            field_ref[k, c, (HALO + rows) * members:(HALO + rows + count) * members, :] = below(c, at, at + size)
            at += size
            for m in range(members):
                field_ref[k, c, pl.ds(HALO * members + m, rows, stride=members), :] = state_ref[m, k, :, lanes]
        pull_above = COURANT * above(c, at, at + HALO - 1)
        pull_here = COURANT * depth_ref[:, lanes]
        pull_below = COURANT * below(c, at, at + HALO - 1)
        for m in range(members):
            pull_ref[c, pl.ds(members + m, HALO - 1, stride=members), :] = pull_above
            pull_ref[c, pl.ds(HALO * members + m, rows, stride=members), :] = pull_here
            pull_ref[c, pl.ds((HALO + rows) * members + m, HALO - 1, stride=members), :] = pull_below

    def cols_diff(parts):
        left = [pltpu.roll(p, 1, 1) for p in parts]
        right = [pltpu.roll(p, LANES - 1, 1) for p in parts]
        return [
            jnp.where(lane == LANES - 1, right[(c + 1) % chunks], right[c]) - jnp.where(lane == 0, left[c - 1], left[c])
            for c in range(chunks)
        ]

    def take(k, first, count):
        return [field_ref[k, c, first * members:(first + count) * members, :] for c in range(chunks)]

    def push_of(first, count):
        if first >= HALO and first + count <= HALO + rows:
            return COURANT
        row = lax.broadcasted_iota(jnp.int32, (count * members, LANES), 0) + (first + band * rows - HALO) * members
        return jnp.where(jnp.logical_and(row >= 0, row < bands * rows * members), COURANT, 0.0)

    def blocks(first, last):
        cuts = sorted({HALO, HALO + rows} | set(range(HALO, HALO + rows, ROW_BLOCK)))
        ends = [first] + [e for e in cuts if first < e < last] + [last]
        return [(lo, hi - lo) for lo, hi in zip(ends[:-1], ends[1:])]

    for step in range(STEPS):
        reach = 2 * (STEPS - 1 - step)
        for first, count in blocks(HALO - reach - 1, HALO + rows + reach + 1):
            height = take(0, first, count)
            slope = cols_diff(take(1, first, count))
            north = take(2, first + 1, count)
            south = take(2, first - 1, count)
            span = slice(first * members, (first + count) * members)
            for c in range(chunks):
                field_ref[0, c, span, :] = height[c] - pull_ref[c, span, :] * (slope[c] + (north[c] - south[c]))
        for first, count in blocks(HALO - reach, HALO + rows + reach):
            slope = cols_diff(take(0, first, count))
            zonal = take(1, first, count)
            meridional = take(2, first, count)
            north = take(0, first + 1, count)
            south = take(0, first - 1, count)
            push = push_of(first, count)
            span = slice(first * members, (first + count) * members)
            for c in range(chunks):
                zonal[c] = zonal[c] - COURANT * slope[c]
                meridional[c] = meridional[c] - push * (north[c] - south[c])
                if step < STEPS - 1:
                    field_ref[1, c, span, :] = zonal[c]
                    field_ref[2, c, span, :] = meridional[c]
            if step == STEPS - 1:
                here = take(0, first, count)
                for k, parts in enumerate((here, zonal, meridional)):
                    for c in range(chunks):
                        for t in range(count):
                            out_ref, start = (height_ref, 0) if k == 0 else (wind_ref, (k - 1) * cols)
                            lanes = slice(start + c * LANES, start + (c + 1) * LANES)
                            out_ref[first - HALO + t, :, lanes] = parts[c][t * members:(t + 1) * members]


def forecast(state, first, second, depth, bands):
    members, fields, rows, cols = state.shape
    total = rows + 2 * HALO
    return pl.pallas_call(
        functools.partial(forecast_kernel, bands),
        out_shape=[
            jax.ShapeDtypeStruct((rows, members, cols), jnp.float32),
            jax.ShapeDtypeStruct((rows, members, 2 * cols), jnp.float32),
        ],
        scratch_shapes=[
            pltpu.VMEM((fields, cols // LANES, total * members, LANES), jnp.float32),
            pltpu.VMEM((cols // LANES, total * members, LANES), jnp.float32),
        ],
        compiler_params=pltpu.CompilerParams(vmem_limit_bytes=VMEM),
        cost_estimate=cost(STEPS * 12 * state.size, 8 * state.size),
        name="forecast",
    )(state, first, second, depth)


def spots(count, block):
    i = lax.broadcasted_iota(jnp.int32, (count, count), 0)
    j = lax.broadcasted_iota(jnp.int32, (count, count), 1)
    return j == (i - i % block) + (i + 1) % block


def gram_kernel(block, height_ref, cell_ref, value_ref, var_ref, keep_ref, send_ref, whole_ref):
    count, cols = height_ref.shape
    number = cell_ref.shape[1]
    picks = lax.broadcasted_iota(jnp.int32, (cols, number), 0) == cell_ref[...]
    seen = picked(height_ref[...], jnp.where(picks, 1.0, 0.0).astype(jnp.bfloat16))
    centre = jnp.sum(seen, axis=0, keepdims=True) / count
    observed = seen - centre
    innovation = value_ref[...] - centre
    weighted = observed / var_ref[...]
    gram = dot(weighted, observed, ((1,), (1,)))
    projection = jnp.sum(weighted * innovation, axis=1, keepdims=True)
    whole_ref[...] = jnp.where(spots(count, block), projection, gram)
    half = count // 2
    core = lax.axis_index("member") % 2
    keep_ref[...] = whole_ref[pl.ds(pl.multiple_of(core * half, half), half), :]
    send_ref[...] = whole_ref[pl.ds(pl.multiple_of((1 - core) * half, half), half), :]


def gram_of(height, cell, value, var, block):
    count, cols = height.shape
    return pl.pallas_call(
        functools.partial(gram_kernel, block),
        out_shape=[jax.ShapeDtypeStruct((count // 2, count), jnp.float32)] * 2,
        scratch_shapes=[pltpu.VMEM((count, count), jnp.float32)],
        compiler_params=pltpu.CompilerParams(vmem_limit_bytes=VMEM),
        cost_estimate=cost(6 * 2 * count * cols * cell.shape[1], 4 * count * cols),
        name="gram",
    )(height, cell, value, var)


def transform_kernel(block, keep_ref, got_ref, weights_ref, packed_ref):
    half, count = keep_ref.shape
    core = lax.axis_index("member") % 2
    packed_ref[pl.ds(pl.multiple_of(core * half, half), half), :] = keep_ref[...]
    packed_ref[pl.ds(pl.multiple_of((1 - core) * half, half), half), :] = got_ref[...]
    packed = packed_ref[...]
    places = spots(count, block)
    projection = jnp.sum(jnp.where(places, packed, 0.0), axis=1, keepdims=True)
    gram = jnp.where(places, packed.T, packed)
    i = lax.broadcasted_iota(jnp.int32, (count, count), 0)
    j = lax.broadcasted_iota(jnp.int32, (count, count), 1)
    identity = jnp.where(i == j, 1.0, 0.0)
    system = identity + gram / (count - 1)
    scale = jnp.sqrt(jnp.sum(jnp.sum(system * system, axis=1, keepdims=True), axis=0, keepdims=True))
    current = system / scale
    root_inv = identity
    for step in range(NS_ITERS):
        parts, inv_parts = halves(current), halves(root_inv)
        product = current if step == 0 else dot3(inv_parts, parts)
        factor = 1.5 * identity - 0.5 * product
        factor_parts = halves(factor)
        if step < NS_ITERS - 1:
            current = dot3(parts, factor_parts)
        root_inv = factor if step == 0 else dot3(factor_parts, inv_parts)
    root = root_inv / jnp.sqrt(scale)

    def times(column):
        return jnp.sum(root * jnp.sum(jnp.where(i == j, column, 0.0), axis=0, keepdims=True), axis=1, keepdims=True)

    weights_ref[...] = times(times(projection)) / (count - 1) + root


def transform(keep, got, block):
    count = keep.shape[1]
    return pl.pallas_call(
        functools.partial(transform_kernel, block),
        out_shape=jax.ShapeDtypeStruct((count, count), jnp.float32),
        scratch_shapes=[pltpu.VMEM((count, count), jnp.float32)],
        compiler_params=pltpu.CompilerParams(vmem_limit_bytes=VMEM),
        cost_estimate=cost(6 * 2 * 14 * count ** 3, 8 * count ** 2),
        name="transform",
    )(keep, got)


def mix_kernel(weights_ref, height_ref, wind_ref, out_ref):
    weights = halves(weights_ref[...])
    count, cols = height_ref.shape
    for first in range(0, 3 * cols, cols):
        values = height_ref[...] if first == 0 else wind_ref[:, first - cols:first]
        centre = jnp.sum(values, axis=0, keepdims=True) / count
        out_ref[:, first:first + cols] = centre + dot3(weights, halves(values - centre), ((0,), (0,)))


def mix(weights, height, wind):
    count, cols = height.shape
    return pl.pallas_call(
        mix_kernel,
        out_shape=jax.ShapeDtypeStruct((count, 3 * cols), jnp.float32),
        compiler_params=pltpu.CompilerParams(vmem_limit_bytes=VMEM),
        cost_estimate=cost(3 * 2 * count * count * 3 * cols, 4 * count * 6 * cols),
        name="mix",
    )(weights, height, wind)


def unfold_kernel(rows_ref, out_ref, lanes_ref, whole_ref, sems):
    members, fields, rows, cols = whole_ref.shape
    chunks = cols // LANES
    copies = []
    for k in range(fields):
        for c in range(k * chunks, (k + 1) * chunks):
            lanes_ref[c] = rows_ref[:, c * LANES:(c + 1) * LANES]
        for m in range(members):
            for c in range(chunks):
                whole_ref[m, k, :, c * LANES:(c + 1) * LANES] = lanes_ref[k * chunks + c, pl.ds(m, rows, stride=members), :]
        copies.append(pltpu.make_async_copy(whole_ref.at[:, k], out_ref.at[:, k], sems.at[k]))
        copies[-1].start()
    for copy in copies:
        copy.wait()


def unfold(rows, shape):
    return pl.pallas_call(
        unfold_kernel,
        out_shape=jax.ShapeDtypeStruct(shape, jnp.float32),
        out_specs=pl.BlockSpec(memory_space=pl.ANY),
        scratch_shapes=[
            pltpu.VMEM((rows.shape[1] // LANES, rows.shape[0], LANES), jnp.float32),
            pltpu.VMEM(shape, jnp.float32),
            pltpu.SemaphoreType.DMA((shape[1],)),
        ],
        compiler_params=pltpu.CompilerParams(vmem_limit_bytes=VMEM),
        cost_estimate=cost(0, 8 * rows.size),
        name="unfold",
    )(rows)


def exchange(blocks, axis, groups=None):
    return lax.all_to_all(blocks, axis, split_axis=0, concat_axis=0, tiled=True, axis_index_groups=groups)


def spread(block, axis, count, groups=None):
    return exchange(jnp.broadcast_to(block, (count,) + block.shape), axis, groups)


def shards(state, depth, obs_cell, obs_value, obs_var):
    bands, tiles = lax.axis_size("space"), lax.axis_size("member")
    members, rows, fields, cols = state.shape
    ensemble, chips = tiles * members, tiles // 2
    sibling = [(i, i ^ 1) for i in range(tiles)]

    state = state.transpose(0, 2, 1, 3)
    every = ("member", "space")
    planes = [
        [(y * tiles // 4 + 2 * z + core) * bands + 4 * low + x for z in range(tiles // 8) for low in range(bands // 4)]
        for y in range(4) for core in range(2) for x in range(4)
    ]
    upper = [(i, i ^ 1) for i in range(bands)]
    lower = [pair for i in range(1, bands - 1, 2) for pair in ((i, i + 1), (i + 1, i))]

    first, second = edges(state, depth)
    first = lax.ppermute(first, "space", upper)
    second = lax.ppermute(second, "space", lower)
    height, wind = forecast(state, first, second, depth, bands)
    height = exchange(height, "member").reshape(ensemble, cols)
    height, wind = lax.optimization_barrier((height, wind))
    wind = exchange(wind, "member").reshape(ensemble, 2 * cols)

    keep, send = gram_of(height, obs_cell[0], obs_value[0], obs_var[0], members)
    half = keep + lax.ppermute(send, "member", sibling)

    def others(value, axis, unit):
        return [lax.ppermute(value, axis, [(i, i ^ (unit * k)) for i in range(lax.axis_size(axis))]) for k in (1, 2, 3)]

    for axis, unit in (("space", 1), ("member", tiles // 4)):
        one, two, three = others(half, axis, unit)
        half = (half + one) + (two + three)
    half, wind = lax.optimization_barrier((half, wind))
    part = jnp.sum(exchange(half.reshape(len(planes[0]), -1, ensemble), every, planes), axis=0)
    half = spread(part, every, len(planes[0]), planes).reshape(half.shape)
    weights = transform(half, lax.ppermute(half, "member", sibling), members)

    analysed = mix(weights, height, wind)
    back = exchange(analysed.reshape(tiles, members, fields * cols), "member").reshape(ensemble, fields * cols)
    return unfold(back, (members, fields, rows, cols)).transpose(0, 2, 1, 3)


def solution(mesh):
    placed = (
        P("member", "space", None, None),
        P("space", None),
        P("space", "member", None),
        P("space", "member", None),
        P("space", "member", None),
    )
    return jax.shard_map(
        shards,
        mesh=mesh,
        in_specs=placed,
        out_specs=P("member", "space", None, None),
        check_vma=False,
    )
```

```python
import functools

import jax
import jax.numpy as jnp
from jax import lax
from jax.experimental import pallas as pl
from jax.experimental.pallas import tpu as pltpu
from jax.sharding import PartitionSpec as P

STEPS = 3
NS_ITERS = 5
COURANT = 0.3
HALO = 2 * STEPS
LANES = 128
ROW_BLOCK = 4
VMEM = 40 * 1024 * 1024
ALL_VMEM = 60 * 1024 * 1024
HIGHEST = lax.Precision.HIGHEST


def dot(a, b, dims=((1,), (0,))):
    return lax.dot_general(a, b, (dims, ((), ())), precision=HIGHEST, preferred_element_type=jnp.float32)


def halves(a):
    high = a.astype(jnp.bfloat16)
    return high, (a - high.astype(jnp.float32)).astype(jnp.bfloat16)


def dot3(a, b, dims=((1,), (0,))):
    def one(x, y):
        return lax.dot_general(x, y, (dims, ((), ())), preferred_element_type=jnp.float32)

    (a_high, a_low), (b_high, b_low) = a, b
    return one(a_high, b_high) + (one(a_high, b_low) + one(a_low, b_high))


def picked(a, picks):
    high, low = halves(a)
    rest = (a - high.astype(jnp.float32) - low.astype(jnp.float32)).astype(jnp.bfloat16)
    parts = [jnp.dot(x, picks, preferred_element_type=jnp.float32) for x in (high, low, rest)]
    return parts[0] + (parts[1] + parts[2])


def cost(flops, bytes_accessed):
    return pl.CostEstimate(flops=flops, bytes_accessed=bytes_accessed, transcendentals=0)


def edges_kernel(state_ref, depth_ref, first_ref, second_ref, top_ref, bottom_ref, depth_top_ref, depth_bottom_ref, sems):
    members, fields, block, cols = top_ref.shape
    rows = depth_ref.shape[0]
    even = lax.axis_index("space") % 2 == 0
    sides = (
        (bottom_ref, depth_bottom_ref, rows - block, True),
        (top_ref, depth_top_ref, 0, False),
    )
    copies = []
    for side, (field_ref, edge_ref, start, _) in enumerate(sides):
        copies.append([
            pltpu.make_async_copy(state_ref.at[m, :, pl.ds(start, block), :], field_ref.at[m], sems.at[side, m])
            for m in range(members)
        ] + [pltpu.make_async_copy(depth_ref.at[pl.ds(start, block), :], edge_ref, sems.at[side, members])])
        for copy in copies[-1]:
            copy.start()

    def write(out_ref, field_ref, edge_ref, last):
        for c in range(cols // LANES):
            lanes = slice(c * LANES, (c + 1) * LANES)
            at = 0
            for k in range(fields):
                count = HALO if k == 2 else HALO - 1
                first = block - count if last else 0
                for m in range(members):
                    out_ref[c, pl.ds(at + m, count, stride=members), :] = field_ref[m, k, first:first + count, lanes]
                at += count * members
            first = block - HALO + 1 if last else 0
            out_ref[c, at:at + HALO - 1, :] = edge_ref[first:first + HALO - 1, lanes]

    for (field_ref, edge_ref, _, last), waits in zip(sides, copies):
        for copy in waits:
            copy.wait()
        for out_ref, here in ((first_ref, even), (second_ref, jnp.logical_not(even))):
            @pl.when(here if last else jnp.logical_not(here))
            def _():
                write(out_ref, field_ref, edge_ref, last)


def edges(state, depth):
    members, fields, rows, cols = state.shape
    block = 8
    shape = jax.ShapeDtypeStruct((cols // LANES, (3 * HALO - 2) * members + 8, LANES), jnp.float32)
    return pl.pallas_call(
        edges_kernel,
        in_specs=[pl.BlockSpec(memory_space=pl.ANY)] * 2,
        out_shape=[shape] * 2,
        scratch_shapes=[
            pltpu.VMEM((members, fields, block, cols), jnp.float32),
            pltpu.VMEM((members, fields, block, cols), jnp.float32),
            pltpu.VMEM((block, cols), jnp.float32),
            pltpu.VMEM((block, cols), jnp.float32),
            pltpu.SemaphoreType.DMA((2, members + 1)),
        ],
        compiler_params=pltpu.CompilerParams(vmem_limit_bytes=ALL_VMEM),
        cost_estimate=cost(0, 2 * state.size),
        name="edges",
    )(state, depth)


def forecast_kernel(bands, state_ref, first_ref, second_ref, depth_ref, height_ref, wind_ref, field_ref, pull_ref):
    members, fields, rows, cols = state_ref.shape
    chunks = cols // LANES
    band = lax.axis_index("space")
    lane = lax.broadcasted_iota(jnp.int32, (1, LANES), 1)

    even = band % 2 == 0

    def above(c, first, last):
        return jnp.where(even, second_ref[c, first:last, :], first_ref[c, first:last, :])

    def below(c, first, last):
        return jnp.where(even, first_ref[c, first:last, :], second_ref[c, first:last, :])

    for c in range(chunks):
        lanes = slice(c * LANES, (c + 1) * LANES)
        at = 0
        for k in range(fields):
            count = HALO if k == 2 else HALO - 1
            size = count * members
            field_ref[k, c, (HALO - count) * members:HALO * members, :] = above(c, at, at + size)
            field_ref[k, c, (HALO + rows) * members:(HALO + rows + count) * members, :] = below(c, at, at + size)
            at += size
            for m in range(members):
                field_ref[k, c, pl.ds(HALO * members + m, rows, stride=members), :] = state_ref[m, k, :, lanes]
        pull_above = COURANT * above(c, at, at + HALO - 1)
        pull_here = COURANT * depth_ref[:, lanes]
        pull_below = COURANT * below(c, at, at + HALO - 1)
        for m in range(members):
            pull_ref[c, pl.ds(members + m, HALO - 1, stride=members), :] = pull_above
            pull_ref[c, pl.ds(HALO * members + m, rows, stride=members), :] = pull_here
            pull_ref[c, pl.ds((HALO + rows) * members + m, HALO - 1, stride=members), :] = pull_below

    def cols_diff(parts):
        left = [pltpu.roll(p, 1, 1) for p in parts]
        right = [pltpu.roll(p, LANES - 1, 1) for p in parts]
        return [
            jnp.where(lane == LANES - 1, right[(c + 1) % chunks], right[c]) - jnp.where(lane == 0, left[c - 1], left[c])
            for c in range(chunks)
        ]

    def take(k, first, count):
        return [field_ref[k, c, first * members:(first + count) * members, :] for c in range(chunks)]

    def push_of(first, count):
        if first >= HALO and first + count <= HALO + rows:
            return COURANT
        row = lax.broadcasted_iota(jnp.int32, (count * members, LANES), 0) + (first + band * rows - HALO) * members
        return jnp.where(jnp.logical_and(row >= 0, row < bands * rows * members), COURANT, 0.0)

    def blocks(first, last):
        cuts = sorted({HALO, HALO + rows} | set(range(HALO, HALO + rows, ROW_BLOCK)))
        ends = [first] + [e for e in cuts if first < e < last] + [last]
        return [(lo, hi - lo) for lo, hi in zip(ends[:-1], ends[1:])]

    for step in range(STEPS):
        reach = 2 * (STEPS - 1 - step)
        for first, count in blocks(HALO - reach - 1, HALO + rows + reach + 1):
            height = take(0, first, count)
            slope = cols_diff(take(1, first, count))
            north = take(2, first + 1, count)
            south = take(2, first - 1, count)
            span = slice(first * members, (first + count) * members)
            for c in range(chunks):
                field_ref[0, c, span, :] = height[c] - pull_ref[c, span, :] * (slope[c] + (north[c] - south[c]))
        for first, count in blocks(HALO - reach, HALO + rows + reach):
            slope = cols_diff(take(0, first, count))
            zonal = take(1, first, count)
            meridional = take(2, first, count)
            north = take(0, first + 1, count)
            south = take(0, first - 1, count)
            push = push_of(first, count)
            span = slice(first * members, (first + count) * members)
            for c in range(chunks):
                zonal[c] = zonal[c] - COURANT * slope[c]
                meridional[c] = meridional[c] - push * (north[c] - south[c])
                if step < STEPS - 1:
                    field_ref[1, c, span, :] = zonal[c]
                    field_ref[2, c, span, :] = meridional[c]
            if step == STEPS - 1:
                here = take(0, first, count)
                for k, parts in enumerate((here, zonal, meridional)):
                    for c in range(chunks):
                        for t in range(count):
                            out_ref, start = (height_ref, 0) if k == 0 else (wind_ref, (k - 1) * cols)
                            lanes = slice(start + c * LANES, start + (c + 1) * LANES)
                            out_ref[first - HALO + t, :, lanes] = parts[c][t * members:(t + 1) * members]


def forecast(state, first, second, depth, bands):
    members, fields, rows, cols = state.shape
    total = rows + 2 * HALO
    return pl.pallas_call(
        functools.partial(forecast_kernel, bands),
        out_shape=[
            jax.ShapeDtypeStruct((rows, members, cols), jnp.float32),
            jax.ShapeDtypeStruct((rows, members, 2 * cols), jnp.float32),
        ],
        scratch_shapes=[
            pltpu.VMEM((fields, cols // LANES, total * members, LANES), jnp.float32),
            pltpu.VMEM((cols // LANES, total * members, LANES), jnp.float32),
        ],
        compiler_params=pltpu.CompilerParams(vmem_limit_bytes=VMEM),
        cost_estimate=cost(STEPS * 12 * state.size, 8 * state.size),
        name="forecast",
    )(state, first, second, depth)


def spots(count, block):
    i = lax.broadcasted_iota(jnp.int32, (count, count), 0)
    j = lax.broadcasted_iota(jnp.int32, (count, count), 1)
    return j == (i - i % block) + (i + 1) % block


def gram_kernel(block, height_ref, cell_ref, value_ref, var_ref, keep_ref, send_ref, whole_ref):
    count, cols = height_ref.shape
    number = cell_ref.shape[1]
    picks = lax.broadcasted_iota(jnp.int32, (cols, number), 0) == cell_ref[...]
    seen = picked(height_ref[...], jnp.where(picks, 1.0, 0.0).astype(jnp.bfloat16))
    centre = jnp.sum(seen, axis=0, keepdims=True) / count
    observed = seen - centre
    innovation = value_ref[...] - centre
    weighted = observed / var_ref[...]
    gram = dot(weighted, observed, ((1,), (1,)))
    projection = jnp.sum(weighted * innovation, axis=1, keepdims=True)
    whole_ref[...] = jnp.where(spots(count, block), projection, gram)
    half = count // 2
    core = lax.axis_index("member") % 2
    keep_ref[...] = whole_ref[pl.ds(pl.multiple_of(core * half, half), half), :]
    send_ref[...] = whole_ref[pl.ds(pl.multiple_of((1 - core) * half, half), half), :]


def gram_of(height, cell, value, var, block):
    count, cols = height.shape
    return pl.pallas_call(
        functools.partial(gram_kernel, block),
        out_shape=[jax.ShapeDtypeStruct((count // 2, count), jnp.float32)] * 2,
        scratch_shapes=[pltpu.VMEM((count, count), jnp.float32)],
        compiler_params=pltpu.CompilerParams(vmem_limit_bytes=VMEM),
        cost_estimate=cost(6 * 2 * count * cols * cell.shape[1], 4 * count * cols),
        name="gram",
    )(height, cell, value, var)


def transform_kernel(block, keep_ref, got_ref, weights_ref, packed_ref):
    half, count = keep_ref.shape
    core = lax.axis_index("member") % 2
    packed_ref[pl.ds(pl.multiple_of(core * half, half), half), :] = keep_ref[...]
    packed_ref[pl.ds(pl.multiple_of((1 - core) * half, half), half), :] = got_ref[...]
    packed = packed_ref[...]
    places = spots(count, block)
    projection = jnp.sum(jnp.where(places, packed, 0.0), axis=1, keepdims=True)
    gram = jnp.where(places, packed.T, packed)
    i = lax.broadcasted_iota(jnp.int32, (count, count), 0)
    j = lax.broadcasted_iota(jnp.int32, (count, count), 1)
    identity = jnp.where(i == j, 1.0, 0.0)
    system = identity + gram / (count - 1)
    scale = jnp.sqrt(jnp.sum(jnp.sum(system * system, axis=1, keepdims=True), axis=0, keepdims=True))
    current = system / scale
    root_inv = identity
    for step in range(NS_ITERS):
        parts, inv_parts = halves(current), halves(root_inv)
        product = current if step == 0 else dot3(inv_parts, parts)
        factor = 1.5 * identity - 0.5 * product
        factor_parts = halves(factor)
        if step < NS_ITERS - 1:
            current = dot3(parts, factor_parts)
        root_inv = factor if step == 0 else dot3(factor_parts, inv_parts)
    root = root_inv / jnp.sqrt(scale)

    def times(column):
        return jnp.sum(root * jnp.sum(jnp.where(i == j, column, 0.0), axis=0, keepdims=True), axis=1, keepdims=True)

    weights_ref[...] = times(times(projection)) / (count - 1) + root


def transform(keep, got, block):
    count = keep.shape[1]
    return pl.pallas_call(
        functools.partial(transform_kernel, block),
        out_shape=jax.ShapeDtypeStruct((count, count), jnp.float32),
        scratch_shapes=[pltpu.VMEM((count, count), jnp.float32)],
        compiler_params=pltpu.CompilerParams(vmem_limit_bytes=VMEM),
        cost_estimate=cost(6 * 2 * 14 * count ** 3, 8 * count ** 2),
        name="transform",
    )(keep, got)


def mix_kernel(weights_ref, height_ref, wind_ref, out_ref):
    weights = halves(weights_ref[...])
    count, cols = height_ref.shape
    for first in range(0, 3 * cols, cols):
        values = height_ref[...] if first == 0 else wind_ref[:, first - cols:first]
        centre = jnp.sum(values, axis=0, keepdims=True) / count
        out_ref[:, first:first + cols] = centre + dot3(weights, halves(values - centre), ((0,), (0,)))


def mix(weights, height, wind):
    count, cols = height.shape
    return pl.pallas_call(
        mix_kernel,
        out_shape=jax.ShapeDtypeStruct((count, 3 * cols), jnp.float32),
        compiler_params=pltpu.CompilerParams(vmem_limit_bytes=VMEM),
        cost_estimate=cost(3 * 2 * count * count * 3 * cols, 4 * count * 6 * cols),
        name="mix",
    )(weights, height, wind)


def unfold_kernel(rows_ref, out_ref, lanes_ref, whole_ref, sems):
    members, fields, rows, cols = whole_ref.shape
    chunks = cols // LANES
    copies = []
    for k in range(fields):
        for c in range(k * chunks, (k + 1) * chunks):
            lanes_ref[c] = rows_ref[:, c * LANES:(c + 1) * LANES]
        for m in range(members):
            for c in range(chunks):
                whole_ref[m, k, :, c * LANES:(c + 1) * LANES] = lanes_ref[k * chunks + c, pl.ds(m, rows, stride=members), :]
        copies.append(pltpu.make_async_copy(whole_ref.at[:, k], out_ref.at[:, k], sems.at[k]))
        copies[-1].start()
    for copy in copies:
        copy.wait()


def unfold(rows, shape):
    return pl.pallas_call(
        unfold_kernel,
        out_shape=jax.ShapeDtypeStruct(shape, jnp.float32),
        out_specs=pl.BlockSpec(memory_space=pl.ANY),
        scratch_shapes=[
            pltpu.VMEM((rows.shape[1] // LANES, rows.shape[0], LANES), jnp.float32),
            pltpu.VMEM(shape, jnp.float32),
            pltpu.SemaphoreType.DMA((shape[1],)),
        ],
        compiler_params=pltpu.CompilerParams(vmem_limit_bytes=VMEM),
        cost_estimate=cost(0, 8 * rows.size),
        name="unfold",
    )(rows)


def exchange(blocks, axis):
    return lax.all_to_all(blocks, axis, split_axis=0, concat_axis=0, tiled=True)


def shards(state, depth, obs_cell, obs_value, obs_var):
    bands, tiles = lax.axis_size("space"), lax.axis_size("member")
    members, rows, fields, cols = state.shape
    ensemble, chips = tiles * members, tiles // 2
    sibling = [(i, i ^ 1) for i in range(tiles)]

    state = state.transpose(0, 2, 1, 3)
    upper = [(i, i ^ 1) for i in range(bands)]
    lower = [pair for i in range(1, bands - 1, 2) for pair in ((i, i + 1), (i + 1, i))]

    first, second = edges(state, depth)
    first = lax.ppermute(first, "space", upper)
    second = lax.ppermute(second, "space", lower)
    height, wind = forecast(state, first, second, depth, bands)
    height = exchange(height, "member").reshape(ensemble, cols)
    height, wind = lax.optimization_barrier((height, wind))
    wind = exchange(wind, "member").reshape(ensemble, 2 * cols)

    keep, send = gram_of(height, obs_cell[0], obs_value[0], obs_var[0], members)
    half = keep + lax.ppermute(send, "member", sibling)

    def others(value, axis, unit):
        return [lax.ppermute(value, axis, [(i, i ^ (unit * k)) for i in range(lax.axis_size(axis))]) for k in (1, 2, 3)]

    for axis, unit in (("space", 1), ("member", tiles // 4)):
        one, two, three = others(half, axis, unit)
        half = (half + one) + (two + three)
    half, wind = lax.optimization_barrier((half, wind))
    half = half + lax.ppermute(half, "space", [(i, i ^ 4) for i in range(bands)])
    one, two, three = others(half, "member", 2)
    half = (half + one) + (two + three)
    weights = transform(half, lax.ppermute(half, "member", sibling), members)

    analysed = mix(weights, height, wind)
    back = exchange(analysed.reshape(tiles, members, fields * cols), "member").reshape(ensemble, fields * cols)
    return unfold(back, (members, fields, rows, cols)).transpose(0, 2, 1, 3)


def solution(mesh):
    placed = (
        P("member", "space", None, None),
        P("space", None),
        P("space", "member", None),
        P("space", "member", None),
        P("space", "member", None),
    )
    return jax.shard_map(
        shards,
        mesh=mesh,
        in_specs=placed,
        out_specs=P("member", "space", None, None),
        check_vma=False,
    )
```

```python
import functools

import jax
import jax.numpy as jnp
from jax import lax
from jax.experimental import pallas as pl
from jax.experimental.pallas import tpu as pltpu
from jax.sharding import PartitionSpec as P

STEPS = 3
NS_ITERS = 5
COURANT = 0.3
HALO = 2 * STEPS
LANES = 128
ROW_BLOCK = 4
VMEM = 40 * 1024 * 1024
ALL_VMEM = 60 * 1024 * 1024
HIGHEST = lax.Precision.HIGHEST


def dot(a, b, dims=((1,), (0,))):
    return lax.dot_general(a, b, (dims, ((), ())), precision=HIGHEST, preferred_element_type=jnp.float32)


def halves(a):
    high = a.astype(jnp.bfloat16)
    return high, (a - high.astype(jnp.float32)).astype(jnp.bfloat16)


def dot3(a, b, dims=((1,), (0,))):
    def one(x, y):
        return lax.dot_general(x, y, (dims, ((), ())), preferred_element_type=jnp.float32)

    (a_high, a_low), (b_high, b_low) = a, b
    return one(a_high, b_high) + (one(a_high, b_low) + one(a_low, b_high))


def picked(a, picks):
    high, low = halves(a)
    rest = (a - high.astype(jnp.float32) - low.astype(jnp.float32)).astype(jnp.bfloat16)
    parts = [jnp.dot(x, picks, preferred_element_type=jnp.float32) for x in (high, low, rest)]
    return parts[0] + (parts[1] + parts[2])


def cost(flops, bytes_accessed):
    return pl.CostEstimate(flops=flops, bytes_accessed=bytes_accessed, transcendentals=0)


def edges_kernel(state_ref, depth_ref, first_ref, second_ref, top_ref, bottom_ref, depth_top_ref, depth_bottom_ref, sems):
    members, fields, block, cols = top_ref.shape
    rows = depth_ref.shape[0]
    even = lax.axis_index("space") % 2 == 0
    sides = (
        (bottom_ref, depth_bottom_ref, rows - block, True),
        (top_ref, depth_top_ref, 0, False),
    )
    copies = []
    for side, (field_ref, edge_ref, start, _) in enumerate(sides):
        copies.append([
            pltpu.make_async_copy(state_ref.at[m, :, pl.ds(start, block), :], field_ref.at[m], sems.at[side, m])
            for m in range(members)
        ] + [pltpu.make_async_copy(depth_ref.at[pl.ds(start, block), :], edge_ref, sems.at[side, members])])
        for copy in copies[-1]:
            copy.start()

    def write(out_ref, field_ref, edge_ref, last):
        for c in range(cols // LANES):
            lanes = slice(c * LANES, (c + 1) * LANES)
            at = 0
            for k in range(fields):
                count = HALO if k == 2 else HALO - 1
                first = block - count if last else 0
                for m in range(members):
                    out_ref[c, pl.ds(at + m, count, stride=members), :] = field_ref[m, k, first:first + count, lanes]
                at += count * members
            first = block - HALO + 1 if last else 0
            out_ref[c, at:at + HALO - 1, :] = edge_ref[first:first + HALO - 1, lanes]

    for (field_ref, edge_ref, _, last), waits in zip(sides, copies):
        for copy in waits:
            copy.wait()
        for out_ref, here in ((first_ref, even), (second_ref, jnp.logical_not(even))):
            @pl.when(here if last else jnp.logical_not(here))
            def _():
                write(out_ref, field_ref, edge_ref, last)


def edges(state, depth):
    members, fields, rows, cols = state.shape
    block = 8
    shape = jax.ShapeDtypeStruct((cols // LANES, (3 * HALO - 2) * members + 8, LANES), jnp.float32)
    return pl.pallas_call(
        edges_kernel,
        in_specs=[pl.BlockSpec(memory_space=pl.ANY)] * 2,
        out_shape=[shape] * 2,
        scratch_shapes=[
            pltpu.VMEM((members, fields, block, cols), jnp.float32),
            pltpu.VMEM((members, fields, block, cols), jnp.float32),
            pltpu.VMEM((block, cols), jnp.float32),
            pltpu.VMEM((block, cols), jnp.float32),
            pltpu.SemaphoreType.DMA((2, members + 1)),
        ],
        compiler_params=pltpu.CompilerParams(vmem_limit_bytes=ALL_VMEM),
        cost_estimate=cost(0, 2 * state.size),
        name="edges",
    )(state, depth)


def forecast_kernel(bands, state_ref, first_ref, second_ref, depth_ref, height_ref, wind_ref, field_ref, pull_ref):
    members, fields, rows, cols = state_ref.shape
    chunks = cols // LANES
    band = lax.axis_index("space")
    lane = lax.broadcasted_iota(jnp.int32, (1, LANES), 1)

    even = band % 2 == 0

    def above(c, first, last):
        return jnp.where(even, second_ref[c, first:last, :], first_ref[c, first:last, :])

    def below(c, first, last):
        return jnp.where(even, first_ref[c, first:last, :], second_ref[c, first:last, :])

    for c in range(chunks):
        lanes = slice(c * LANES, (c + 1) * LANES)
        at = 0
        for k in range(fields):
            count = HALO if k == 2 else HALO - 1
            size = count * members
            field_ref[k, c, (HALO - count) * members:HALO * members, :] = above(c, at, at + size)
            field_ref[k, c, (HALO + rows) * members:(HALO + rows + count) * members, :] = below(c, at, at + size)
            at += size
            for m in range(members):
                field_ref[k, c, pl.ds(HALO * members + m, rows, stride=members), :] = state_ref[m, k, :, lanes]
        pull_above = COURANT * above(c, at, at + HALO - 1)
        pull_here = COURANT * depth_ref[:, lanes]
        pull_below = COURANT * below(c, at, at + HALO - 1)
        for m in range(members):
            pull_ref[c, pl.ds(members + m, HALO - 1, stride=members), :] = pull_above
            pull_ref[c, pl.ds(HALO * members + m, rows, stride=members), :] = pull_here
            pull_ref[c, pl.ds((HALO + rows) * members + m, HALO - 1, stride=members), :] = pull_below

    def cols_diff(parts):
        left = [pltpu.roll(p, 1, 1) for p in parts]
        right = [pltpu.roll(p, LANES - 1, 1) for p in parts]
        return [
            jnp.where(lane == LANES - 1, right[(c + 1) % chunks], right[c]) - jnp.where(lane == 0, left[c - 1], left[c])
            for c in range(chunks)
        ]

    def take(k, first, count):
        return [field_ref[k, c, first * members:(first + count) * members, :] for c in range(chunks)]

    def push_of(first, count):
        if first >= HALO and first + count <= HALO + rows:
            return COURANT
        row = lax.broadcasted_iota(jnp.int32, (count * members, LANES), 0) + (first + band * rows - HALO) * members
        return jnp.where(jnp.logical_and(row >= 0, row < bands * rows * members), COURANT, 0.0)

    def blocks(first, last):
        cuts = sorted({HALO, HALO + rows} | set(range(HALO, HALO + rows, ROW_BLOCK)))
        ends = [first] + [e for e in cuts if first < e < last] + [last]
        return [(lo, hi - lo) for lo, hi in zip(ends[:-1], ends[1:])]

    for step in range(STEPS):
        reach = 2 * (STEPS - 1 - step)
        for first, count in blocks(HALO - reach - 1, HALO + rows + reach + 1):
            height = take(0, first, count)
            slope = cols_diff(take(1, first, count))
            north = take(2, first + 1, count)
            south = take(2, first - 1, count)
            span = slice(first * members, (first + count) * members)
            for c in range(chunks):
                field_ref[0, c, span, :] = height[c] - pull_ref[c, span, :] * (slope[c] + (north[c] - south[c]))
        for first, count in blocks(HALO - reach, HALO + rows + reach):
            slope = cols_diff(take(0, first, count))
            zonal = take(1, first, count)
            meridional = take(2, first, count)
            north = take(0, first + 1, count)
            south = take(0, first - 1, count)
            push = push_of(first, count)
            span = slice(first * members, (first + count) * members)
            for c in range(chunks):
                zonal[c] = zonal[c] - COURANT * slope[c]
                meridional[c] = meridional[c] - push * (north[c] - south[c])
                if step < STEPS - 1:
                    field_ref[1, c, span, :] = zonal[c]
                    field_ref[2, c, span, :] = meridional[c]
            if step == STEPS - 1:
                here = take(0, first, count)
                for k, parts in enumerate((here, zonal, meridional)):
                    for c in range(chunks):
                        for t in range(count):
                            out_ref, start = (height_ref, 0) if k == 0 else (wind_ref, (k - 1) * cols)
                            lanes = slice(start + c * LANES, start + (c + 1) * LANES)
                            out_ref[first - HALO + t, :, lanes] = parts[c][t * members:(t + 1) * members]


def forecast(state, first, second, depth, bands):
    members, fields, rows, cols = state.shape
    total = rows + 2 * HALO
    return pl.pallas_call(
        functools.partial(forecast_kernel, bands),
        out_shape=[
            jax.ShapeDtypeStruct((rows, members, cols), jnp.float32),
            jax.ShapeDtypeStruct((rows, members, 2 * cols), jnp.float32),
        ],
        scratch_shapes=[
            pltpu.VMEM((fields, cols // LANES, total * members, LANES), jnp.float32),
            pltpu.VMEM((cols // LANES, total * members, LANES), jnp.float32),
        ],
        compiler_params=pltpu.CompilerParams(vmem_limit_bytes=VMEM),
        cost_estimate=cost(STEPS * 12 * state.size, 8 * state.size),
        name="forecast",
    )(state, first, second, depth)


TAIL = 8


def corners(size):
    i = lax.broadcasted_iota(jnp.int32, (size, size), 0)
    j = lax.broadcasted_iota(jnp.int32, (size, size), 1)
    return i < j, i == j


def gram_kernel(height_ref, cell_ref, value_ref, var_ref, keep_ref, send_ref, whole_ref):
    count, cols = height_ref.shape
    number, half, share = cell_ref.shape[1], count // 2, keep_ref.shape[0]
    picks = lax.broadcasted_iota(jnp.int32, (cols, number), 0) == cell_ref[...]
    seen = picked(height_ref[...], jnp.where(picks, 1.0, 0.0).astype(jnp.bfloat16))
    centre = jnp.sum(seen, axis=0, keepdims=True) / count
    observed = seen - centre
    innovation = value_ref[...] - centre
    weighted = observed / var_ref[...]
    gram = dot(weighted, observed, ((1,), (1,)))
    projection = jnp.sum(weighted * innovation, axis=1, keepdims=True)
    above, diagonal = corners(half)
    last = gram[half:, half:]
    both = jnp.concatenate([jnp.where(jnp.logical_or(above, diagonal), gram[:half, :half], last), gram[:half, half:]], axis=1)
    tails = (
        jnp.sum(jnp.where(corners(count)[1], projection, 0.0), axis=0, keepdims=True),
        jnp.concatenate([jnp.sum(jnp.where(diagonal, last, 0.0), axis=0, keepdims=True), jnp.zeros((1, half), jnp.float32)], axis=1),
    )
    for side, tail in enumerate(tails):
        first, rows = side * share, share - TAIL
        whole_ref[first:first + rows, :] = both[side * rows:(side + 1) * rows]
        whole_ref[first + rows:first + share, :] = jnp.broadcast_to(tail, (TAIL, count))
    core = lax.axis_index("member") % 2
    keep_ref[...] = whole_ref[pl.ds(pl.multiple_of(core * share, TAIL), share), :]
    send_ref[...] = whole_ref[pl.ds(pl.multiple_of((1 - core) * share, TAIL), share), :]


def gram_of(height, cell, value, var):
    count, cols = height.shape
    return pl.pallas_call(
        gram_kernel,
        out_shape=[jax.ShapeDtypeStruct((count // 4 + TAIL, count), jnp.float32)] * 2,
        scratch_shapes=[pltpu.VMEM((count // 2 + 2 * TAIL, count), jnp.float32)],
        compiler_params=pltpu.CompilerParams(vmem_limit_bytes=VMEM),
        cost_estimate=cost(6 * 2 * count * cols * cell.shape[1], 4 * count * cols),
        name="gram",
    )(height, cell, value, var)


def transform_kernel(keep_ref, got_ref, weights_ref, packed_ref):
    share, count = keep_ref.shape
    half, rows = count // 2, share - TAIL
    core = lax.axis_index("member") % 2
    packed_ref[pl.ds(pl.multiple_of(core * share, TAIL), share), :] = keep_ref[...]
    packed_ref[pl.ds(pl.multiple_of((1 - core) * share, TAIL), share), :] = got_ref[...]
    both = jnp.concatenate([packed_ref[:rows, :], packed_ref[share:share + rows, :]], axis=0)
    above, diagonal = corners(half)
    corner, side = both[:, :half], both[:, half:]
    upper = jnp.where(above, corner, 0.0)
    lower = jnp.where(jnp.logical_or(above, diagonal), 0.0, corner)
    one = upper + upper.T + jnp.where(diagonal, corner, 0.0)
    two = lower + lower.T + jnp.where(diagonal, packed_ref[share + rows:share + rows + 1, :half], 0.0)
    gram = jnp.concatenate([jnp.concatenate([one, side], axis=1), jnp.concatenate([side.T, two], axis=1)], axis=0)
    projection = jnp.sum(jnp.where(corners(count)[1], packed_ref[rows:rows + 1, :], 0.0), axis=1, keepdims=True)
    i = lax.broadcasted_iota(jnp.int32, (count, count), 0)
    j = lax.broadcasted_iota(jnp.int32, (count, count), 1)
    identity = jnp.where(i == j, 1.0, 0.0)
    system = identity + gram / (count - 1)
    scale = jnp.sqrt(jnp.sum(jnp.sum(system * system, axis=1, keepdims=True), axis=0, keepdims=True))
    current = system / scale
    root_inv = identity
    for step in range(NS_ITERS):
        parts, inv_parts = halves(current), halves(root_inv)
        product = current if step == 0 else dot3(inv_parts, parts)
        factor = 1.5 * identity - 0.5 * product
        factor_parts = halves(factor)
        if step < NS_ITERS - 1:
            current = dot3(parts, factor_parts)
        root_inv = factor if step == 0 else dot3(factor_parts, inv_parts)
    root = root_inv / jnp.sqrt(scale)

    def times(column):
        return jnp.sum(root * jnp.sum(jnp.where(i == j, column, 0.0), axis=0, keepdims=True), axis=1, keepdims=True)

    weights_ref[...] = times(times(projection)) / (count - 1) + root


def transform(keep, got):
    share, count = keep.shape
    return pl.pallas_call(
        transform_kernel,
        out_shape=jax.ShapeDtypeStruct((count, count), jnp.float32),
        scratch_shapes=[pltpu.VMEM((2 * share, count), jnp.float32)],
        compiler_params=pltpu.CompilerParams(vmem_limit_bytes=VMEM),
        cost_estimate=cost(6 * 2 * 14 * count ** 3, 8 * count ** 2),
        name="transform",
    )(keep, got)


def mix_kernel(weights_ref, height_ref, wind_ref, out_ref):
    weights = halves(weights_ref[...])
    count, cols = height_ref.shape
    for first in range(0, 3 * cols, cols):
        values = height_ref[...] if first == 0 else wind_ref[:, first - cols:first]
        centre = jnp.sum(values, axis=0, keepdims=True) / count
        out_ref[:, first:first + cols] = centre + dot3(weights, halves(values - centre), ((0,), (0,)))


def mix(weights, height, wind):
    count, cols = height.shape
    return pl.pallas_call(
        mix_kernel,
        out_shape=jax.ShapeDtypeStruct((count, 3 * cols), jnp.float32),
        compiler_params=pltpu.CompilerParams(vmem_limit_bytes=VMEM),
        cost_estimate=cost(3 * 2 * count * count * 3 * cols, 4 * count * 6 * cols),
        name="mix",
    )(weights, height, wind)


def unfold_kernel(rows_ref, out_ref, lanes_ref, whole_ref, sems):
    members, fields, rows, cols = whole_ref.shape
    chunks = cols // LANES
    copies = []
    for k in range(fields):
        for c in range(k * chunks, (k + 1) * chunks):
            lanes_ref[c] = rows_ref[:, c * LANES:(c + 1) * LANES]
        for m in range(members):
            for c in range(chunks):
                whole_ref[m, k, :, c * LANES:(c + 1) * LANES] = lanes_ref[k * chunks + c, pl.ds(m, rows, stride=members), :]
        copies.append(pltpu.make_async_copy(whole_ref.at[:, k], out_ref.at[:, k], sems.at[k]))
        copies[-1].start()
    for copy in copies:
        copy.wait()


def unfold(rows, shape):
    return pl.pallas_call(
        unfold_kernel,
        out_shape=jax.ShapeDtypeStruct(shape, jnp.float32),
        out_specs=pl.BlockSpec(memory_space=pl.ANY),
        scratch_shapes=[
            pltpu.VMEM((rows.shape[1] // LANES, rows.shape[0], LANES), jnp.float32),
            pltpu.VMEM(shape, jnp.float32),
            pltpu.SemaphoreType.DMA((shape[1],)),
        ],
        compiler_params=pltpu.CompilerParams(vmem_limit_bytes=VMEM),
        cost_estimate=cost(0, 8 * rows.size),
        name="unfold",
    )(rows)


def exchange(blocks, axis):
    return lax.all_to_all(blocks, axis, split_axis=0, concat_axis=0, tiled=True)


def shards(state, depth, obs_cell, obs_value, obs_var):
    bands, tiles = lax.axis_size("space"), lax.axis_size("member")
    members, rows, fields, cols = state.shape
    ensemble, chips = tiles * members, tiles // 2
    sibling = [(i, i ^ 1) for i in range(tiles)]

    state = state.transpose(0, 2, 1, 3)
    upper = [(i, i ^ 1) for i in range(bands)]
    lower = [pair for i in range(1, bands - 1, 2) for pair in ((i, i + 1), (i + 1, i))]

    first, second = edges(state, depth)
    first = lax.ppermute(first, "space", upper)
    second = lax.ppermute(second, "space", lower)
    height, wind = forecast(state, first, second, depth, bands)
    height = exchange(height, "member").reshape(ensemble, cols)
    height, wind = lax.optimization_barrier((height, wind))
    wind = exchange(wind, "member").reshape(ensemble, 2 * cols)

    keep, send = gram_of(height, obs_cell[0], obs_value[0], obs_var[0])
    half = keep + lax.ppermute(send, "member", sibling)

    def others(value, axis, unit):
        return [lax.ppermute(value, axis, [(i, i ^ (unit * k)) for i in range(lax.axis_size(axis))]) for k in (1, 2, 3)]

    for axis, unit in (("space", 1), ("member", tiles // 4)):
        one, two, three = others(half, axis, unit)
        half = (half + one) + (two + three)
    half = half + lax.ppermute(half, "space", [(i, i ^ 4) for i in range(bands)])
    half, wind = lax.optimization_barrier((half, wind))
    one, two, three = others(half, "member", 2)
    half = (half + one) + (two + three)
    weights = transform(half, lax.ppermute(half, "member", sibling))

    analysed = mix(weights, height, wind)
    back = exchange(analysed.reshape(tiles, members, fields * cols), "member").reshape(ensemble, fields * cols)
    return unfold(back, (members, fields, rows, cols)).transpose(0, 2, 1, 3)


def solution(mesh):
    placed = (
        P("member", "space", None, None),
        P("space", None),
        P("space", "member", None),
        P("space", "member", None),
        P("space", "member", None),
    )
    return jax.shard_map(
        shards,
        mesh=mesh,
        in_specs=placed,
        out_specs=P("member", "space", None, None),
        check_vma=False,
    )
```

```python
import functools

import jax
import jax.numpy as jnp
from jax import lax
from jax.experimental import pallas as pl
from jax.experimental.pallas import tpu as pltpu
from jax.sharding import PartitionSpec as P

STEPS = 3
NS_ITERS = 5
COURANT = 0.3
HALO = 2 * STEPS
LANES = 128
ROW_BLOCK = 4
VMEM = 40 * 1024 * 1024
ALL_VMEM = 60 * 1024 * 1024
HIGHEST = lax.Precision.HIGHEST


def dot(a, b, dims=((1,), (0,))):
    return lax.dot_general(a, b, (dims, ((), ())), precision=HIGHEST, preferred_element_type=jnp.float32)


def halves(a):
    high = a.astype(jnp.bfloat16)
    return high, (a - high.astype(jnp.float32)).astype(jnp.bfloat16)


def dot3(a, b, dims=((1,), (0,))):
    def one(x, y):
        return lax.dot_general(x, y, (dims, ((), ())), preferred_element_type=jnp.float32)

    (a_high, a_low), (b_high, b_low) = a, b
    return one(a_high, b_high) + (one(a_high, b_low) + one(a_low, b_high))


def picked(a, picks):
    high, low = halves(a)
    rest = (a - high.astype(jnp.float32) - low.astype(jnp.float32)).astype(jnp.bfloat16)
    parts = [jnp.dot(x, picks, preferred_element_type=jnp.float32) for x in (high, low, rest)]
    return parts[0] + (parts[1] + parts[2])


def cost(flops, bytes_accessed):
    return pl.CostEstimate(flops=flops, bytes_accessed=bytes_accessed, transcendentals=0)


def edges_kernel(state_ref, depth_ref, first_ref, second_ref, top_ref, bottom_ref, depth_top_ref, depth_bottom_ref, sems):
    members, fields, block, cols = top_ref.shape
    rows = depth_ref.shape[0]
    even = lax.axis_index("space") % 2 == 0
    sides = (
        (bottom_ref, depth_bottom_ref, rows - block, True),
        (top_ref, depth_top_ref, 0, False),
    )
    copies = []
    for side, (field_ref, edge_ref, start, _) in enumerate(sides):
        copies.append([
            pltpu.make_async_copy(state_ref.at[m, :, pl.ds(start, block), :], field_ref.at[m], sems.at[side, m])
            for m in range(members)
        ] + [pltpu.make_async_copy(depth_ref.at[pl.ds(start, block), :], edge_ref, sems.at[side, members])])
        for copy in copies[-1]:
            copy.start()

    def write(out_ref, field_ref, edge_ref, last):
        for c in range(cols // LANES):
            lanes = slice(c * LANES, (c + 1) * LANES)
            at = 0
            for k in range(fields):
                count = HALO if k == 2 else HALO - 1
                first = block - count if last else 0
                for m in range(members):
                    out_ref[c, pl.ds(at + m, count, stride=members), :] = field_ref[m, k, first:first + count, lanes]
                at += count * members
            first = block - HALO + 1 if last else 0
            out_ref[c, at:at + HALO - 1, :] = edge_ref[first:first + HALO - 1, lanes]

    for (field_ref, edge_ref, _, last), waits in zip(sides, copies):
        for copy in waits:
            copy.wait()
        for out_ref, here in ((first_ref, even), (second_ref, jnp.logical_not(even))):
            @pl.when(here if last else jnp.logical_not(here))
            def _():
                write(out_ref, field_ref, edge_ref, last)


def edges(state, depth):
    members, fields, rows, cols = state.shape
    block = 8
    shape = jax.ShapeDtypeStruct((cols // LANES, (3 * HALO - 2) * members + 8, LANES), jnp.float32)
    return pl.pallas_call(
        edges_kernel,
        in_specs=[pl.BlockSpec(memory_space=pl.ANY)] * 2,
        out_shape=[shape] * 2,
        scratch_shapes=[
            pltpu.VMEM((members, fields, block, cols), jnp.float32),
            pltpu.VMEM((members, fields, block, cols), jnp.float32),
            pltpu.VMEM((block, cols), jnp.float32),
            pltpu.VMEM((block, cols), jnp.float32),
            pltpu.SemaphoreType.DMA((2, members + 1)),
        ],
        compiler_params=pltpu.CompilerParams(vmem_limit_bytes=ALL_VMEM),
        cost_estimate=cost(0, 2 * state.size),
        name="edges",
    )(state, depth)


def forecast_kernel(bands, state_ref, first_ref, second_ref, depth_ref, height_ref, wind_ref, field_ref, pull_ref, made_ref, sems):
    members, fields, rows, cols = state_ref.shape
    chunks = cols // LANES
    band = lax.axis_index("space")
    lane = lax.broadcasted_iota(jnp.int32, (1, LANES), 1)

    even = band % 2 == 0

    def above(c, first, last):
        return jnp.where(even, second_ref[c, first:last, :], first_ref[c, first:last, :])

    def below(c, first, last):
        return jnp.where(even, first_ref[c, first:last, :], second_ref[c, first:last, :])

    for c in range(chunks):
        lanes = slice(c * LANES, (c + 1) * LANES)
        at = 0
        for k in range(fields):
            count = HALO if k == 2 else HALO - 1
            size = count * members
            field_ref[k, c, (HALO - count) * members:HALO * members, :] = above(c, at, at + size)
            field_ref[k, c, (HALO + rows) * members:(HALO + rows + count) * members, :] = below(c, at, at + size)
            at += size
            for m in range(members):
                field_ref[k, c, pl.ds(HALO * members + m, rows, stride=members), :] = state_ref[m, k, :, lanes]
        pull_above = COURANT * above(c, at, at + HALO - 1)
        pull_here = COURANT * depth_ref[:, lanes]
        pull_below = COURANT * below(c, at, at + HALO - 1)
        for m in range(members):
            pull_ref[c, pl.ds(members + m, HALO - 1, stride=members), :] = pull_above
            pull_ref[c, pl.ds(HALO * members + m, rows, stride=members), :] = pull_here
            pull_ref[c, pl.ds((HALO + rows) * members + m, HALO - 1, stride=members), :] = pull_below

    def cols_diff(parts):
        left = [pltpu.roll(p, 1, 1) for p in parts]
        right = [pltpu.roll(p, LANES - 1, 1) for p in parts]
        return [
            jnp.where(lane == LANES - 1, right[(c + 1) % chunks], right[c]) - jnp.where(lane == 0, left[c - 1], left[c])
            for c in range(chunks)
        ]

    def take(k, first, count):
        return [field_ref[k, c, first * members:(first + count) * members, :] for c in range(chunks)]

    def push_of(first, count):
        if first >= HALO and first + count <= HALO + rows:
            return COURANT
        row = lax.broadcasted_iota(jnp.int32, (count * members, LANES), 0) + (first + band * rows - HALO) * members
        return jnp.where(jnp.logical_and(row >= 0, row < bands * rows * members), COURANT, 0.0)

    def blocks(first, last):
        cuts = sorted({HALO, HALO + rows} | set(range(HALO, HALO + rows, ROW_BLOCK)))
        ends = [first] + [e for e in cuts if first < e < last] + [last]
        return [(lo, hi - lo) for lo, hi in zip(ends[:-1], ends[1:])]

    copies = []
    for step in range(STEPS):
        reach = 2 * (STEPS - 1 - step)
        for first, count in blocks(HALO - reach - 1, HALO + rows + reach + 1):
            height = take(0, first, count)
            slope = cols_diff(take(1, first, count))
            north = take(2, first + 1, count)
            south = take(2, first - 1, count)
            span = slice(first * members, (first + count) * members)
            for c in range(chunks):
                field_ref[0, c, span, :] = height[c] - pull_ref[c, span, :] * (slope[c] + (north[c] - south[c]))
        for first, count in blocks(HALO - reach, HALO + rows + reach):
            slope = cols_diff(take(0, first, count))
            zonal = take(1, first, count)
            meridional = take(2, first, count)
            north = take(0, first + 1, count)
            south = take(0, first - 1, count)
            push = push_of(first, count)
            span = slice(first * members, (first + count) * members)
            for c in range(chunks):
                zonal[c] = zonal[c] - COURANT * slope[c]
                meridional[c] = meridional[c] - push * (north[c] - south[c])
                if step < STEPS - 1:
                    field_ref[1, c, span, :] = zonal[c]
                    field_ref[2, c, span, :] = meridional[c]
            if step == STEPS - 1:
                here = take(0, first, count)
                for k, parts in enumerate((here, zonal, meridional)):
                    for c in range(chunks):
                        for t in range(count):
                            out_ref, start = (height_ref, 0) if k == 0 else (made_ref, (k - 1) * cols)
                            lanes = slice(start + c * LANES, start + (c + 1) * LANES)
                            out_ref[first - HALO + t, :, lanes] = parts[c][t * members:(t + 1) * members]
                leaving = pl.ds(first - HALO, count)
                copies.append(pltpu.make_async_copy(made_ref.at[leaving], wind_ref.at[leaving], sems.at[len(copies)]))
                copies[-1].start()
    for copy in copies:
        copy.wait()


def forecast(state, first, second, depth, bands):
    members, fields, rows, cols = state.shape
    total = rows + 2 * HALO
    return pl.pallas_call(
        functools.partial(forecast_kernel, bands),
        out_shape=[
            jax.ShapeDtypeStruct((rows, members, cols), jnp.float32),
            jax.ShapeDtypeStruct((rows, members, 2 * cols), jnp.float32),
        ],
        scratch_shapes=[
            pltpu.VMEM((fields, cols // LANES, total * members, LANES), jnp.float32),
            pltpu.VMEM((cols // LANES, total * members, LANES), jnp.float32),
            pltpu.VMEM((rows, members, 2 * cols), jnp.float32),
            pltpu.SemaphoreType.DMA((rows // ROW_BLOCK,)),
        ],
        out_specs=[pl.BlockSpec(memory_space=pltpu.VMEM), pl.BlockSpec(memory_space=pl.ANY)],
        compiler_params=pltpu.CompilerParams(vmem_limit_bytes=VMEM),
        cost_estimate=cost(STEPS * 12 * state.size, 8 * state.size),
        name="forecast",
    )(state, first, second, depth)


TAIL = 8


def corners(size):
    i = lax.broadcasted_iota(jnp.int32, (size, size), 0)
    j = lax.broadcasted_iota(jnp.int32, (size, size), 1)
    return i < j, i == j


def gram_kernel(height_ref, cell_ref, value_ref, var_ref, keep_ref, send_ref, whole_ref):
    count, cols = height_ref.shape
    number, half, share = cell_ref.shape[1], count // 2, keep_ref.shape[0]
    picks = lax.broadcasted_iota(jnp.int32, (cols, number), 0) == cell_ref[...]
    seen = picked(height_ref[...], jnp.where(picks, 1.0, 0.0).astype(jnp.bfloat16))
    centre = jnp.sum(seen, axis=0, keepdims=True) / count
    observed = seen - centre
    innovation = value_ref[...] - centre
    weighted = observed / var_ref[...]
    gram = dot(weighted, observed, ((1,), (1,)))
    projection = jnp.sum(weighted * innovation, axis=1, keepdims=True)
    above, diagonal = corners(half)
    last = gram[half:, half:]
    both = jnp.concatenate([jnp.where(jnp.logical_or(above, diagonal), gram[:half, :half], last), gram[:half, half:]], axis=1)
    tails = (
        jnp.sum(jnp.where(corners(count)[1], projection, 0.0), axis=0, keepdims=True),
        jnp.concatenate([jnp.sum(jnp.where(diagonal, last, 0.0), axis=0, keepdims=True), jnp.zeros((1, half), jnp.float32)], axis=1),
    )
    for side, tail in enumerate(tails):
        first, rows = side * share, share - TAIL
        whole_ref[first:first + rows, :] = both[side * rows:(side + 1) * rows]
        whole_ref[first + rows:first + share, :] = jnp.broadcast_to(tail, (TAIL, count))
    core = lax.axis_index("member") % 2
    keep_ref[...] = whole_ref[pl.ds(pl.multiple_of(core * share, TAIL), share), :]
    send_ref[...] = whole_ref[pl.ds(pl.multiple_of((1 - core) * share, TAIL), share), :]


def gram_of(height, cell, value, var):
    count, cols = height.shape
    return pl.pallas_call(
        gram_kernel,
        out_shape=[jax.ShapeDtypeStruct((count // 4 + TAIL, count), jnp.float32)] * 2,
        scratch_shapes=[pltpu.VMEM((count // 2 + 2 * TAIL, count), jnp.float32)],
        compiler_params=pltpu.CompilerParams(vmem_limit_bytes=VMEM),
        cost_estimate=cost(6 * 2 * count * cols * cell.shape[1], 4 * count * cols),
        name="gram",
    )(height, cell, value, var)


def transform_kernel(keep_ref, got_ref, weights_ref, packed_ref):
    share, count = keep_ref.shape
    half, rows = count // 2, share - TAIL
    core = lax.axis_index("member") % 2
    packed_ref[pl.ds(pl.multiple_of(core * share, TAIL), share), :] = keep_ref[...]
    packed_ref[pl.ds(pl.multiple_of((1 - core) * share, TAIL), share), :] = got_ref[...]
    both = jnp.concatenate([packed_ref[:rows, :], packed_ref[share:share + rows, :]], axis=0)
    above, diagonal = corners(half)
    corner, side = both[:, :half], both[:, half:]
    upper = jnp.where(above, corner, 0.0)
    lower = jnp.where(jnp.logical_or(above, diagonal), 0.0, corner)
    one = upper + upper.T + jnp.where(diagonal, corner, 0.0)
    two = lower + lower.T + jnp.where(diagonal, packed_ref[share + rows:share + rows + 1, :half], 0.0)
    gram = jnp.concatenate([jnp.concatenate([one, side], axis=1), jnp.concatenate([side.T, two], axis=1)], axis=0)
    projection = jnp.sum(jnp.where(corners(count)[1], packed_ref[rows:rows + 1, :], 0.0), axis=1, keepdims=True)
    i = lax.broadcasted_iota(jnp.int32, (count, count), 0)
    j = lax.broadcasted_iota(jnp.int32, (count, count), 1)
    identity = jnp.where(i == j, 1.0, 0.0)
    system = identity + gram / (count - 1)
    scale = jnp.sqrt(jnp.sum(jnp.sum(system * system, axis=1, keepdims=True), axis=0, keepdims=True))
    current = system / scale
    root_inv = identity
    for step in range(NS_ITERS):
        parts, inv_parts = halves(current), halves(root_inv)
        product = current if step == 0 else dot3(inv_parts, parts)
        factor = 1.5 * identity - 0.5 * product
        factor_parts = halves(factor)
        if step < NS_ITERS - 1:
            current = dot3(parts, factor_parts)
        root_inv = factor if step == 0 else dot3(factor_parts, inv_parts)
    root = root_inv / jnp.sqrt(scale)

    def times(column):
        return jnp.sum(root * jnp.sum(jnp.where(i == j, column, 0.0), axis=0, keepdims=True), axis=1, keepdims=True)

    weights_ref[...] = times(times(projection)) / (count - 1) + root


def transform(keep, got):
    share, count = keep.shape
    return pl.pallas_call(
        transform_kernel,
        out_shape=jax.ShapeDtypeStruct((count, count), jnp.float32),
        scratch_shapes=[pltpu.VMEM((2 * share, count), jnp.float32)],
        compiler_params=pltpu.CompilerParams(vmem_limit_bytes=VMEM),
        cost_estimate=cost(6 * 2 * 14 * count ** 3, 8 * count ** 2),
        name="transform",
    )(keep, got)


def mix_kernel(weights_ref, height_ref, wind_ref, out_ref):
    weights = halves(weights_ref[...])
    count, cols = height_ref.shape
    for first in range(0, 3 * cols, cols):
        values = height_ref[...] if first == 0 else wind_ref[:, first - cols:first]
        centre = jnp.sum(values, axis=0, keepdims=True) / count
        out_ref[:, first:first + cols] = centre + dot3(weights, halves(values - centre), ((0,), (0,)))


def mix(weights, height, wind):
    count, cols = height.shape
    return pl.pallas_call(
        mix_kernel,
        out_shape=jax.ShapeDtypeStruct((count, 3 * cols), jnp.float32),
        compiler_params=pltpu.CompilerParams(vmem_limit_bytes=VMEM),
        cost_estimate=cost(3 * 2 * count * count * 3 * cols, 4 * count * 6 * cols),
        name="mix",
    )(weights, height, wind)


def unfold_kernel(rows_ref, out_ref, lanes_ref, whole_ref, sems):
    members, fields, rows, cols = whole_ref.shape
    chunks = cols // LANES
    copies = []
    for k in range(fields):
        for c in range(k * chunks, (k + 1) * chunks):
            lanes_ref[c] = rows_ref[:, c * LANES:(c + 1) * LANES]
        for m in range(members):
            for c in range(chunks):
                whole_ref[m, k, :, c * LANES:(c + 1) * LANES] = lanes_ref[k * chunks + c, pl.ds(m, rows, stride=members), :]
        copies.append(pltpu.make_async_copy(whole_ref.at[:, k], out_ref.at[:, k], sems.at[k]))
        copies[-1].start()
    for copy in copies:
        copy.wait()


def unfold(rows, shape):
    return pl.pallas_call(
        unfold_kernel,
        out_shape=jax.ShapeDtypeStruct(shape, jnp.float32),
        out_specs=pl.BlockSpec(memory_space=pl.ANY),
        scratch_shapes=[
            pltpu.VMEM((rows.shape[1] // LANES, rows.shape[0], LANES), jnp.float32),
            pltpu.VMEM(shape, jnp.float32),
            pltpu.SemaphoreType.DMA((shape[1],)),
        ],
        compiler_params=pltpu.CompilerParams(vmem_limit_bytes=VMEM),
        cost_estimate=cost(0, 8 * rows.size),
        name="unfold",
    )(rows)


def exchange(blocks, axis):
    return lax.all_to_all(blocks, axis, split_axis=0, concat_axis=0, tiled=True)


def shards(state, depth, obs_cell, obs_value, obs_var):
    bands, tiles = lax.axis_size("space"), lax.axis_size("member")
    members, rows, fields, cols = state.shape
    ensemble, chips = tiles * members, tiles // 2
    sibling = [(i, i ^ 1) for i in range(tiles)]

    state = state.transpose(0, 2, 1, 3)
    upper = [(i, i ^ 1) for i in range(bands)]
    lower = [pair for i in range(1, bands - 1, 2) for pair in ((i, i + 1), (i + 1, i))]

    first, second = edges(state, depth)
    first = lax.ppermute(first, "space", upper)
    second = lax.ppermute(second, "space", lower)
    height, wind = forecast(state, first, second, depth, bands)
    height = exchange(height, "member").reshape(ensemble, cols)
    height, wind = lax.optimization_barrier((height, wind))
    wind = exchange(wind, "member").reshape(ensemble, 2 * cols)

    keep, send = gram_of(height, obs_cell[0], obs_value[0], obs_var[0])
    half = keep + lax.ppermute(send, "member", sibling)

    def others(value, axis, unit):
        return [lax.ppermute(value, axis, [(i, i ^ (unit * k)) for i in range(lax.axis_size(axis))]) for k in (1, 2, 3)]

    for axis, unit in (("space", 1), ("member", tiles // 4)):
        one, two, three = others(half, axis, unit)
        half = (half + one) + (two + three)
    one, two, three = others(half, "member", 2)
    half = (half + one) + (two + three)
    half, wind = lax.optimization_barrier((half, wind))
    half = half + lax.ppermute(half, "space", [(i, i ^ 4) for i in range(bands)])
    weights = transform(half, lax.ppermute(half, "member", sibling))

    analysed = mix(weights, height, wind)
    back = exchange(analysed.reshape(tiles, members, fields * cols), "member").reshape(ensemble, fields * cols)
    return unfold(back, (members, fields, rows, cols)).transpose(0, 2, 1, 3)


def solution(mesh):
    placed = (
        P("member", "space", None, None),
        P("space", None),
        P("space", "member", None),
        P("space", "member", None),
        P("space", "member", None),
    )
    return jax.shard_map(
        shards,
        mesh=mesh,
        in_specs=placed,
        out_specs=P("member", "space", None, None),
        check_vma=False,
    )
```

```python
import functools

import jax
import jax.numpy as jnp
from jax import lax
from jax.experimental import pallas as pl
from jax.experimental.pallas import tpu as pltpu
from jax.sharding import PartitionSpec as P

STEPS = 3
NS_ITERS = 5
COURANT = 0.3
HALO = 2 * STEPS
LANES = 128
ROW_BLOCK = 4
VMEM = 40 * 1024 * 1024
ALL_VMEM = 60 * 1024 * 1024
HIGHEST = lax.Precision.HIGHEST


def dot(a, b, dims=((1,), (0,))):
    return lax.dot_general(a, b, (dims, ((), ())), precision=HIGHEST, preferred_element_type=jnp.float32)


def halves(a):
    high = a.astype(jnp.bfloat16)
    return high, (a - high.astype(jnp.float32)).astype(jnp.bfloat16)


def dot3(a, b, dims=((1,), (0,))):
    def one(x, y):
        return lax.dot_general(x, y, (dims, ((), ())), preferred_element_type=jnp.float32)

    (a_high, a_low), (b_high, b_low) = a, b
    return one(a_high, b_high) + (one(a_high, b_low) + one(a_low, b_high))


def picked(a, picks):
    high, low = halves(a)
    rest = (a - high.astype(jnp.float32) - low.astype(jnp.float32)).astype(jnp.bfloat16)
    parts = [jnp.dot(x, picks, preferred_element_type=jnp.float32) for x in (high, low, rest)]
    return parts[0] + (parts[1] + parts[2])


def cost(flops, bytes_accessed):
    return pl.CostEstimate(flops=flops, bytes_accessed=bytes_accessed, transcendentals=0)


def edges_kernel(state_ref, depth_ref, first_ref, second_ref, top_ref, bottom_ref, depth_top_ref, depth_bottom_ref, sems):
    members, fields, block, cols = top_ref.shape
    rows = depth_ref.shape[0]
    even = lax.axis_index("space") % 2 == 0
    sides = (
        (bottom_ref, depth_bottom_ref, rows - block, True),
        (top_ref, depth_top_ref, 0, False),
    )
    copies = []
    for side, (field_ref, edge_ref, start, _) in enumerate(sides):
        copies.append([
            pltpu.make_async_copy(state_ref.at[m, :, pl.ds(start, block), :], field_ref.at[m], sems.at[side, m])
            for m in range(members)
        ] + [pltpu.make_async_copy(depth_ref.at[pl.ds(start, block), :], edge_ref, sems.at[side, members])])
        for copy in copies[-1]:
            copy.start()

    def write(out_ref, field_ref, edge_ref, last):
        for c in range(cols // LANES):
            lanes = slice(c * LANES, (c + 1) * LANES)
            at = 0
            for k in range(fields):
                count = HALO if k == 2 else HALO - 1
                first = block - count if last else 0
                for m in range(members):
                    out_ref[c, pl.ds(at + m, count, stride=members), :] = field_ref[m, k, first:first + count, lanes]
                at += count * members
            first = block - HALO + 1 if last else 0
            out_ref[c, at:at + HALO - 1, :] = edge_ref[first:first + HALO - 1, lanes]

    for (field_ref, edge_ref, _, last), waits in zip(sides, copies):
        for copy in waits:
            copy.wait()
        for out_ref, here in ((first_ref, even), (second_ref, jnp.logical_not(even))):
            @pl.when(here if last else jnp.logical_not(here))
            def _():
                write(out_ref, field_ref, edge_ref, last)


def edges(state, depth):
    members, fields, rows, cols = state.shape
    block = 8
    shape = jax.ShapeDtypeStruct((cols // LANES, (3 * HALO - 2) * members + 8, LANES), jnp.float32)
    return pl.pallas_call(
        edges_kernel,
        in_specs=[pl.BlockSpec(memory_space=pl.ANY)] * 2,
        out_shape=[shape] * 2,
        scratch_shapes=[
            pltpu.VMEM((members, fields, block, cols), jnp.float32),
            pltpu.VMEM((members, fields, block, cols), jnp.float32),
            pltpu.VMEM((block, cols), jnp.float32),
            pltpu.VMEM((block, cols), jnp.float32),
            pltpu.SemaphoreType.DMA((2, members + 1)),
        ],
        compiler_params=pltpu.CompilerParams(vmem_limit_bytes=ALL_VMEM),
        cost_estimate=cost(0, 2 * state.size),
        name="edges",
    )(state, depth)


def forecast_kernel(bands, state_ref, first_ref, second_ref, depth_ref, height_ref, wind_ref, field_ref, pull_ref, made_ref, sems):
    members, fields, rows, cols = state_ref.shape
    chunks = cols // LANES
    band = lax.axis_index("space")
    lane = lax.broadcasted_iota(jnp.int32, (1, LANES), 1)

    even = band % 2 == 0

    def above(c, first, last):
        return jnp.where(even, second_ref[c, first:last, :], first_ref[c, first:last, :])

    def below(c, first, last):
        return jnp.where(even, first_ref[c, first:last, :], second_ref[c, first:last, :])

    for c in range(chunks):
        lanes = slice(c * LANES, (c + 1) * LANES)
        at = 0
        for k in range(fields):
            count = HALO if k == 2 else HALO - 1
            size = count * members
            field_ref[k, c, (HALO - count) * members:HALO * members, :] = above(c, at, at + size)
            field_ref[k, c, (HALO + rows) * members:(HALO + rows + count) * members, :] = below(c, at, at + size)
            at += size
            for m in range(members):
                field_ref[k, c, pl.ds(HALO * members + m, rows, stride=members), :] = state_ref[m, k, :, lanes]
        pull_above = COURANT * above(c, at, at + HALO - 1)
        pull_here = COURANT * depth_ref[:, lanes]
        pull_below = COURANT * below(c, at, at + HALO - 1)
        for m in range(members):
            pull_ref[c, pl.ds(members + m, HALO - 1, stride=members), :] = pull_above
            pull_ref[c, pl.ds(HALO * members + m, rows, stride=members), :] = pull_here
            pull_ref[c, pl.ds((HALO + rows) * members + m, HALO - 1, stride=members), :] = pull_below

    def cols_diff(parts):
        left = [pltpu.roll(p, 1, 1) for p in parts]
        right = [pltpu.roll(p, LANES - 1, 1) for p in parts]
        return [
            jnp.where(lane == LANES - 1, right[(c + 1) % chunks], right[c]) - jnp.where(lane == 0, left[c - 1], left[c])
            for c in range(chunks)
        ]

    def take(k, first, count):
        return [field_ref[k, c, first * members:(first + count) * members, :] for c in range(chunks)]

    def push_of(first, count):
        if first >= HALO and first + count <= HALO + rows:
            return COURANT
        row = lax.broadcasted_iota(jnp.int32, (count * members, LANES), 0) + (first + band * rows - HALO) * members
        return jnp.where(jnp.logical_and(row >= 0, row < bands * rows * members), COURANT, 0.0)

    def blocks(first, last):
        cuts = sorted({HALO, HALO + rows} | set(range(HALO, HALO + rows, ROW_BLOCK)))
        ends = [first] + [e for e in cuts if first < e < last] + [last]
        return [(lo, hi - lo) for lo, hi in zip(ends[:-1], ends[1:])]

    copies = []
    for step in range(STEPS):
        reach = 2 * (STEPS - 1 - step)
        for first, count in blocks(HALO - reach - 1, HALO + rows + reach + 1):
            height = take(0, first, count)
            slope = cols_diff(take(1, first, count))
            north = take(2, first + 1, count)
            south = take(2, first - 1, count)
            span = slice(first * members, (first + count) * members)
            for c in range(chunks):
                field_ref[0, c, span, :] = height[c] - pull_ref[c, span, :] * (slope[c] + (north[c] - south[c]))
        for first, count in blocks(HALO - reach, HALO + rows + reach):
            slope = cols_diff(take(0, first, count))
            zonal = take(1, first, count)
            meridional = take(2, first, count)
            north = take(0, first + 1, count)
            south = take(0, first - 1, count)
            push = push_of(first, count)
            span = slice(first * members, (first + count) * members)
            for c in range(chunks):
                zonal[c] = zonal[c] - COURANT * slope[c]
                meridional[c] = meridional[c] - push * (north[c] - south[c])
                if step < STEPS - 1:
                    field_ref[1, c, span, :] = zonal[c]
                    field_ref[2, c, span, :] = meridional[c]
            if step == STEPS - 1:
                here = take(0, first, count)
                for k, parts in enumerate((here, zonal, meridional)):
                    for c in range(chunks):
                        for t in range(count):
                            out_ref, start = (height_ref, 0) if k == 0 else (made_ref, (k - 1) * cols)
                            lanes = slice(start + c * LANES, start + (c + 1) * LANES)
                            out_ref[first - HALO + t, :, lanes] = parts[c][t * members:(t + 1) * members]
                leaving = pl.ds(first - HALO, count)
                copies.append(pltpu.make_async_copy(made_ref.at[leaving], wind_ref.at[leaving], sems.at[len(copies)]))
                copies[-1].start()
    for copy in copies:
        copy.wait()


def forecast(state, first, second, depth, bands):
    members, fields, rows, cols = state.shape
    total = rows + 2 * HALO
    return pl.pallas_call(
        functools.partial(forecast_kernel, bands),
        out_shape=[
            jax.ShapeDtypeStruct((rows, members, cols), jnp.float32),
            jax.ShapeDtypeStruct((rows, members, 2 * cols), jnp.float32),
        ],
        scratch_shapes=[
            pltpu.VMEM((fields, cols // LANES, total * members, LANES), jnp.float32),
            pltpu.VMEM((cols // LANES, total * members, LANES), jnp.float32),
            pltpu.VMEM((rows, members, 2 * cols), jnp.float32),
            pltpu.SemaphoreType.DMA((rows // ROW_BLOCK,)),
        ],
        out_specs=[pl.BlockSpec(memory_space=pltpu.VMEM), pl.BlockSpec(memory_space=pl.ANY)],
        compiler_params=pltpu.CompilerParams(vmem_limit_bytes=VMEM),
        cost_estimate=cost(STEPS * 12 * state.size, 8 * state.size),
        name="forecast",
    )(state, first, second, depth)


TAIL = 8


def corners(size):
    i = lax.broadcasted_iota(jnp.int32, (size, size), 0)
    j = lax.broadcasted_iota(jnp.int32, (size, size), 1)
    return i < j, i == j


def gram_kernel(height_ref, got_ref, cell_ref, value_ref, var_ref, keep_ref, send_ref, seen_ref, whole_ref):
    chips, cores, members, cols = height_ref.shape
    count = chips * cores * members
    number, half, share = cell_ref.shape[1], count // 2, keep_ref.shape[0]
    picks = lax.broadcasted_iota(jnp.int32, (cols, number), 0) == cell_ref[...]
    picks = jnp.where(picks, 1.0, 0.0).astype(jnp.bfloat16)
    core = lax.axis_index("member") % cores
    own = height_ref[:, pl.ds(core, 1)].reshape(half, cols)
    seen_ref[:, pl.ds(core, 1)] = picked(own, picks).reshape(chips, 1, members, number)
    seen_ref[:, pl.ds(1 - core, 1)] = picked(got_ref[...].reshape(half, cols), picks).reshape(chips, 1, members, number)
    seen = seen_ref[...].reshape(count, number)
    centre = jnp.sum(seen, axis=0, keepdims=True) / count
    observed = seen - centre
    innovation = value_ref[...] - centre
    weighted = observed / var_ref[...]
    gram = dot(weighted, observed, ((1,), (1,)))
    projection = jnp.sum(weighted * innovation, axis=1, keepdims=True)
    above, diagonal = corners(half)
    last = gram[half:, half:]
    both = jnp.concatenate([jnp.where(jnp.logical_or(above, diagonal), gram[:half, :half], last), gram[:half, half:]], axis=1)
    tails = (
        jnp.sum(jnp.where(corners(count)[1], projection, 0.0), axis=0, keepdims=True),
        jnp.concatenate([jnp.sum(jnp.where(diagonal, last, 0.0), axis=0, keepdims=True), jnp.zeros((1, half), jnp.float32)], axis=1),
    )
    for side, tail in enumerate(tails):
        first, rows = side * share, share - TAIL
        whole_ref[first:first + rows, :] = both[side * rows:(side + 1) * rows]
        whole_ref[first + rows:first + share, :] = jnp.broadcast_to(tail, (TAIL, count))
    keep_ref[...] = whole_ref[pl.ds(pl.multiple_of(core * share, TAIL), share), :]
    send_ref[...] = whole_ref[pl.ds(pl.multiple_of((1 - core) * share, TAIL), share), :]


def gram_of(height, got, cell, value, var):
    chips, cores, members, cols = height.shape
    count = chips * cores * members
    return pl.pallas_call(
        gram_kernel,
        out_shape=[jax.ShapeDtypeStruct((count // 4 + TAIL, count), jnp.float32)] * 2,
        scratch_shapes=[
            pltpu.VMEM((chips, cores, members, cell.shape[1]), jnp.float32),
            pltpu.VMEM((count // 2 + 2 * TAIL, count), jnp.float32),
        ],
        compiler_params=pltpu.CompilerParams(vmem_limit_bytes=VMEM),
        cost_estimate=cost(6 * 2 * count * cols * cell.shape[1], 4 * count * cols),
        name="gram",
    )(height, got, cell, value, var)


def pick_kernel(first, state_ref, out_ref):
    chips, members, width = out_ref.shape
    other = 1 - lax.axis_index("member") % 2
    out_ref[...] = state_ref[:, pl.ds(other, 1), :, first:first + width].reshape(out_ref.shape)


def pick(state, first, last):
    chips, cores, members, _ = state.shape
    shape = jax.ShapeDtypeStruct((chips, members, last - first), jnp.float32)
    return pl.pallas_call(
        functools.partial(pick_kernel, first),
        out_shape=shape,
        compiler_params=pltpu.CompilerParams(vmem_limit_bytes=VMEM),
        cost_estimate=cost(0, 8 * shape.size),
        name="pick",
    )(state)


def transform_kernel(keep_ref, got_ref, weights_ref, packed_ref):
    share, count = keep_ref.shape
    half, rows = count // 2, share - TAIL
    core = lax.axis_index("member") % 2
    packed_ref[pl.ds(pl.multiple_of(core * share, TAIL), share), :] = keep_ref[...]
    packed_ref[pl.ds(pl.multiple_of((1 - core) * share, TAIL), share), :] = got_ref[...]
    both = jnp.concatenate([packed_ref[:rows, :], packed_ref[share:share + rows, :]], axis=0)
    above, diagonal = corners(half)
    corner, side = both[:, :half], both[:, half:]
    upper = jnp.where(above, corner, 0.0)
    lower = jnp.where(jnp.logical_or(above, diagonal), 0.0, corner)
    one = upper + upper.T + jnp.where(diagonal, corner, 0.0)
    two = lower + lower.T + jnp.where(diagonal, packed_ref[share + rows:share + rows + 1, :half], 0.0)
    gram = jnp.concatenate([jnp.concatenate([one, side], axis=1), jnp.concatenate([side.T, two], axis=1)], axis=0)
    projection = jnp.sum(jnp.where(corners(count)[1], packed_ref[rows:rows + 1, :], 0.0), axis=1, keepdims=True)
    i = lax.broadcasted_iota(jnp.int32, (count, count), 0)
    j = lax.broadcasted_iota(jnp.int32, (count, count), 1)
    identity = jnp.where(i == j, 1.0, 0.0)
    system = identity + gram / (count - 1)
    scale = jnp.sqrt(jnp.sum(jnp.sum(system * system, axis=1, keepdims=True), axis=0, keepdims=True))
    current = system / scale
    root_inv = identity
    for step in range(NS_ITERS):
        parts, inv_parts = halves(current), halves(root_inv)
        product = current if step == 0 else dot3(inv_parts, parts)
        factor = 1.5 * identity - 0.5 * product
        factor_parts = halves(factor)
        if step < NS_ITERS - 1:
            current = dot3(parts, factor_parts)
        root_inv = factor if step == 0 else dot3(factor_parts, inv_parts)
    root = root_inv / jnp.sqrt(scale)

    def times(column):
        return jnp.sum(root * jnp.sum(jnp.where(i == j, column, 0.0), axis=0, keepdims=True), axis=1, keepdims=True)

    weights_ref[...] = times(times(projection)) / (count - 1) + root


def transform(keep, got):
    share, count = keep.shape
    return pl.pallas_call(
        transform_kernel,
        out_shape=jax.ShapeDtypeStruct((count, count), jnp.float32),
        scratch_shapes=[pltpu.VMEM((2 * share, count), jnp.float32)],
        compiler_params=pltpu.CompilerParams(vmem_limit_bytes=VMEM),
        cost_estimate=cost(6 * 2 * 14 * count ** 3, 8 * count ** 2),
        name="transform",
    )(keep, got)


def mix_kernel(weights_ref, height_ref, got_height_ref, wind_ref, got_wind_ref, out_ref, order_ref):
    chips, cores, members, cols = height_ref.shape
    half, count = chips * members, chips * cores * members
    core = lax.axis_index("member") % cores
    for q in range(chips):
        for side, other in ((0, core), (1, 1 - core)):
            start = pl.multiple_of((q * cores + other) * members, members)
            order_ref[side * half + q * members:side * half + (q + 1) * members, :] = weights_ref[pl.ds(start, members), :]
    order = halves(order_ref[...])
    for first in range(0, 3 * cols, cols):
        if first == 0:
            own, got = height_ref[:, pl.ds(core, 1)], got_height_ref[...]
        else:
            own, got = wind_ref[:, pl.ds(core, 1), :, first - cols:first], got_wind_ref[:, :, first - cols:first]
        values = jnp.concatenate([own.reshape(half, cols), got.reshape(half, cols)], axis=0)
        centre = jnp.sum(values, axis=0, keepdims=True) / count
        out_ref[:, first:first + cols] = centre + dot3(order, halves(values - centre), ((0,), (0,)))


def mix(weights, height, got_height, wind, got_wind):
    count, cols = weights.shape[0], height.shape[-1]
    return pl.pallas_call(
        mix_kernel,
        out_shape=jax.ShapeDtypeStruct((count, 3 * cols), jnp.float32),
        scratch_shapes=[pltpu.VMEM(weights.shape, jnp.float32)],
        compiler_params=pltpu.CompilerParams(vmem_limit_bytes=VMEM),
        cost_estimate=cost(3 * 2 * count * count * 3 * cols, 4 * count * 6 * cols),
        name="mix",
    )(weights, height, got_height, wind, got_wind)


def unfold_kernel(rows_ref, out_ref, lanes_ref, whole_ref, sems):
    members, fields, rows, cols = whole_ref.shape
    chunks = cols // LANES
    copies = []
    for k in range(fields):
        for c in range(k * chunks, (k + 1) * chunks):
            lanes_ref[c] = rows_ref[:, c * LANES:(c + 1) * LANES]
        for m in range(members):
            for c in range(chunks):
                whole_ref[m, k, :, c * LANES:(c + 1) * LANES] = lanes_ref[k * chunks + c, pl.ds(m, rows, stride=members), :]
        copies.append(pltpu.make_async_copy(whole_ref.at[:, k], out_ref.at[:, k], sems.at[k]))
        copies[-1].start()
    for copy in copies:
        copy.wait()


def unfold(rows, shape):
    return pl.pallas_call(
        unfold_kernel,
        out_shape=jax.ShapeDtypeStruct(shape, jnp.float32),
        out_specs=pl.BlockSpec(memory_space=pl.ANY),
        scratch_shapes=[
            pltpu.VMEM((rows.shape[1] // LANES, rows.shape[0], LANES), jnp.float32),
            pltpu.VMEM(shape, jnp.float32),
            pltpu.SemaphoreType.DMA((shape[1],)),
        ],
        compiler_params=pltpu.CompilerParams(vmem_limit_bytes=VMEM),
        cost_estimate=cost(0, 8 * rows.size),
        name="unfold",
    )(rows)


def exchange(blocks, axis, groups=None):
    return lax.all_to_all(blocks, axis, split_axis=0, concat_axis=0, tiled=True, axis_index_groups=groups)


def shards(state, depth, obs_cell, obs_value, obs_var):
    bands, tiles = lax.axis_size("space"), lax.axis_size("member")
    members, rows, fields, cols = state.shape
    ensemble, chips = tiles * members, tiles // 2
    sibling = [(i, i ^ 1) for i in range(tiles)]

    state = state.transpose(0, 2, 1, 3)
    upper = [(i, i ^ 1) for i in range(bands)]
    lower = [pair for i in range(1, bands - 1, 2) for pair in ((i, i + 1), (i + 1, i))]

    first, second = edges(state, depth)
    first = lax.ppermute(first, "space", upper)
    second = lax.ppermute(second, "space", lower)
    height, wind = forecast(state, first, second, depth, bands)
    same_core = [[2 * q + core for q in range(chips)] for core in range(2)]

    def to_sibling(values):
        return lax.ppermute(pick(values, 0, values.shape[-1]), "member", sibling)

    height = exchange(height.reshape(chips, 2, members, cols), "member", same_core)
    height, wind = lax.optimization_barrier((height, wind))
    wind = exchange(wind.reshape(chips, 2, members, 2 * cols), "member", same_core)
    got_height = to_sibling(height)

    keep, send = gram_of(height, got_height, obs_cell[0], obs_value[0], obs_var[0])
    half = keep + lax.ppermute(send, "member", sibling)

    def others(value, axis, unit):
        return [lax.ppermute(value, axis, [(i, i ^ (unit * k)) for i in range(lax.axis_size(axis))]) for k in (1, 2, 3)]

    for axis, unit in (("space", 1), ("member", tiles // 4)):
        one, two, three = others(half, axis, unit)
        half = (half + one) + (two + three)
    one, two, three = others(half, "member", 2)
    half = (half + one) + (two + three)
    half, wind = lax.optimization_barrier((half, wind))
    beside = [(m * bands + i, (m ^ 1) * bands + (i ^ 4)) for m in range(tiles) for i in range(bands)]
    near = lax.ppermute(half, "space", [(i, i ^ 4) for i in range(bands)])
    far = lax.ppermute(half, ("member", "space"), beside)
    weights = transform(half + near, lax.ppermute(half, "member", sibling) + far)

    analysed = mix(weights, height, got_height, wind, to_sibling(wind))
    back = exchange(analysed.reshape(tiles, members, fields * cols), "member").reshape(ensemble, fields * cols)
    return unfold(back, (members, fields, rows, cols)).transpose(0, 2, 1, 3)


def solution(mesh):
    placed = (
        P("member", "space", None, None),
        P("space", None),
        P("space", "member", None),
        P("space", "member", None),
        P("space", "member", None),
    )
    return jax.shard_map(
        shards,
        mesh=mesh,
        in_specs=placed,
        out_specs=P("member", "space", None, None),
        check_vma=False,
    )
```

```python
import functools

import jax
import jax.numpy as jnp
from jax import lax
from jax.experimental import pallas as pl
from jax.experimental.pallas import tpu as pltpu
from jax.sharding import PartitionSpec as P

STEPS = 3
NS_ITERS = 5
COURANT = 0.3
HALO = 2 * STEPS
LANES = 128
ROW_BLOCK = 4
VMEM = 40 * 1024 * 1024
ALL_VMEM = 60 * 1024 * 1024
HIGHEST = lax.Precision.HIGHEST


def dot(a, b, dims=((1,), (0,))):
    return lax.dot_general(a, b, (dims, ((), ())), precision=HIGHEST, preferred_element_type=jnp.float32)


def halves(a):
    high = a.astype(jnp.bfloat16)
    return high, (a - high.astype(jnp.float32)).astype(jnp.bfloat16)


def dot3(a, b, dims=((1,), (0,))):
    def one(x, y):
        return lax.dot_general(x, y, (dims, ((), ())), preferred_element_type=jnp.float32)

    (a_high, a_low), (b_high, b_low) = a, b
    return one(a_high, b_high) + (one(a_high, b_low) + one(a_low, b_high))


def picked(a, picks):
    high, low = halves(a)
    rest = (a - high.astype(jnp.float32) - low.astype(jnp.float32)).astype(jnp.bfloat16)
    parts = [jnp.dot(x, picks, preferred_element_type=jnp.float32) for x in (high, low, rest)]
    return parts[0] + (parts[1] + parts[2])


def cost(flops, bytes_accessed):
    return pl.CostEstimate(flops=flops, bytes_accessed=bytes_accessed, transcendentals=0)


def edge_kernel(turn, state_ref, depth_ref, out_ref, field_ref, edge_ref, sems):
    members, fields, block, cols = field_ref.shape
    rows = depth_ref.shape[0]
    even = lax.axis_index("space") % 2 == 0
    below = even if turn == 0 else jnp.logical_not(even)
    rows_sent = pl.ds(pl.multiple_of(jnp.where(below, rows - block, 0), block), block)
    copies = [
        pltpu.make_async_copy(state_ref.at[m, :, rows_sent, :], field_ref.at[m], sems.at[m]) for m in range(members)
    ] + [pltpu.make_async_copy(depth_ref.at[rows_sent, :], edge_ref, sems.at[members])]
    for copy in copies:
        copy.start()
    for copy in copies:
        copy.wait()

    def write(last):
        for c in range(cols // LANES):
            lanes = slice(c * LANES, (c + 1) * LANES)
            at = 0
            for k in range(fields):
                count = HALO if k == 2 else HALO - 1
                first = block - count if last else 0
                for m in range(members):
                    out_ref[c, pl.ds(at + m, count, stride=members), :] = field_ref[m, k, first:first + count, lanes]
                at += count * members
            first = block - HALO + 1 if last else 0
            out_ref[c, at:at + HALO - 1, :] = edge_ref[first:first + HALO - 1, lanes]

    pl.when(below)(lambda: write(True))
    pl.when(jnp.logical_not(below))(lambda: write(False))


def edge(state, depth, turn):
    members, fields, rows, cols = state.shape
    block = 8
    return pl.pallas_call(
        functools.partial(edge_kernel, turn),
        in_specs=[pl.BlockSpec(memory_space=pl.ANY)] * 2,
        out_shape=jax.ShapeDtypeStruct((cols // LANES, (3 * HALO - 2) * members + 8, LANES), jnp.float32),
        scratch_shapes=[
            pltpu.VMEM((members, fields, block, cols), jnp.float32),
            pltpu.VMEM((block, cols), jnp.float32),
            pltpu.SemaphoreType.DMA((members + 1,)),
        ],
        compiler_params=pltpu.CompilerParams(vmem_limit_bytes=ALL_VMEM),
        cost_estimate=cost(0, state.size),
        name="edge",
    )(state, depth)


def forecast_kernel(bands, state_ref, first_ref, second_ref, depth_ref, height_ref, wind_ref, field_ref, pull_ref, made_ref, sems):
    members, fields, rows, cols = state_ref.shape
    chunks = cols // LANES
    band = lax.axis_index("space")
    lane = lax.broadcasted_iota(jnp.int32, (1, LANES), 1)

    even = band % 2 == 0

    def above(c, first, last):
        return jnp.where(even, second_ref[c, first:last, :], first_ref[c, first:last, :])

    def below(c, first, last):
        return jnp.where(even, first_ref[c, first:last, :], second_ref[c, first:last, :])

    for c in range(chunks):
        lanes = slice(c * LANES, (c + 1) * LANES)
        at = 0
        for k in range(fields):
            count = HALO if k == 2 else HALO - 1
            size = count * members
            field_ref[k, c, (HALO - count) * members:HALO * members, :] = above(c, at, at + size)
            field_ref[k, c, (HALO + rows) * members:(HALO + rows + count) * members, :] = below(c, at, at + size)
            at += size
            for m in range(members):
                field_ref[k, c, pl.ds(HALO * members + m, rows, stride=members), :] = state_ref[m, k, :, lanes]
        pull_above = COURANT * above(c, at, at + HALO - 1)
        pull_here = COURANT * depth_ref[:, lanes]
        pull_below = COURANT * below(c, at, at + HALO - 1)
        for m in range(members):
            pull_ref[c, pl.ds(members + m, HALO - 1, stride=members), :] = pull_above
            pull_ref[c, pl.ds(HALO * members + m, rows, stride=members), :] = pull_here
            pull_ref[c, pl.ds((HALO + rows) * members + m, HALO - 1, stride=members), :] = pull_below

    def cols_diff(parts):
        left = [pltpu.roll(p, 1, 1) for p in parts]
        right = [pltpu.roll(p, LANES - 1, 1) for p in parts]
        return [
            jnp.where(lane == LANES - 1, right[(c + 1) % chunks], right[c]) - jnp.where(lane == 0, left[c - 1], left[c])
            for c in range(chunks)
        ]

    def take(k, first, count):
        return [field_ref[k, c, first * members:(first + count) * members, :] for c in range(chunks)]

    def push_of(first, count):
        if first >= HALO and first + count <= HALO + rows:
            return COURANT
        row = lax.broadcasted_iota(jnp.int32, (count * members, LANES), 0) + (first + band * rows - HALO) * members
        return jnp.where(jnp.logical_and(row >= 0, row < bands * rows * members), COURANT, 0.0)

    def blocks(first, last):
        cuts = sorted({HALO, HALO + rows} | set(range(HALO, HALO + rows, ROW_BLOCK)))
        ends = [first] + [e for e in cuts if first < e < last] + [last]
        return [(lo, hi - lo) for lo, hi in zip(ends[:-1], ends[1:])]

    copies = []
    for step in range(STEPS):
        reach = 2 * (STEPS - 1 - step)
        for first, count in blocks(HALO - reach - 1, HALO + rows + reach + 1):
            height = take(0, first, count)
            slope = cols_diff(take(1, first, count))
            north = take(2, first + 1, count)
            south = take(2, first - 1, count)
            span = slice(first * members, (first + count) * members)
            for c in range(chunks):
                field_ref[0, c, span, :] = height[c] - pull_ref[c, span, :] * (slope[c] + (north[c] - south[c]))
        for first, count in blocks(HALO - reach, HALO + rows + reach):
            slope = cols_diff(take(0, first, count))
            zonal = take(1, first, count)
            meridional = take(2, first, count)
            north = take(0, first + 1, count)
            south = take(0, first - 1, count)
            push = push_of(first, count)
            span = slice(first * members, (first + count) * members)
            for c in range(chunks):
                zonal[c] = zonal[c] - COURANT * slope[c]
                meridional[c] = meridional[c] - push * (north[c] - south[c])
                if step < STEPS - 1:
                    field_ref[1, c, span, :] = zonal[c]
                    field_ref[2, c, span, :] = meridional[c]
            if step == STEPS - 1:
                here = take(0, first, count)
                for k, parts in enumerate((here, zonal, meridional)):
                    for c in range(chunks):
                        for t in range(count):
                            out_ref, start = (height_ref, 0) if k == 0 else (made_ref, (k - 1) * cols)
                            lanes = slice(start + c * LANES, start + (c + 1) * LANES)
                            out_ref[first - HALO + t, :, lanes] = parts[c][t * members:(t + 1) * members]
                leaving = pl.ds(first - HALO, count)
                copies.append(pltpu.make_async_copy(made_ref.at[leaving], wind_ref.at[leaving], sems.at[len(copies)]))
                copies[-1].start()
    for copy in copies:
        copy.wait()


def forecast(state, first, second, depth, bands):
    members, fields, rows, cols = state.shape
    total = rows + 2 * HALO
    return pl.pallas_call(
        functools.partial(forecast_kernel, bands),
        out_shape=[
            jax.ShapeDtypeStruct((rows, members, cols), jnp.float32),
            jax.ShapeDtypeStruct((rows, members, 2 * cols), jnp.float32),
        ],
        scratch_shapes=[
            pltpu.VMEM((fields, cols // LANES, total * members, LANES), jnp.float32),
            pltpu.VMEM((cols // LANES, total * members, LANES), jnp.float32),
            pltpu.VMEM((rows, members, 2 * cols), jnp.float32),
            pltpu.SemaphoreType.DMA((rows // ROW_BLOCK,)),
        ],
        out_specs=[pl.BlockSpec(memory_space=pltpu.VMEM), pl.BlockSpec(memory_space=pl.ANY)],
        compiler_params=pltpu.CompilerParams(vmem_limit_bytes=VMEM),
        cost_estimate=cost(STEPS * 12 * state.size, 8 * state.size),
        name="forecast",
    )(state, first, second, depth)


TAIL = 8


def corners(size):
    i = lax.broadcasted_iota(jnp.int32, (size, size), 0)
    j = lax.broadcasted_iota(jnp.int32, (size, size), 1)
    return i < j, i == j


def gram_kernel(height_ref, cell_ref, value_ref, var_ref, keep_ref, send_ref, whole_ref):
    count, cols = height_ref.shape
    number, half, share = cell_ref.shape[1], count // 2, keep_ref.shape[0]
    picks = lax.broadcasted_iota(jnp.int32, (cols, number), 0) == cell_ref[...]
    seen = picked(height_ref[...], jnp.where(picks, 1.0, 0.0).astype(jnp.bfloat16))
    centre = jnp.sum(seen, axis=0, keepdims=True) / count
    observed = seen - centre
    innovation = value_ref[...] - centre
    weighted = observed / var_ref[...]
    gram = dot(weighted, observed, ((1,), (1,)))
    projection = jnp.sum(weighted * innovation, axis=1, keepdims=True)
    above, diagonal = corners(half)
    last = gram[half:, half:]
    both = jnp.concatenate([jnp.where(jnp.logical_or(above, diagonal), gram[:half, :half], last), gram[:half, half:]], axis=1)
    tails = (
        jnp.sum(jnp.where(corners(count)[1], projection, 0.0), axis=0, keepdims=True),
        jnp.concatenate([jnp.sum(jnp.where(diagonal, last, 0.0), axis=0, keepdims=True), jnp.zeros((1, half), jnp.float32)], axis=1),
    )
    for side, tail in enumerate(tails):
        first, rows = side * share, share - TAIL
        whole_ref[first:first + rows, :] = both[side * rows:(side + 1) * rows]
        whole_ref[first + rows:first + share, :] = jnp.broadcast_to(tail, (TAIL, count))
    core = lax.axis_index("member") % 2
    keep_ref[...] = whole_ref[pl.ds(pl.multiple_of(core * share, TAIL), share), :]
    send_ref[...] = whole_ref[pl.ds(pl.multiple_of((1 - core) * share, TAIL), share), :]


def gram_of(height, cell, value, var):
    count, cols = height.shape
    return pl.pallas_call(
        gram_kernel,
        out_shape=[jax.ShapeDtypeStruct((count // 4 + TAIL, count), jnp.float32)] * 2,
        scratch_shapes=[pltpu.VMEM((count // 2 + 2 * TAIL, count), jnp.float32)],
        compiler_params=pltpu.CompilerParams(vmem_limit_bytes=VMEM),
        cost_estimate=cost(6 * 2 * count * cols * cell.shape[1], 4 * count * cols),
        name="gram",
    )(height, cell, value, var)


def transform_kernel(keep_ref, got_ref, weights_ref, packed_ref):
    share, count = keep_ref.shape
    half, rows = count // 2, share - TAIL
    core = lax.axis_index("member") % 2
    packed_ref[pl.ds(pl.multiple_of(core * share, TAIL), share), :] = keep_ref[...]
    packed_ref[pl.ds(pl.multiple_of((1 - core) * share, TAIL), share), :] = got_ref[...]
    both = jnp.concatenate([packed_ref[:rows, :], packed_ref[share:share + rows, :]], axis=0)
    above, diagonal = corners(half)
    corner, side = both[:, :half], both[:, half:]
    upper = jnp.where(above, corner, 0.0)
    lower = jnp.where(jnp.logical_or(above, diagonal), 0.0, corner)
    one = upper + upper.T + jnp.where(diagonal, corner, 0.0)
    two = lower + lower.T + jnp.where(diagonal, packed_ref[share + rows:share + rows + 1, :half], 0.0)
    gram = jnp.concatenate([jnp.concatenate([one, side], axis=1), jnp.concatenate([side.T, two], axis=1)], axis=0)
    projection = jnp.sum(jnp.where(corners(count)[1], packed_ref[rows:rows + 1, :], 0.0), axis=1, keepdims=True)
    i = lax.broadcasted_iota(jnp.int32, (count, count), 0)
    j = lax.broadcasted_iota(jnp.int32, (count, count), 1)
    identity = jnp.where(i == j, 1.0, 0.0)
    system = identity + gram / (count - 1)
    scale = jnp.sqrt(jnp.sum(jnp.sum(system * system, axis=1, keepdims=True), axis=0, keepdims=True))
    current = system / scale
    root_inv = identity
    for step in range(NS_ITERS):
        parts, inv_parts = halves(current), halves(root_inv)
        product = current if step == 0 else dot3(inv_parts, parts)
        factor = 1.5 * identity - 0.5 * product
        factor_parts = halves(factor)
        if step < NS_ITERS - 1:
            current = dot3(parts, factor_parts)
        root_inv = factor if step == 0 else dot3(factor_parts, inv_parts)
    root = root_inv / jnp.sqrt(scale)

    def times(column):
        return jnp.sum(root * jnp.sum(jnp.where(i == j, column, 0.0), axis=0, keepdims=True), axis=1, keepdims=True)

    weights_ref[...] = times(times(projection)) / (count - 1) + root


def transform(keep, got):
    share, count = keep.shape
    return pl.pallas_call(
        transform_kernel,
        out_shape=jax.ShapeDtypeStruct((count, count), jnp.float32),
        scratch_shapes=[pltpu.VMEM((2 * share, count), jnp.float32)],
        compiler_params=pltpu.CompilerParams(vmem_limit_bytes=VMEM),
        cost_estimate=cost(6 * 2 * 14 * count ** 3, 8 * count ** 2),
        name="transform",
    )(keep, got)


def mix_kernel(weights_ref, height_ref, wind_ref, out_ref):
    weights = halves(weights_ref[...])
    count, cols = height_ref.shape
    for first in range(0, 3 * cols, cols):
        values = height_ref[...] if first == 0 else wind_ref[:, first - cols:first]
        centre = jnp.sum(values, axis=0, keepdims=True) / count
        out_ref[:, first:first + cols] = centre + dot3(weights, halves(values - centre), ((0,), (0,)))


def mix(weights, height, wind):
    count, cols = height.shape
    return pl.pallas_call(
        mix_kernel,
        out_shape=jax.ShapeDtypeStruct((count, 3 * cols), jnp.float32),
        compiler_params=pltpu.CompilerParams(vmem_limit_bytes=VMEM),
        cost_estimate=cost(3 * 2 * count * count * 3 * cols, 4 * count * 6 * cols),
        name="mix",
    )(weights, height, wind)


def unfold_kernel(rows_ref, out_ref, lanes_ref, whole_ref, sems):
    members, fields, rows, cols = whole_ref.shape
    chunks = cols // LANES
    copies = []
    for k in range(fields):
        for c in range(k * chunks, (k + 1) * chunks):
            lanes_ref[c] = rows_ref[:, c * LANES:(c + 1) * LANES]
        for m in range(members):
            for c in range(chunks):
                whole_ref[m, k, :, c * LANES:(c + 1) * LANES] = lanes_ref[k * chunks + c, pl.ds(m, rows, stride=members), :]
        copies.append(pltpu.make_async_copy(whole_ref.at[:, k], out_ref.at[:, k], sems.at[k]))
        copies[-1].start()
    for copy in copies:
        copy.wait()


def unfold(rows, shape):
    return pl.pallas_call(
        unfold_kernel,
        out_shape=jax.ShapeDtypeStruct(shape, jnp.float32),
        out_specs=pl.BlockSpec(memory_space=pl.ANY),
        scratch_shapes=[
            pltpu.VMEM((rows.shape[1] // LANES, rows.shape[0], LANES), jnp.float32),
            pltpu.VMEM(shape, jnp.float32),
            pltpu.SemaphoreType.DMA((shape[1],)),
        ],
        compiler_params=pltpu.CompilerParams(vmem_limit_bytes=VMEM),
        cost_estimate=cost(0, 8 * rows.size),
        name="unfold",
    )(rows)


def exchange(blocks, axis):
    return lax.all_to_all(blocks, axis, split_axis=0, concat_axis=0, tiled=True)


def shards(state, depth, obs_cell, obs_value, obs_var):
    bands, tiles = lax.axis_size("space"), lax.axis_size("member")
    members, rows, fields, cols = state.shape
    ensemble, chips = tiles * members, tiles // 2
    sibling = [(i, i ^ 1) for i in range(tiles)]

    state = state.transpose(0, 2, 1, 3)
    upper = [(i, i ^ 1) for i in range(bands)]
    lower = [pair for i in range(1, bands - 1, 2) for pair in ((i, i + 1), (i + 1, i))]

    first = lax.ppermute(edge(state, depth, 0), "space", upper)
    second = lax.ppermute(edge(state, depth, 1), "space", lower)
    height, wind = forecast(state, first, second, depth, bands)
    height = exchange(height, "member").reshape(ensemble, cols)
    height, wind = lax.optimization_barrier((height, wind))
    wind = exchange(wind, "member").reshape(ensemble, 2 * cols)

    keep, send = gram_of(height, obs_cell[0], obs_value[0], obs_var[0])
    half = keep + lax.ppermute(send, "member", sibling)

    def others(value, axis, unit):
        return [lax.ppermute(value, axis, [(i, i ^ (unit * k)) for i in range(lax.axis_size(axis))]) for k in (1, 2, 3)]

    for axis, unit in (("space", 1), ("member", tiles // 4)):
        one, two, three = others(half, axis, unit)
        half = (half + one) + (two + three)
    one, two, three = others(half, "member", 2)
    half = (half + one) + (two + three)
    half, wind = lax.optimization_barrier((half, wind))
    beside = [(m * bands + i, (m ^ 1) * bands + (i ^ 4)) for m in range(tiles) for i in range(bands)]
    near = lax.ppermute(half, "space", [(i, i ^ 4) for i in range(bands)])
    far = lax.ppermute(half, ("member", "space"), beside)
    weights = transform(half + near, lax.ppermute(half, "member", sibling) + far)

    analysed = mix(weights, height, wind)
    back = exchange(analysed.reshape(tiles, members, fields * cols), "member").reshape(ensemble, fields * cols)
    return unfold(back, (members, fields, rows, cols)).transpose(0, 2, 1, 3)


def solution(mesh):
    placed = (
        P("member", "space", None, None),
        P("space", None),
        P("space", "member", None),
        P("space", "member", None),
        P("space", "member", None),
    )
    return jax.shard_map(
        shards,
        mesh=mesh,
        in_specs=placed,
        out_specs=P("member", "space", None, None),
        check_vma=False,
    )
```

```python
import functools

import jax
import jax.numpy as jnp
from jax import lax
from jax.experimental import pallas as pl
from jax.experimental.pallas import tpu as pltpu
from jax.sharding import PartitionSpec as P

STEPS = 3
NS_ITERS = 5
COURANT = 0.3
HALO = 2 * STEPS
LANES = 128
ROW_BLOCK = 4
VMEM = 40 * 1024 * 1024
ALL_VMEM = 60 * 1024 * 1024
HIGHEST = lax.Precision.HIGHEST


def dot(a, b, dims=((1,), (0,))):
    return lax.dot_general(a, b, (dims, ((), ())), precision=HIGHEST, preferred_element_type=jnp.float32)


def halves(a):
    high = a.astype(jnp.bfloat16)
    return high, (a - high.astype(jnp.float32)).astype(jnp.bfloat16)


def dot3(a, b, dims=((1,), (0,))):
    def one(x, y):
        return lax.dot_general(x, y, (dims, ((), ())), preferred_element_type=jnp.float32)

    (a_high, a_low), (b_high, b_low) = a, b
    return one(a_high, b_high) + (one(a_high, b_low) + one(a_low, b_high))


def picked(a, picks):
    high, low = halves(a)
    rest = (a - high.astype(jnp.float32) - low.astype(jnp.float32)).astype(jnp.bfloat16)
    parts = [jnp.dot(x, picks, preferred_element_type=jnp.float32) for x in (high, low, rest)]
    return parts[0] + (parts[1] + parts[2])


def cost(flops, bytes_accessed):
    return pl.CostEstimate(flops=flops, bytes_accessed=bytes_accessed, transcendentals=0)


def edges_kernel(state_ref, depth_ref, first_ref, second_ref, top_ref, bottom_ref, depth_top_ref, depth_bottom_ref, sems):
    members, fields, block, cols = top_ref.shape
    rows = depth_ref.shape[0]
    even = lax.axis_index("space") % 2 == 0
    sides = (
        (bottom_ref, depth_bottom_ref, rows - block, True),
        (top_ref, depth_top_ref, 0, False),
    )
    copies = []
    for side, (field_ref, edge_ref, start, _) in enumerate(sides):
        copies.append([
            pltpu.make_async_copy(state_ref.at[m, :, pl.ds(start, block), :], field_ref.at[m], sems.at[side, m])
            for m in range(members)
        ] + [pltpu.make_async_copy(depth_ref.at[pl.ds(start, block), :], edge_ref, sems.at[side, members])])
        for copy in copies[-1]:
            copy.start()

    def write(out_ref, field_ref, edge_ref, last):
        for c in range(cols // LANES):
            lanes = slice(c * LANES, (c + 1) * LANES)
            at = 0
            for k in range(fields):
                count = HALO if k == 2 else HALO - 1
                first = block - count if last else 0
                for m in range(members):
                    out_ref[c, pl.ds(at + m, count, stride=members), :] = field_ref[m, k, first:first + count, lanes]
                at += count * members
            first = block - HALO + 1 if last else 0
            out_ref[c, at:at + HALO - 1, :] = edge_ref[first:first + HALO - 1, lanes]

    for (field_ref, edge_ref, _, last), waits in zip(sides, copies):
        for copy in waits:
            copy.wait()
        for out_ref, here in ((first_ref, even), (second_ref, jnp.logical_not(even))):
            @pl.when(here if last else jnp.logical_not(here))
            def _():
                write(out_ref, field_ref, edge_ref, last)


def edges(state, depth):
    members, fields, rows, cols = state.shape
    block = 8
    shape = jax.ShapeDtypeStruct((cols // LANES, (3 * HALO - 2) * members + 8, LANES), jnp.float32)
    return pl.pallas_call(
        edges_kernel,
        in_specs=[pl.BlockSpec(memory_space=pl.ANY)] * 2,
        out_shape=[shape] * 2,
        scratch_shapes=[
            pltpu.VMEM((members, fields, block, cols), jnp.float32),
            pltpu.VMEM((members, fields, block, cols), jnp.float32),
            pltpu.VMEM((block, cols), jnp.float32),
            pltpu.VMEM((block, cols), jnp.float32),
            pltpu.SemaphoreType.DMA((2, members + 1)),
        ],
        compiler_params=pltpu.CompilerParams(vmem_limit_bytes=ALL_VMEM),
        cost_estimate=cost(0, 2 * state.size),
        name="edges",
    )(state, depth)


def forecast_kernel(bands, state_ref, first_ref, second_ref, depth_ref, height_ref, wind_ref, field_ref, pull_ref, made_ref, sems):
    members, fields, rows, cols = state_ref.shape
    chunks = cols // LANES
    band = lax.axis_index("space")
    lane = lax.broadcasted_iota(jnp.int32, (1, LANES), 1)

    even = band % 2 == 0

    def above(c, first, last):
        return jnp.where(even, second_ref[c, first:last, :], first_ref[c, first:last, :])

    def below(c, first, last):
        return jnp.where(even, first_ref[c, first:last, :], second_ref[c, first:last, :])

    for c in range(chunks):
        lanes = slice(c * LANES, (c + 1) * LANES)
        at = 0
        for k in range(fields):
            count = HALO if k == 2 else HALO - 1
            size = count * members
            field_ref[k, c, (HALO - count) * members:HALO * members, :] = above(c, at, at + size)
            field_ref[k, c, (HALO + rows) * members:(HALO + rows + count) * members, :] = below(c, at, at + size)
            at += size
            for m in range(members):
                field_ref[k, c, pl.ds(HALO * members + m, rows, stride=members), :] = state_ref[m, k, :, lanes]
        pull_above = COURANT * above(c, at, at + HALO - 1)
        pull_here = COURANT * depth_ref[:, lanes]
        pull_below = COURANT * below(c, at, at + HALO - 1)
        for m in range(members):
            pull_ref[c, pl.ds(members + m, HALO - 1, stride=members), :] = pull_above
            pull_ref[c, pl.ds(HALO * members + m, rows, stride=members), :] = pull_here
            pull_ref[c, pl.ds((HALO + rows) * members + m, HALO - 1, stride=members), :] = pull_below

    def cols_diff(parts):
        left = [pltpu.roll(p, 1, 1) for p in parts]
        right = [pltpu.roll(p, LANES - 1, 1) for p in parts]
        return [
            jnp.where(lane == LANES - 1, right[(c + 1) % chunks], right[c]) - jnp.where(lane == 0, left[c - 1], left[c])
            for c in range(chunks)
        ]

    def take(k, first, count):
        return [field_ref[k, c, first * members:(first + count) * members, :] for c in range(chunks)]

    def push_of(first, count):
        if first >= HALO and first + count <= HALO + rows:
            return COURANT
        row = lax.broadcasted_iota(jnp.int32, (count * members, LANES), 0) + (first + band * rows - HALO) * members
        return jnp.where(jnp.logical_and(row >= 0, row < bands * rows * members), COURANT, 0.0)

    def blocks(first, last):
        cuts = sorted({HALO, HALO + rows} | set(range(HALO, HALO + rows, ROW_BLOCK)))
        ends = [first] + [e for e in cuts if first < e < last] + [last]
        return [(lo, hi - lo) for lo, hi in zip(ends[:-1], ends[1:])]

    copies = []
    for step in range(STEPS):
        reach = 2 * (STEPS - 1 - step)
        for first, count in blocks(HALO - reach - 1, HALO + rows + reach + 1):
            height = take(0, first, count)
            slope = cols_diff(take(1, first, count))
            north = take(2, first + 1, count)
            south = take(2, first - 1, count)
            span = slice(first * members, (first + count) * members)
            for c in range(chunks):
                field_ref[0, c, span, :] = height[c] - pull_ref[c, span, :] * (slope[c] + (north[c] - south[c]))
        for first, count in blocks(HALO - reach, HALO + rows + reach):
            slope = cols_diff(take(0, first, count))
            zonal = take(1, first, count)
            meridional = take(2, first, count)
            north = take(0, first + 1, count)
            south = take(0, first - 1, count)
            push = push_of(first, count)
            span = slice(first * members, (first + count) * members)
            for c in range(chunks):
                zonal[c] = zonal[c] - COURANT * slope[c]
                meridional[c] = meridional[c] - push * (north[c] - south[c])
                if step < STEPS - 1:
                    field_ref[1, c, span, :] = zonal[c]
                    field_ref[2, c, span, :] = meridional[c]
            if step == STEPS - 1:
                here = take(0, first, count)
                for k, parts in enumerate((here, zonal, meridional)):
                    for c in range(chunks):
                        for t in range(count):
                            out_ref, start = (height_ref, 0) if k == 0 else (made_ref, (k - 1) * cols)
                            lanes = slice(start + c * LANES, start + (c + 1) * LANES)
                            out_ref[first - HALO + t, :, lanes] = parts[c][t * members:(t + 1) * members]
                leaving = pl.ds(first - HALO, count)
                copies.append(pltpu.make_async_copy(made_ref.at[leaving], wind_ref.at[leaving], sems.at[len(copies)]))
                copies[-1].start()
    for copy in copies:
        copy.wait()


def forecast(state, first, second, depth, bands):
    members, fields, rows, cols = state.shape
    total = rows + 2 * HALO
    return pl.pallas_call(
        functools.partial(forecast_kernel, bands),
        out_shape=[
            jax.ShapeDtypeStruct((rows, members, cols), jnp.float32),
            jax.ShapeDtypeStruct((rows, members, 2 * cols), jnp.float32),
        ],
        scratch_shapes=[
            pltpu.VMEM((fields, cols // LANES, total * members, LANES), jnp.float32),
            pltpu.VMEM((cols // LANES, total * members, LANES), jnp.float32),
            pltpu.VMEM((rows, members, 2 * cols), jnp.float32),
            pltpu.SemaphoreType.DMA((rows // ROW_BLOCK,)),
        ],
        out_specs=[pl.BlockSpec(memory_space=pltpu.VMEM), pl.BlockSpec(memory_space=pl.ANY)],
        compiler_params=pltpu.CompilerParams(vmem_limit_bytes=VMEM),
        cost_estimate=cost(STEPS * 12 * state.size, 8 * state.size),
        name="forecast",
    )(state, first, second, depth)


TAIL = 8


def corners(size):
    i = lax.broadcasted_iota(jnp.int32, (size, size), 0)
    j = lax.broadcasted_iota(jnp.int32, (size, size), 1)
    return i < j, i == j


def gram_kernel(height_ref, got_ref, cell_ref, value_ref, var_ref, keep_ref, send_ref, seen_ref, whole_ref):
    chips, cores, members, cols = height_ref.shape
    count = chips * cores * members
    number, half, share = cell_ref.shape[1], count // 2, keep_ref.shape[0]
    picks = lax.broadcasted_iota(jnp.int32, (cols, number), 0) == cell_ref[...]
    picks = jnp.where(picks, 1.0, 0.0).astype(jnp.bfloat16)
    core = lax.axis_index("member") % cores
    own = height_ref[:, pl.ds(core, 1)].reshape(half, cols)
    seen_ref[:, pl.ds(core, 1)] = picked(own, picks).reshape(chips, 1, members, number)
    seen_ref[:, pl.ds(1 - core, 1)] = picked(got_ref[...].reshape(half, cols), picks).reshape(chips, 1, members, number)
    seen = seen_ref[...].reshape(count, number)
    centre = jnp.sum(seen, axis=0, keepdims=True) / count
    observed = seen - centre
    innovation = value_ref[...] - centre
    weighted = observed / var_ref[...]
    gram = dot(weighted, observed, ((1,), (1,)))
    projection = jnp.sum(weighted * innovation, axis=1, keepdims=True)
    above, diagonal = corners(half)
    last = gram[half:, half:]
    both = jnp.concatenate([jnp.where(jnp.logical_or(above, diagonal), gram[:half, :half], last), gram[:half, half:]], axis=1)
    tails = (
        jnp.sum(jnp.where(corners(count)[1], projection, 0.0), axis=0, keepdims=True),
        jnp.concatenate([jnp.sum(jnp.where(diagonal, last, 0.0), axis=0, keepdims=True), jnp.zeros((1, half), jnp.float32)], axis=1),
    )
    for side, tail in enumerate(tails):
        first, rows = side * share, share - TAIL
        whole_ref[first:first + rows, :] = both[side * rows:(side + 1) * rows]
        whole_ref[first + rows:first + share, :] = jnp.broadcast_to(tail, (TAIL, count))
    keep_ref[...] = whole_ref[pl.ds(pl.multiple_of(core * share, TAIL), share), :]
    send_ref[...] = whole_ref[pl.ds(pl.multiple_of((1 - core) * share, TAIL), share), :]


def gram_of(height, got, cell, value, var):
    chips, cores, members, cols = height.shape
    count = chips * cores * members
    return pl.pallas_call(
        gram_kernel,
        out_shape=[jax.ShapeDtypeStruct((count // 4 + TAIL, count), jnp.float32)] * 2,
        scratch_shapes=[
            pltpu.VMEM((chips, cores, members, cell.shape[1]), jnp.float32),
            pltpu.VMEM((count // 2 + 2 * TAIL, count), jnp.float32),
        ],
        compiler_params=pltpu.CompilerParams(vmem_limit_bytes=VMEM),
        cost_estimate=cost(6 * 2 * count * cols * cell.shape[1], 4 * count * cols),
        name="gram",
    )(height, got, cell, value, var)


def pick_kernel(first, state_ref, out_ref):
    chips, members, width = out_ref.shape
    other = 1 - lax.axis_index("member") % 2
    out_ref[...] = state_ref[:, pl.ds(other, 1), :, first:first + width].reshape(out_ref.shape)


def pick(state, first, last):
    chips, cores, members, _ = state.shape
    shape = jax.ShapeDtypeStruct((chips, members, last - first), jnp.float32)
    return pl.pallas_call(
        functools.partial(pick_kernel, first),
        out_shape=shape,
        compiler_params=pltpu.CompilerParams(vmem_limit_bytes=VMEM),
        cost_estimate=cost(0, 8 * shape.size),
        name="pick",
    )(state)


def transform_kernel(keep_ref, got_ref, weights_ref, packed_ref):
    share, count = keep_ref.shape
    half, rows = count // 2, share - TAIL
    core = lax.axis_index("member") % 2
    packed_ref[pl.ds(pl.multiple_of(core * share, TAIL), share), :] = keep_ref[...]
    packed_ref[pl.ds(pl.multiple_of((1 - core) * share, TAIL), share), :] = got_ref[...]
    both = jnp.concatenate([packed_ref[:rows, :], packed_ref[share:share + rows, :]], axis=0)
    above, diagonal = corners(half)
    corner, side = both[:, :half], both[:, half:]
    upper = jnp.where(above, corner, 0.0)
    lower = jnp.where(jnp.logical_or(above, diagonal), 0.0, corner)
    one = upper + upper.T + jnp.where(diagonal, corner, 0.0)
    two = lower + lower.T + jnp.where(diagonal, packed_ref[share + rows:share + rows + 1, :half], 0.0)
    gram = jnp.concatenate([jnp.concatenate([one, side], axis=1), jnp.concatenate([side.T, two], axis=1)], axis=0)
    projection = jnp.sum(jnp.where(corners(count)[1], packed_ref[rows:rows + 1, :], 0.0), axis=1, keepdims=True)
    i = lax.broadcasted_iota(jnp.int32, (count, count), 0)
    j = lax.broadcasted_iota(jnp.int32, (count, count), 1)
    identity = jnp.where(i == j, 1.0, 0.0)
    system = identity + gram / (count - 1)
    scale = jnp.sqrt(jnp.sum(jnp.sum(system * system, axis=1, keepdims=True), axis=0, keepdims=True))
    current = system / scale
    root_inv = identity
    for step in range(NS_ITERS):
        parts, inv_parts = halves(current), halves(root_inv)
        product = current if step == 0 else dot3(inv_parts, parts)
        factor = 1.5 * identity - 0.5 * product
        factor_parts = halves(factor)
        if step < NS_ITERS - 1:
            current = dot3(parts, factor_parts)
        root_inv = factor if step == 0 else dot3(factor_parts, inv_parts)
    root = root_inv / jnp.sqrt(scale)

    def times(column):
        return jnp.sum(root * jnp.sum(jnp.where(i == j, column, 0.0), axis=0, keepdims=True), axis=1, keepdims=True)

    weights_ref[...] = times(times(projection)) / (count - 1) + root


def transform(keep, got):
    share, count = keep.shape
    return pl.pallas_call(
        transform_kernel,
        out_shape=jax.ShapeDtypeStruct((count, count), jnp.float32),
        scratch_shapes=[pltpu.VMEM((2 * share, count), jnp.float32)],
        compiler_params=pltpu.CompilerParams(vmem_limit_bytes=VMEM),
        cost_estimate=cost(6 * 2 * 14 * count ** 3, 8 * count ** 2),
        name="transform",
    )(keep, got)


def mix_kernel(weights_ref, height_ref, got_height_ref, wind_ref, out_ref, order_ref):
    chips, cores, members, cols = height_ref.shape
    half, count = chips * members, chips * cores * members
    core = lax.axis_index("member") % cores
    for q in range(chips):
        for side, other in ((0, core), (1, 1 - core)):
            start = pl.multiple_of((q * cores + other) * members, members)
            order_ref[side * half + q * members:side * half + (q + 1) * members, :] = weights_ref[pl.ds(start, members), :]

    def mixed(values, coefficients):
        centre = jnp.sum(values, axis=0, keepdims=True) / count
        return centre + dot3(coefficients, halves(values - centre), ((0,), (0,)))

    own = height_ref[:, pl.ds(core, 1)].reshape(half, cols)
    heights = jnp.concatenate([own, got_height_ref[...].reshape(half, cols)], axis=0)
    out_ref[:, :cols] = mixed(heights, halves(order_ref[...]))
    weights = halves(weights_ref[...])
    for first in (0, cols):
        out_ref[:, cols + first:2 * cols + first] = mixed(wind_ref[:, first:first + cols], weights)


def mix(weights, height, got_height, wind):
    count, cols = weights.shape[0], height.shape[-1]
    return pl.pallas_call(
        mix_kernel,
        out_shape=jax.ShapeDtypeStruct((count, 3 * cols), jnp.float32),
        scratch_shapes=[pltpu.VMEM(weights.shape, jnp.float32)],
        compiler_params=pltpu.CompilerParams(vmem_limit_bytes=VMEM),
        cost_estimate=cost(3 * 2 * count * count * 3 * cols, 4 * count * 6 * cols),
        name="mix",
    )(weights, height, got_height, wind)


def unfold_kernel(rows_ref, out_ref, lanes_ref, whole_ref, sems):
    members, fields, rows, cols = whole_ref.shape
    chunks = cols // LANES
    copies = []
    for k in range(fields):
        for c in range(k * chunks, (k + 1) * chunks):
            lanes_ref[c] = rows_ref[:, c * LANES:(c + 1) * LANES]
        for m in range(members):
            for c in range(chunks):
                whole_ref[m, k, :, c * LANES:(c + 1) * LANES] = lanes_ref[k * chunks + c, pl.ds(m, rows, stride=members), :]
        copies.append(pltpu.make_async_copy(whole_ref.at[:, k], out_ref.at[:, k], sems.at[k]))
        copies[-1].start()
    for copy in copies:
        copy.wait()


def unfold(rows, shape):
    return pl.pallas_call(
        unfold_kernel,
        out_shape=jax.ShapeDtypeStruct(shape, jnp.float32),
        out_specs=pl.BlockSpec(memory_space=pl.ANY),
        scratch_shapes=[
            pltpu.VMEM((rows.shape[1] // LANES, rows.shape[0], LANES), jnp.float32),
            pltpu.VMEM(shape, jnp.float32),
            pltpu.SemaphoreType.DMA((shape[1],)),
        ],
        compiler_params=pltpu.CompilerParams(vmem_limit_bytes=VMEM),
        cost_estimate=cost(0, 8 * rows.size),
        name="unfold",
    )(rows)


def exchange(blocks, axis, groups=None):
    return lax.all_to_all(blocks, axis, split_axis=0, concat_axis=0, tiled=True, axis_index_groups=groups)


def shards(state, depth, obs_cell, obs_value, obs_var):
    bands, tiles = lax.axis_size("space"), lax.axis_size("member")
    members, rows, fields, cols = state.shape
    ensemble, chips = tiles * members, tiles // 2
    sibling = [(i, i ^ 1) for i in range(tiles)]

    state = state.transpose(0, 2, 1, 3)
    upper = [(i, i ^ 1) for i in range(bands)]
    lower = [pair for i in range(1, bands - 1, 2) for pair in ((i, i + 1), (i + 1, i))]

    first, second = edges(state, depth)
    first = lax.ppermute(first, "space", upper)
    second = lax.ppermute(second, "space", lower)
    height, wind = forecast(state, first, second, depth, bands)
    same_core = [[2 * q + core for q in range(chips)] for core in range(2)]

    height = exchange(height.reshape(chips, 2, members, cols), "member", same_core)
    height, wind = lax.optimization_barrier((height, wind))
    wind = exchange(wind, "member").reshape(ensemble, 2 * cols)
    got_height = lax.ppermute(pick(height, 0, cols), "member", sibling)

    keep, send = gram_of(height, got_height, obs_cell[0], obs_value[0], obs_var[0])
    half = keep + lax.ppermute(send, "member", sibling)

    def others(value, axis, unit):
        return [lax.ppermute(value, axis, [(i, i ^ (unit * k)) for i in range(lax.axis_size(axis))]) for k in (1, 2, 3)]

    for axis, unit in (("space", 1), ("member", tiles // 4)):
        one, two, three = others(half, axis, unit)
        half = (half + one) + (two + three)
    one, two, three = others(half, "member", 2)
    half = (half + one) + (two + three)
    half, wind = lax.optimization_barrier((half, wind))
    beside = [(m * bands + i, (m ^ 1) * bands + (i ^ 4)) for m in range(tiles) for i in range(bands)]
    near = lax.ppermute(half, "space", [(i, i ^ 4) for i in range(bands)])
    far = lax.ppermute(half, ("member", "space"), beside)
    weights = transform(half + near, lax.ppermute(half, "member", sibling) + far)

    analysed = mix(weights, height, got_height, wind)
    back = exchange(analysed.reshape(tiles, members, fields * cols), "member").reshape(ensemble, fields * cols)
    return unfold(back, (members, fields, rows, cols)).transpose(0, 2, 1, 3)


def solution(mesh):
    placed = (
        P("member", "space", None, None),
        P("space", None),
        P("space", "member", None),
        P("space", "member", None),
        P("space", "member", None),
    )
    return jax.shard_map(
        shards,
        mesh=mesh,
        in_specs=placed,
        out_specs=P("member", "space", None, None),
        check_vma=False,
    )
```

```python
import functools

import jax
import jax.numpy as jnp
from jax import lax
from jax.experimental import pallas as pl
from jax.experimental.pallas import tpu as pltpu
from jax.sharding import PartitionSpec as P

STEPS = 3
NS_ITERS = 5
COURANT = 0.3
HALO = 2 * STEPS
LANES = 128
ROW_BLOCK = 4
VMEM = 40 * 1024 * 1024
ALL_VMEM = 60 * 1024 * 1024
HIGHEST = lax.Precision.HIGHEST


def dot(a, b, dims=((1,), (0,))):
    return lax.dot_general(a, b, (dims, ((), ())), precision=HIGHEST, preferred_element_type=jnp.float32)


def halves(a):
    high = a.astype(jnp.bfloat16)
    return high, (a - high.astype(jnp.float32)).astype(jnp.bfloat16)


def dot3(a, b, dims=((1,), (0,))):
    def one(x, y):
        return lax.dot_general(x, y, (dims, ((), ())), preferred_element_type=jnp.float32)

    (a_high, a_low), (b_high, b_low) = a, b
    return one(a_high, b_high) + (one(a_high, b_low) + one(a_low, b_high))


def picked(a, picks):
    high, low = halves(a)
    rest = (a - high.astype(jnp.float32) - low.astype(jnp.float32)).astype(jnp.bfloat16)
    parts = [jnp.dot(x, picks, preferred_element_type=jnp.float32) for x in (high, low, rest)]
    return parts[0] + (parts[1] + parts[2])


def cost(flops, bytes_accessed):
    return pl.CostEstimate(flops=flops, bytes_accessed=bytes_accessed, transcendentals=0)


def edges_kernel(state_ref, depth_ref, first_ref, second_ref, top_ref, bottom_ref, depth_top_ref, depth_bottom_ref, sems):
    members, fields, block, cols = top_ref.shape
    rows = depth_ref.shape[0]
    even = lax.axis_index("space") % 2 == 0
    sides = (
        (bottom_ref, depth_bottom_ref, rows - block, True),
        (top_ref, depth_top_ref, 0, False),
    )
    copies = []
    for side, (field_ref, edge_ref, start, _) in enumerate(sides):
        copies.append([
            pltpu.make_async_copy(state_ref.at[m, :, pl.ds(start, block), :], field_ref.at[m], sems.at[side, m])
            for m in range(members)
        ] + [pltpu.make_async_copy(depth_ref.at[pl.ds(start, block), :], edge_ref, sems.at[side, members])])
        for copy in copies[-1]:
            copy.start()

    def write(out_ref, field_ref, edge_ref, last):
        for c in range(cols // LANES):
            lanes = slice(c * LANES, (c + 1) * LANES)
            at = 0
            for k in range(fields):
                count = HALO if k == 2 else HALO - 1
                first = block - count if last else 0
                for m in range(members):
                    out_ref[c, pl.ds(at + m, count, stride=members), :] = field_ref[m, k, first:first + count, lanes]
                at += count * members
            first = block - HALO + 1 if last else 0
            out_ref[c, at:at + HALO - 1, :] = edge_ref[first:first + HALO - 1, lanes]

    for (field_ref, edge_ref, _, last), waits in zip(sides, copies):
        for copy in waits:
            copy.wait()
        for out_ref, here in ((first_ref, even), (second_ref, jnp.logical_not(even))):
            @pl.when(here if last else jnp.logical_not(here))
            def _():
                write(out_ref, field_ref, edge_ref, last)


def edges(state, depth):
    members, fields, rows, cols = state.shape
    block = 8
    shape = jax.ShapeDtypeStruct((cols // LANES, (3 * HALO - 2) * members + 16, LANES), jnp.float32)
    return pl.pallas_call(
        edges_kernel,
        in_specs=[pl.BlockSpec(memory_space=pl.ANY)] * 2,
        out_shape=[shape] * 2,
        scratch_shapes=[
            pltpu.VMEM((members, fields, block, cols), jnp.float32),
            pltpu.VMEM((members, fields, block, cols), jnp.float32),
            pltpu.VMEM((block, cols), jnp.float32),
            pltpu.VMEM((block, cols), jnp.float32),
            pltpu.SemaphoreType.DMA((2, members + 1)),
        ],
        compiler_params=pltpu.CompilerParams(vmem_limit_bytes=ALL_VMEM),
        cost_estimate=cost(0, 2 * state.size),
        name="edges",
    )(state, depth)


def forecast_kernel(bands, state_ref, first_ref, second_ref, depth_ref, height_ref, wind_ref, field_ref, pull_ref, made_ref, sems):
    members, fields, rows, cols = state_ref.shape
    chunks = cols // LANES
    band = lax.axis_index("space")
    lane = lax.broadcasted_iota(jnp.int32, (1, LANES), 1)

    even = band % 2 == 0

    def above(c, first, last):
        return jnp.where(even, second_ref[c, first:last, :], first_ref[c, first:last, :])

    def below(c, first, last):
        return jnp.where(even, first_ref[c, first:last, :], second_ref[c, first:last, :])

    for c in range(chunks):
        lanes = slice(c * LANES, (c + 1) * LANES)
        at = 0
        for k in range(fields):
            count = HALO if k == 2 else HALO - 1
            size = count * members
            field_ref[k, c, (HALO - count) * members:HALO * members, :] = above(c, at, at + size)
            field_ref[k, c, (HALO + rows) * members:(HALO + rows + count) * members, :] = below(c, at, at + size)
            at += size
            for m in range(members):
                field_ref[k, c, pl.ds(HALO * members + m, rows, stride=members), :] = state_ref[m, k, :, lanes]
        pull_above = COURANT * above(c, at, at + HALO - 1)
        pull_here = COURANT * depth_ref[:, lanes]
        pull_below = COURANT * below(c, at, at + HALO - 1)
        for m in range(members):
            pull_ref[c, pl.ds(members + m, HALO - 1, stride=members), :] = pull_above
            pull_ref[c, pl.ds(HALO * members + m, rows, stride=members), :] = pull_here
            pull_ref[c, pl.ds((HALO + rows) * members + m, HALO - 1, stride=members), :] = pull_below

    def cols_diff(parts):
        left = [pltpu.roll(p, 1, 1) for p in parts]
        right = [pltpu.roll(p, LANES - 1, 1) for p in parts]
        return [
            jnp.where(lane == LANES - 1, right[(c + 1) % chunks], right[c]) - jnp.where(lane == 0, left[c - 1], left[c])
            for c in range(chunks)
        ]

    def take(k, first, count):
        return [field_ref[k, c, first * members:(first + count) * members, :] for c in range(chunks)]

    def push_of(first, count):
        if first >= HALO and first + count <= HALO + rows:
            return COURANT
        row = lax.broadcasted_iota(jnp.int32, (count * members, LANES), 0) + (first + band * rows - HALO) * members
        return jnp.where(jnp.logical_and(row >= 0, row < bands * rows * members), COURANT, 0.0)

    def blocks(first, last):
        cuts = sorted({HALO, HALO + rows} | set(range(HALO, HALO + rows, ROW_BLOCK)))
        ends = [first] + [e for e in cuts if first < e < last] + [last]
        return [(lo, hi - lo) for lo, hi in zip(ends[:-1], ends[1:])]

    copies = []
    for step in range(STEPS):
        reach = 2 * (STEPS - 1 - step)
        for first, count in blocks(HALO - reach - 1, HALO + rows + reach + 1):
            height = take(0, first, count)
            slope = cols_diff(take(1, first, count))
            north = take(2, first + 1, count)
            south = take(2, first - 1, count)
            span = slice(first * members, (first + count) * members)
            for c in range(chunks):
                field_ref[0, c, span, :] = height[c] - pull_ref[c, span, :] * (slope[c] + (north[c] - south[c]))
        for first, count in blocks(HALO - reach, HALO + rows + reach):
            slope = cols_diff(take(0, first, count))
            zonal = take(1, first, count)
            meridional = take(2, first, count)
            north = take(0, first + 1, count)
            south = take(0, first - 1, count)
            push = push_of(first, count)
            span = slice(first * members, (first + count) * members)
            for c in range(chunks):
                zonal[c] = zonal[c] - COURANT * slope[c]
                meridional[c] = meridional[c] - push * (north[c] - south[c])
                if step < STEPS - 1:
                    field_ref[1, c, span, :] = zonal[c]
                    field_ref[2, c, span, :] = meridional[c]
            if step == STEPS - 1:
                here = take(0, first, count)
                for k, parts in enumerate((here, zonal, meridional)):
                    for c in range(chunks):
                        for t in range(count):
                            out_ref, start = (height_ref, 0) if k == 0 else (made_ref, (k - 1) * cols)
                            lanes = slice(start + c * LANES, start + (c + 1) * LANES)
                            out_ref[first - HALO + t, :, lanes] = parts[c][t * members:(t + 1) * members]
                leaving = pl.ds(first - HALO, count)
                copies.append(pltpu.make_async_copy(made_ref.at[leaving], wind_ref.at[leaving], sems.at[len(copies)]))
                copies[-1].start()
    for copy in copies:
        copy.wait()


def forecast(state, first, second, depth, bands):
    members, fields, rows, cols = state.shape
    total = rows + 2 * HALO
    return pl.pallas_call(
        functools.partial(forecast_kernel, bands),
        out_shape=[
            jax.ShapeDtypeStruct((rows, members, cols), jnp.float32),
            jax.ShapeDtypeStruct((rows, members, 2 * cols), jnp.float32),
        ],
        scratch_shapes=[
            pltpu.VMEM((fields, cols // LANES, total * members, LANES), jnp.float32),
            pltpu.VMEM((cols // LANES, (total + 2) * members, LANES), jnp.float32),
            pltpu.VMEM((rows, members, 2 * cols), jnp.float32),
            pltpu.SemaphoreType.DMA((rows // ROW_BLOCK,)),
        ],
        out_specs=[pl.BlockSpec(memory_space=pltpu.VMEM), pl.BlockSpec(memory_space=pl.ANY)],
        compiler_params=pltpu.CompilerParams(vmem_limit_bytes=VMEM),
        cost_estimate=cost(STEPS * 12 * state.size, 8 * state.size),
        name="forecast",
    )(state, first, second, depth)


TAIL = 8


def corners(size):
    i = lax.broadcasted_iota(jnp.int32, (size, size), 0)
    j = lax.broadcasted_iota(jnp.int32, (size, size), 1)
    return i < j, i == j


def gram_kernel(height_ref, got_ref, cell_ref, value_ref, var_ref, keep_ref, send_ref, seen_ref, whole_ref):
    chips, cores, members, cols = height_ref.shape
    count = chips * cores * members
    number, half, share = cell_ref.shape[1], count // 2, keep_ref.shape[0]
    picks = lax.broadcasted_iota(jnp.int32, (cols, number), 0) == cell_ref[...]
    picks = jnp.where(picks, 1.0, 0.0).astype(jnp.bfloat16)
    core = lax.axis_index("member") % cores
    own = height_ref[:, pl.ds(core, 1)].reshape(half, cols)
    seen_ref[:, pl.ds(core, 1)] = picked(own, picks).reshape(chips, 1, members, number)
    seen_ref[:, pl.ds(1 - core, 1)] = picked(got_ref[...].reshape(half, cols), picks).reshape(chips, 1, members, number)
    seen = seen_ref[...].reshape(count, number)
    centre = jnp.sum(seen, axis=0, keepdims=True) / count
    observed = seen - centre
    innovation = value_ref[...] - centre
    weighted = observed / var_ref[...]
    gram = dot(weighted, observed, ((1,), (1,)))
    projection = jnp.sum(weighted * innovation, axis=1, keepdims=True)
    above, diagonal = corners(half)
    last = gram[half:, half:]
    both = jnp.concatenate([jnp.where(jnp.logical_or(above, diagonal), gram[:half, :half], last), gram[:half, half:]], axis=1)
    tails = (
        jnp.sum(jnp.where(corners(count)[1], projection, 0.0), axis=0, keepdims=True),
        jnp.concatenate([jnp.sum(jnp.where(diagonal, last, 0.0), axis=0, keepdims=True), jnp.zeros((1, half), jnp.float32)], axis=1),
    )
    for side, tail in enumerate(tails):
        first, rows = side * share, share - TAIL
        whole_ref[first:first + rows, :] = both[side * rows:(side + 1) * rows]
        whole_ref[first + rows:first + share, :] = jnp.broadcast_to(tail, (TAIL, count))
    keep_ref[...] = whole_ref[pl.ds(pl.multiple_of(core * share, TAIL), share), :]
    send_ref[...] = whole_ref[pl.ds(pl.multiple_of((1 - core) * share, TAIL), share), :]


def gram_of(height, got, cell, value, var):
    chips, cores, members, cols = height.shape
    count = chips * cores * members
    return pl.pallas_call(
        gram_kernel,
        out_shape=[jax.ShapeDtypeStruct((count // 4 + TAIL, count), jnp.float32)] * 2,
        scratch_shapes=[
            pltpu.VMEM((chips, cores, members, cell.shape[1]), jnp.float32),
            pltpu.VMEM((count // 2 + 2 * TAIL, count), jnp.float32),
        ],
        compiler_params=pltpu.CompilerParams(vmem_limit_bytes=VMEM),
        cost_estimate=cost(6 * 2 * count * cols * cell.shape[1], 4 * count * cols),
        name="gram",
    )(height, got, cell, value, var)


def pick_kernel(first, state_ref, out_ref):
    chips, members, width = out_ref.shape
    other = 1 - lax.axis_index("member") % 2
    out_ref[...] = state_ref[:, pl.ds(other, 1), :, first:first + width].reshape(out_ref.shape)


def pick(state, first, last):
    chips, cores, members, _ = state.shape
    shape = jax.ShapeDtypeStruct((chips, members, last - first), jnp.float32)
    return pl.pallas_call(
        functools.partial(pick_kernel, first),
        out_shape=shape,
        compiler_params=pltpu.CompilerParams(vmem_limit_bytes=VMEM),
        cost_estimate=cost(0, 8 * shape.size),
        name="pick",
    )(state)


def transform_kernel(keep_ref, got_ref, weights_ref, packed_ref):
    share, count = keep_ref.shape
    half, rows = count // 2, share - TAIL
    core = lax.axis_index("member") % 2
    packed_ref[pl.ds(pl.multiple_of(core * share, TAIL), share), :] = keep_ref[...]
    packed_ref[pl.ds(pl.multiple_of((1 - core) * share, TAIL), share), :] = got_ref[...]
    both = jnp.concatenate([packed_ref[:rows, :], packed_ref[share:share + rows, :]], axis=0)
    above, diagonal = corners(half)
    corner, side = both[:, :half], both[:, half:]
    upper = jnp.where(above, corner, 0.0)
    lower = jnp.where(jnp.logical_or(above, diagonal), 0.0, corner)
    one = upper + upper.T + jnp.where(diagonal, corner, 0.0)
    two = lower + lower.T + jnp.where(diagonal, packed_ref[share + rows:share + rows + 1, :half], 0.0)
    gram = jnp.concatenate([jnp.concatenate([one, side], axis=1), jnp.concatenate([side.T, two], axis=1)], axis=0)
    projection = jnp.sum(jnp.where(corners(count)[1], packed_ref[rows:rows + 1, :], 0.0), axis=1, keepdims=True)
    i = lax.broadcasted_iota(jnp.int32, (count, count), 0)
    j = lax.broadcasted_iota(jnp.int32, (count, count), 1)
    identity = jnp.where(i == j, 1.0, 0.0)
    system = identity + gram / (count - 1)
    scale = jnp.sqrt(jnp.sum(jnp.sum(system * system, axis=1, keepdims=True), axis=0, keepdims=True))
    current = system / scale
    root_inv = identity
    for step in range(NS_ITERS):
        parts, inv_parts = halves(current), halves(root_inv)
        product = current if step == 0 else dot3(inv_parts, parts)
        factor = 1.5 * identity - 0.5 * product
        factor_parts = halves(factor)
        if step < NS_ITERS - 1:
            current = dot3(parts, factor_parts)
        root_inv = factor if step == 0 else dot3(factor_parts, inv_parts)
    root = root_inv / jnp.sqrt(scale)

    def times(column):
        return jnp.sum(root * jnp.sum(jnp.where(i == j, column, 0.0), axis=0, keepdims=True), axis=1, keepdims=True)

    weights_ref[...] = times(times(projection)) / (count - 1) + root


def transform(keep, got):
    share, count = keep.shape
    return pl.pallas_call(
        transform_kernel,
        out_shape=jax.ShapeDtypeStruct((count, count), jnp.float32),
        scratch_shapes=[pltpu.VMEM((2 * share, count), jnp.float32)],
        compiler_params=pltpu.CompilerParams(vmem_limit_bytes=VMEM),
        cost_estimate=cost(6 * 2 * 14 * count ** 3, 8 * count ** 2),
        name="transform",
    )(keep, got)


def mix_kernel(weights_ref, height_ref, got_height_ref, wind_ref, out_ref, order_ref):
    chips, cores, members, cols = height_ref.shape
    half, count = chips * members, chips * cores * members
    core = lax.axis_index("member") % cores
    for q in range(chips):
        for side, other in ((0, core), (1, 1 - core)):
            start = pl.multiple_of((q * cores + other) * members, members)
            order_ref[side * half + q * members:side * half + (q + 1) * members, :] = weights_ref[pl.ds(start, members), :]

    def mixed(values, coefficients):
        centre = jnp.sum(values, axis=0, keepdims=True) / count
        return centre + dot3(coefficients, halves(values - centre), ((0,), (0,)))

    own = height_ref[:, pl.ds(core, 1)].reshape(half, cols)
    heights = jnp.concatenate([own, got_height_ref[...].reshape(half, cols)], axis=0)
    out_ref[:, :cols] = mixed(heights, halves(order_ref[...]))
    weights = halves(weights_ref[...])
    for first in (0, cols):
        out_ref[:, cols + first:2 * cols + first] = mixed(wind_ref[:, first:first + cols], weights)


def mix(weights, height, got_height, wind):
    count, cols = weights.shape[0], height.shape[-1]
    return pl.pallas_call(
        mix_kernel,
        out_shape=jax.ShapeDtypeStruct((count, 3 * cols), jnp.float32),
        scratch_shapes=[pltpu.VMEM(weights.shape, jnp.float32)],
        compiler_params=pltpu.CompilerParams(vmem_limit_bytes=VMEM),
        cost_estimate=cost(3 * 2 * count * count * 3 * cols, 4 * count * 6 * cols),
        name="mix",
    )(weights, height, got_height, wind)


def unfold_kernel(rows_ref, out_ref, lanes_ref, whole_ref, sems):
    members, fields, rows, cols = whole_ref.shape
    chunks = cols // LANES
    copies = []
    for k in range(fields):
        for c in range(k * chunks, (k + 1) * chunks):
            lanes_ref[c] = rows_ref[:, c * LANES:(c + 1) * LANES]
        for m in range(members):
            for c in range(chunks):
                whole_ref[m, k, :, c * LANES:(c + 1) * LANES] = lanes_ref[k * chunks + c, pl.ds(m, rows, stride=members), :]
        copies.append(pltpu.make_async_copy(whole_ref.at[:, k], out_ref.at[:, k], sems.at[k]))
        copies[-1].start()
    for copy in copies:
        copy.wait()


def unfold(rows, shape):
    return pl.pallas_call(
        unfold_kernel,
        out_shape=jax.ShapeDtypeStruct(shape, jnp.float32),
        out_specs=pl.BlockSpec(memory_space=pl.ANY),
        scratch_shapes=[
            pltpu.VMEM((rows.shape[1] // LANES, rows.shape[0], LANES), jnp.float32),
            pltpu.VMEM(shape, jnp.float32),
            pltpu.SemaphoreType.DMA((shape[1],)),
        ],
        compiler_params=pltpu.CompilerParams(vmem_limit_bytes=VMEM),
        cost_estimate=cost(0, 8 * rows.size),
        name="unfold",
    )(rows)


def exchange(blocks, axis, groups=None):
    return lax.all_to_all(blocks, axis, split_axis=0, concat_axis=0, tiled=True, axis_index_groups=groups)


def shards(state, depth, obs_cell, obs_value, obs_var):
    bands, tiles = lax.axis_size("space"), lax.axis_size("member")
    members, rows, fields, cols = state.shape
    ensemble, chips = tiles * members, tiles // 2
    sibling = [(i, i ^ 1) for i in range(tiles)]

    state = state.transpose(0, 2, 1, 3)
    upper = [(i, i ^ 1) for i in range(bands)]
    lower = [pair for i in range(1, bands - 1, 2) for pair in ((i, i + 1), (i + 1, i))]

    first, second = edges(state, depth)
    first = lax.ppermute(first, "space", upper)
    second = lax.ppermute(second, "space", lower)
    height, wind = forecast(state, first, second, depth, bands)
    same_core = [[2 * q + core for q in range(chips)] for core in range(2)]

    height = exchange(height.reshape(chips, 2, members, cols), "member", same_core)
    height, wind = lax.optimization_barrier((height, wind))
    wind = exchange(wind, "member").reshape(ensemble, 2 * cols)
    got_height = lax.ppermute(pick(height, 0, cols), "member", sibling)

    keep, send = gram_of(height, got_height, obs_cell[0], obs_value[0], obs_var[0])
    half = keep + lax.ppermute(send, "member", sibling)

    def others(value, axis, unit):
        return [lax.ppermute(value, axis, [(i, i ^ (unit * k)) for i in range(lax.axis_size(axis))]) for k in (1, 2, 3)]

    for axis, unit in (("space", 1), ("member", tiles // 4)):
        one, two, three = others(half, axis, unit)
        half = (half + one) + (two + three)
    one, two, three = others(half, "member", 2)
    half = (half + one) + (two + three)
    half, wind = lax.optimization_barrier((half, wind))
    beside = [(m * bands + i, (m ^ 1) * bands + (i ^ 4)) for m in range(tiles) for i in range(bands)]
    near = lax.ppermute(half, "space", [(i, i ^ 4) for i in range(bands)])
    far = lax.ppermute(half, ("member", "space"), beside)
    weights = transform(half + near, lax.ppermute(half, "member", sibling) + far)

    analysed = mix(weights, height, got_height, wind)
    back = exchange(analysed.reshape(tiles, members, fields * cols), "member").reshape(ensemble, fields * cols)
    return unfold(back, (members, fields, rows, cols)).transpose(0, 2, 1, 3)


def solution(mesh):
    placed = (
        P("member", "space", None, None),
        P("space", None),
        P("space", "member", None),
        P("space", "member", None),
        P("space", "member", None),
    )
    return jax.shard_map(
        shards,
        mesh=mesh,
        in_specs=placed,
        out_specs=P("member", "space", None, None),
        check_vma=False,
    )
```
